32 devices in a mesh: ctx: 8 (over y, x, core), ch: 4 (over z).
Axes of the slice: x: 2, y: 2, z: 4, core: 2. Of those that a mesh axis runs over, the one named last changes fastest.
Arguments:
- query_short: bfloat16 [1024, 8192], P('ctx', 'ch'), may hold values from -6 to 6
- key_short: bfloat16 [1024, 8192], P('ctx', 'ch'), may hold values from -6 to 6
- value_short: bfloat16 [1024, 8192], P('ctx', 'ch'), may hold values from -6 to 6
- short_taps: float32 [128, 8192], P(None, 'ch'), may hold values from -0.5 to 0.5
- query_long: bfloat16 [1024, 8192], P('ctx', 'ch'), may hold values from -6 to 6
- key_long: bfloat16 [1024, 8192], P('ctx', 'ch'), may hold values from -6 to 6
- long_residue: float32 [16, 8192], P(None, 'ch'), may hold values from -0.5 to 0.5
- long_rate: float32 [16, 8192], P(None, 'ch'), may hold values from 0.0009765625 to 0.05
- cotangent: bfloat16 [1024, 8192], P('ctx', 'ch'), may hold values from -6 to 6
Outputs:
- core_output: bfloat16 [1024, 8192], P('ctx', 'ch')
- query_short_grad: bfloat16 [1024, 8192], P('ctx', 'ch')
- key_short_grad: bfloat16 [1024, 8192], P('ctx', 'ch')
- value_short_grad: bfloat16 [1024, 8192], P('ctx', 'ch')
- query_long_grad: bfloat16 [1024, 8192], P('ctx', 'ch')
- key_long_grad: bfloat16 [1024, 8192], P('ctx', 'ch')
- taps_grad: float32 [128, 8192], P(None, 'ch')
The draws below stay inside these ranges and needn't reach their ends.
All inputs are finite; a program needn't handle non-finite values.
Results may differ from the reference program's by a relative error of at most 0.0064.
Values may be sent and summed in bfloat16 or wider, within the bound.
No kernel may reach another device: no remote copies, remote signals or barrier semaphores. Data moves between devices by JAX's collectives and lax.ppermute only.
A program may use at most 128 MiB of HBM per device.

```python
import math
import jax
import jax.numpy as jnp
from jax import lax

D = 8192
MR_LEN = 128
MODES = 16
SEQ = 1024


def steps_of(key, extent, shards, least, largest):
    loudness = 1.0
    for position, shards_of in shards:
        heights = jax.random.uniform(jax.random.fold_in(jax.random.fold_in(key, 6), position), (shards_of,), jnp.float32, least / len(shards), largest / len(shards))
        loudness = loudness * jnp.repeat(jnp.exp(heights), extent[position] // shards_of).reshape((-1,) + (1,) * (len(extent) - 1 - position))
    return loudness


def gaussian(stream_key, dims, deviation, bound, shards=(), held_as=jnp.bfloat16):
    values = jax.random.normal(stream_key, dims, jnp.float32) * deviation
    if len(shards) > 0:
        values = steps_of(stream_key, dims, shards, -0.22, 0.18) * values
    return jnp.clip(values, min=-bound, max=bound).astype(held_as)


def setup_inputs(seed: int = 0) -> dict:
    key_list = jax.random.split(jax.random.key(seed), 10)
    query_short = gaussian(key_list[0], (SEQ, D), 1.0, 6.0, ((0, 8), (1, 4)))
    key_short = gaussian(key_list[1], (SEQ, D), 1.0, 6.0, ((0, 8), (1, 4)))
    value_short = gaussian(key_list[2], (SEQ, D), 1.0, 6.0, ((0, 8), (1, 4)))
    short_taps = gaussian(key_list[3], (MR_LEN, D), MR_LEN ** -0.5, 0.5, ((1, 4),), jnp.float32)
    query_long = gaussian(key_list[4], (SEQ, D), 1.0, 6.0, ((0, 8), (1, 4)))
    key_long = gaussian(key_list[5], (SEQ, D), 1.0, 6.0, ((0, 8), (1, 4)))
    long_residue = gaussian(key_list[6], (MODES, D), (1.0 / SEQ ** 0.5), 0.5, ((1, 4),), jnp.float32)
    long_rate = jnp.clip(jnp.exp(math.log(0.05) - 3.9357395 * jax.random.uniform(key_list[7], (MODES, D), jnp.float32) ** steps_of(key_list[7], (MODES, D), ((1, 4),), -0.2, 0.2)), 0.0009765625, 0.05)
    cotangent = gaussian(key_list[8], (SEQ, D), 1.0, 6.0, ((0, 8), (1, 4)))
    return dict(query_short=query_short, key_short=key_short, value_short=value_short, short_taps=short_taps, query_long=query_long, key_long=key_long, long_residue=long_residue, long_rate=long_rate, cotangent=cotangent)


def settled(value):
    return lax.optimization_barrier(value.astype(jnp.bfloat16)).astype(jnp.float32)


def causal_apply(signal, kernel, total, keep):
    spectrum = jnp.fft.rfft(signal, total, axis=0) * jnp.fft.rfft(kernel, total, axis=0)
    return jnp.fft.irfft(spectrum, total, axis=0)[:keep]


def correlate(signal, kernel, total, keep):
    spectrum = jnp.fft.rfft(signal, total, axis=0) * jnp.conj(jnp.fft.rfft(kernel, total, axis=0))
    return jnp.fft.irfft(spectrum, total, axis=0)[:keep]


def channel_block(inputs):
    short_q, short_k, short_v, taps_block, long_q, long_k, residue_block, rate_block, upstream = inputs
    short_q = short_q.astype(jnp.float32)
    short_k = short_k.astype(jnp.float32)
    short_v = short_v.astype(jnp.float32)
    long_q = long_q.astype(jnp.float32)
    long_k = long_k.astype(jnp.float32)
    upstream = upstream.astype(jnp.float32)
    total = 2 * SEQ
    short_input = settled(short_k * short_v)
    short_mix = causal_apply(short_input, taps_block, total, SEQ)
    hidden = settled(short_q * short_mix)
    long_input = settled(long_k * hidden)
    times = jnp.arange(SEQ, dtype=jnp.float32)[:, None]
    long_filter = jnp.zeros((SEQ, taps_block.shape[1]), jnp.float32)
    for mode_index in range(MODES):
        long_filter = long_filter + residue_block[mode_index][None, :] * jnp.exp(-rate_block[mode_index][None, :] * times)
    long_mix = causal_apply(long_input, long_filter, total, SEQ)
    core_output = (long_q * long_mix).astype(jnp.bfloat16)
    query_long_grad = (upstream * long_mix).astype(jnp.bfloat16)
    long_back = upstream * long_q
    long_input_grad = settled(correlate(long_back, long_filter, total, SEQ))
    key_long_grad = (long_input_grad * hidden).astype(jnp.bfloat16)
    hidden_grad = long_input_grad * long_k
    query_short_grad = (hidden_grad * short_mix).astype(jnp.bfloat16)
    short_back = settled(hidden_grad * short_q)
    short_input_grad = correlate(short_back, taps_block, total, SEQ)
    key_short_grad = (short_input_grad * short_v).astype(jnp.bfloat16)
    value_short_grad = (short_input_grad * short_k).astype(jnp.bfloat16)
    taps_grad = correlate(short_back, short_input, total, MR_LEN) * (SEQ ** -0.5)
    return (core_output, query_short_grad, key_short_grad, value_short_grad, query_long_grad, key_long_grad, taps_grad.astype(jnp.float32))


def reference(query_short, key_short, value_short, short_taps, query_long, key_long, long_residue, long_rate, cotangent):
    block_width = 256
    count = D // block_width

    def split(array):
        return array.reshape(array.shape[0], count, block_width).transpose(1, 0, 2)

    def merge(array):
        return array.transpose(1, 0, 2).reshape(array.shape[1], D)

    pieces = (split(query_short), split(key_short), split(value_short), split(short_taps), split(query_long), split(key_long), split(long_residue), split(long_rate), split(cotangent))
    results = lax.map(channel_block, pieces)
    return (merge(results[0]), merge(results[1]), merge(results[2]), merge(results[3]), merge(results[4]), merge(results[5]), merge(results[6]))
```

```python
import jax
import jax.numpy as jnp
import numpy as np
from jax import lax
from jax.experimental import pallas as pl
from jax.experimental.pallas import tpu as pltpu
from jax.sharding import PartitionSpec as P

ROWS = 8
LANES = 128
VMEM_BYTES = 48 * 1024 * 1024


def split_np(matrix):
    high = matrix.astype(jnp.bfloat16)
    low = (matrix - high.astype(np.float64)).astype(jnp.bfloat16)
    return high, low


def tables(block):
    length = 2 * block
    freq = np.pi * (2 * np.arange(block)[:, None] + 1) / length
    here = freq * np.arange(block)[None, :]
    after = freq * (np.arange(block)[None, :] + block)
    own = np.concatenate([np.cos(here), -np.sin(here)], axis=0)
    nxt = np.concatenate([np.cos(after), -np.sin(after)], axis=0)
    own_hi, own_lo = split_np(own)
    nxt_hi, nxt_lo = split_np(nxt)
    own_two = np.concatenate([own_hi, own_lo], axis=1)
    own_three = np.concatenate([own_hi, own_hi, own_lo], axis=1)
    nxt_two = np.concatenate([nxt_hi, nxt_lo], axis=1)
    back = np.concatenate([own_hi.T, own_lo.T], axis=0)
    return own_two, own_three, nxt_two, back


def mxu(matrix, data):
    return lax.dot_general(
        matrix, data, (((1,), (0,)), ((), ())), preferred_element_type=jnp.float32
    )


def split(value):
    high = value.astype(jnp.bfloat16)
    low = (value - high.astype(jnp.float32)).astype(jnp.bfloat16)
    return high, low


def dft_exact(matrix_two, data):
    return mxu(matrix_two, jnp.concatenate([data, data], axis=0))


def dft_full(matrix_three, data):
    high, low = split(data)
    return mxu(matrix_three, jnp.concatenate([high, low, high], axis=0))


def dft_back(back, spec_re, spec_im):
    block = spec_re.shape[0]
    high, low = split(jnp.concatenate([spec_re, spec_im], axis=0))
    both = mxu(back, high)
    return both[:block] + both[block:] + mxu(back[:block], low)


def halves(spec):
    block = spec.shape[0] // 2
    return spec[:block], spec[block:]


def times(left, right):
    left_re, left_im = halves(left)
    right_re, right_im = halves(right)
    return left_re * right_re - left_im * right_im, left_re * right_im + left_im * right_re


def times_conj(left, right):
    left_re, left_im = halves(left)
    right_re, right_im = halves(right)
    return left_re * right_re + left_im * right_im, left_im * right_re - left_re * right_im


def sublane(shape):
    return lax.broadcasted_iota(jnp.int32, shape, 0).astype(jnp.float32)


def spread(row):
    return jnp.broadcast_to(row, (ROWS, row.shape[1]))


def mode_sum(rate, weight, start, forward, block):
    sub = sublane((ROWS, rate.shape[1]))
    age = start + (sub if forward else ROWS - 1 - sub)
    waves, falls = [], []
    for mode in range(rate.shape[0]):
        pace = spread(rate[mode : mode + 1])
        waves.append(spread(weight[mode : mode + 1]) * jnp.exp(-pace * age))
        falls.append(jnp.exp(-ROWS * pace))
    tiles = []
    count = block // ROWS
    for step in range(count):
        total = waves[0]
        for wave in waves[1:]:
            total = total + wave
        tiles.append(total)
        if step < count - 1:
            waves = [wave * fall for wave, fall in zip(waves, falls)]
    if not forward:
        tiles = tiles[::-1]
    return jnp.concatenate(tiles, axis=0)


def mode_state(rate, data, forward, out_ref, lanes):
    block = data.shape[0]
    sub = sublane((ROWS, rate.shape[1]))
    age = (ROWS - 1 - sub) if forward else sub
    tiles = [data[t : t + ROWS] for t in range(0, block, ROWS)]
    if not forward:
        tiles = tiles[::-1]
    for mode in range(rate.shape[0]):
        pace = spread(rate[mode : mode + 1])
        fall = jnp.exp(-ROWS * pace)
        total = tiles[0]
        for tile in tiles[1:]:
            total = total * fall + tile
        out_ref[mode : mode + 1, lanes] = jnp.sum(total * jnp.exp(-pace * age), axis=0, keepdims=True)


def lane_blocks(width):
    return [slice(at, at + LANES) for at in range(0, width, LANES)]


def wide(ref, lanes=slice(None)):
    return ref[:, lanes].astype(jnp.float32)


def front_kernel(ks, vs, ql, ct, rate, si_out, state_out):
    si_out[...] = (wide(ks) * wide(vs)).astype(jnp.bfloat16)
    for lanes in lane_blocks(ks.shape[1]):
        back = wide(ct, lanes) * wide(ql, lanes)
        mode_state(rate[:, lanes], back, False, state_out, lanes)


def filters_kernel(ql, ct, taps, rate, res, own_three, back, local_out, long_spec, short_spec, hold):
    block = ql.shape[0]
    for lanes in lane_blocks(ql.shape[1]):
        hold[:, lanes] = mode_sum(rate[:, lanes], res[:, lanes], 0.0, True, block)
    scale = 1.0 / block
    filt = dft_full(own_three[...], hold[...]) * scale
    long_spec[...] = filt
    short_spec[...] = dft_full(own_three[...], taps[...]) * scale
    upstream = dft_full(own_three[...], wide(ct) * wide(ql))
    local_out[...] = dft_back(back[...], *times_conj(upstream, filt))


def long_grad_kernel(local, state, rate, res, kl, qs, grad_out, back_out):
    block = local.shape[0]
    for lanes in lane_blocks(local.shape[1]):
        far = mode_sum(rate[:, lanes], res[:, lanes] * state[:, lanes], 1.0, False, block)
        grad = (local[:, lanes] + far).astype(jnp.bfloat16)
        grad_out[:, lanes] = grad
        hidden_grad = grad.astype(jnp.float32) * wide(kl, lanes)
        back_out[:, lanes] = (hidden_grad * wide(qs, lanes)).astype(jnp.bfloat16)


def short_kernel(si, halo, spec, qs, kl, rate, own_two, nxt_two, back, in_spec, mix_out, hidden_out, long_in, state_out):
    signal = dft_exact(own_two[...], si[...]) - dft_exact(nxt_two[...], halo[...])
    in_spec[...] = signal
    mix = dft_back(back[...], *times(signal, spec[...]))
    mix_out[...] = mix
    hidden = (wide(qs) * mix).astype(jnp.bfloat16)
    hidden_out[...] = hidden
    values = (wide(kl) * hidden.astype(jnp.float32)).astype(jnp.bfloat16)
    long_in[...] = values
    for lanes in lane_blocks(si.shape[1]):
        mode_state(rate[:, lanes], values[:, lanes].astype(jnp.float32), True, state_out, lanes)


def taps_kernel(sb, in_spec, grad, kl, hidden, mix, own_two, back, sb_spec, part_out, key_grad, query_grad):
    spec = dft_exact(own_two[...], sb[...])
    sb_spec[...] = spec
    scale = 1.0 / sb.shape[0]
    part = dft_back(back[...], *times_conj(spec, in_spec[...])) * scale
    part_out[...] = part.astype(jnp.bfloat16)
    slope = wide(grad)
    key_grad[...] = (slope * wide(hidden)).astype(jnp.bfloat16)
    query_grad[...] = (slope * wide(kl) * mix[...]).astype(jnp.bfloat16)


def input_grad_kernel(sb_next, sb_spec, spec, ks, vs, nxt_two, back, key_out, value_out):
    total = sb_spec[...] + dft_exact(nxt_two[...], sb_next[...])
    grad = dft_back(back[...], *times_conj(total, spec[...]))
    key_out[...] = (grad * wide(vs)).astype(jnp.bfloat16)
    value_out[...] = (grad * wide(ks)).astype(jnp.bfloat16)


def long_kernel(values, long_spec, state, rate, res, ql, ct, own_two, back, core_out, gate_out, hold):
    block = values.shape[0]
    for lanes in lane_blocks(values.shape[1]):
        weight = res[:, lanes] * state[:, lanes]
        hold[:, lanes] = mode_sum(rate[:, lanes], weight, 1.0, True, block)
    spec = dft_exact(own_two[...], values[...])
    mix = dft_back(back[...], *times(spec, long_spec[...])) + hold[...]
    core_out[...] = (wide(ql) * mix).astype(jnp.bfloat16)
    gate_out[...] = (wide(ct) * mix).astype(jnp.bfloat16)


def run(body, name, blocked, fixed, outs, width, flops, scratch=()):
    channels = blocked[0].shape[1]
    in_specs = [pl.BlockSpec((a.shape[0], width), lambda i: (0, i)) for a in blocked]
    in_specs += [pl.BlockSpec(a.shape, lambda i: (0, 0)) for a in fixed]
    out_specs = [pl.BlockSpec((rows, width), lambda i: (0, i)) for rows, _ in outs]
    out_shape = [jax.ShapeDtypeStruct((rows, channels), dtype) for rows, dtype in outs]
    moved = sum(a.size * a.dtype.itemsize for a in [*blocked, *fixed])
    moved += sum(s.size * s.dtype.itemsize for s in out_shape)
    return pl.pallas_call(
        body,
        grid=(channels // width,),
        in_specs=in_specs,
        out_specs=out_specs,
        out_shape=out_shape,
        scratch_shapes=[pltpu.VMEM((rows, width), dtype) for rows, dtype in scratch],
        compiler_params=pltpu.CompilerParams(vmem_limit_bytes=VMEM_BYTES),
        cost_estimate=pl.CostEstimate(flops=flops, bytes_accessed=moved, transcendentals=0),
        name=name,
    )(*blocked, *fixed)


def shifted(value, distance):
    size = lax.axis_size("ctx")
    pairs = [(i, i + distance) for i in range(size) if 0 <= i + distance < size]
    return lax.ppermute(value, "ctx", pairs)


def swapped(value, mask):
    size = lax.axis_size("ctx")
    return lax.ppermute(value, "ctx", [(i, i ^ mask) for i in range(size)])


def masks():
    size = lax.axis_size("ctx")
    return [1 << bit for bit in range(size.bit_length() - 1)]


def states_from(state, rate, block, later):
    me = lax.axis_index("ctx")
    got = jnp.zeros_like(state)
    total = state
    for mask in masks():
        other = swapped(total, mask)
        place = me % mask
        mine_low = (me // mask) % 2 == 0
        fade = jnp.exp(-(block * mask) * rate)
        if later:
            takes = mine_low
            steps = mask - 1 - place
        else:
            takes = jnp.logical_not(mine_low)
            steps = place
        near = jnp.exp(-(block * steps).astype(jnp.float32) * rate)
        got = got + jnp.where(takes, near, 0.0) * other
        total = jnp.where(takes, total + fade * other, other + fade * total)
    return got


def taps_total(part):
    me = lax.axis_index("ctx")
    steps = masks()
    channels = part.shape[1]
    half = channels // 2
    first = me % 2 == 0
    keep = jnp.where(first, part[:, :half], part[:, half:])
    send = jnp.where(first, part[:, half:], part[:, :half])
    mine = (keep.astype(jnp.float32) + swapped(send, 1).astype(jnp.float32)).astype(jnp.bfloat16)
    pieces = [mine[:, : half // 2], mine[:, half // 2 :]]
    rest = steps[1:]
    orders = [rest, rest[1:] + rest[:1]]
    for at in range(len(rest)):
        others = [swapped(piece, order[at]) for piece, order in zip(pieces, orders)]
        pieces = [
            (piece.astype(jnp.float32) + other.astype(jnp.float32)).astype(jnp.bfloat16)
            for piece, other in zip(pieces, others)
        ]
    mine = jnp.concatenate(pieces, axis=1)
    other = swapped(mine, 1)
    low = jnp.where(first, mine, other)
    high = jnp.where(first, other, mine)
    return jnp.concatenate([low, high], axis=1)


def local(
    query_short,
    key_short,
    value_short,
    short_taps,
    query_long,
    key_long,
    long_residue,
    long_rate,
    cotangent,
):
    block, channels = query_short.shape
    modes = long_rate.shape[0]
    sequence = block * lax.axis_size("ctx")
    half, full = jnp.bfloat16, jnp.float32
    own_two, own_three, nxt_two, back = [jnp.asarray(t) for t in tables(block)]
    width = 512
    unit = 2 * block * block * channels * 2

    short_in, back_state = run(
        front_kernel,
        "front",
        [key_short, value_short, query_long, cotangent, long_rate],
        [],
        [(block, half), (modes, full)],
        width,
        4 * modes * block * channels,
    )
    halo = shifted(short_in, 1)
    back_far = states_from(back_state, long_rate, block, True)
    grad_local, long_spec, short_spec = run(
        filters_kernel,
        "filters",
        [query_long, cotangent, short_taps, long_rate, long_residue],
        [own_three, back],
        [(block, full), (2 * block, full), (2 * block, full)],
        width,
        12 * unit,
        [(block, full)],
    )
    long_grad, short_back = run(
        long_grad_kernel,
        "long_grad",
        [grad_local, back_far, long_rate, long_residue, key_long, query_short],
        [],
        [(block, half), (block, half)],
        width,
        4 * modes * block * channels,
    )
    in_spec, short_mix, hidden, long_in, fore_state = run(
        short_kernel,
        "short",
        [short_in, halo, short_spec, query_short, key_long, long_rate],
        [own_two, nxt_two, back],
        [(2 * block, full), (block, full), (block, half), (block, half), (modes, full)],
        width,
        7 * unit,
    )
    sb_spec, part, key_long_grad, query_short_grad = run(
        taps_kernel,
        "taps",
        [short_back, in_spec, long_grad, key_long, hidden, short_mix],
        [own_two, back],
        [(2 * block, full), (block, half), (block, half), (block, half)],
        width,
        5 * unit,
    )
    sb_next = shifted(short_back, -1)
    taps_sum = taps_total(part)
    taps_grad = taps_sum.astype(full) * (sequence ** (-0.5))
    fore_far = states_from(fore_state, long_rate, block, False)
    core_output, query_long_grad = run(
        long_kernel,
        "long",
        [long_in, long_spec, fore_far, long_rate, long_residue, query_long, cotangent],
        [own_two, back],
        [(block, half), (block, half)],
        width,
        5 * unit,
        [(block, full)],
    )
    key_short_grad, value_short_grad = run(
        input_grad_kernel,
        "input_grad",
        [sb_next, sb_spec, short_spec, key_short, value_short],
        [nxt_two, back],
        [(block, half), (block, half)],
        width,
        5 * unit,
    )
    return (
        core_output,
        query_short_grad,
        key_short_grad,
        value_short_grad,
        query_long_grad,
        key_long_grad,
        taps_grad,
    )


def solution(mesh):
    tokens, shared = P("ctx", "ch"), P(None, "ch")
    return jax.shard_map(
        local,
        mesh=mesh,
        in_specs=(tokens, tokens, tokens, shared, tokens, tokens, shared, shared, tokens),
        out_specs=(tokens,) * 6 + (shared,),
        check_vma=False,
    )
```

```python
import jax
import jax.numpy as jnp
import numpy as np
from jax import lax
from jax.experimental import pallas as pl
from jax.experimental.pallas import tpu as pltpu
from jax.sharding import PartitionSpec as P

ROWS = 8
LANES = 128
VMEM_BYTES = 16 * 1024 * 1024


def split_np(matrix):
    high = matrix.astype(jnp.bfloat16)
    low = (matrix - high.astype(np.float64)).astype(jnp.bfloat16)
    return high, low


def tables(block):
    length = 2 * block
    freq = np.pi * (2 * np.arange(block)[:, None] + 1) / length
    here = freq * np.arange(block)[None, :]
    after = freq * (np.arange(block)[None, :] + block)
    own = np.concatenate([np.cos(here), -np.sin(here)], axis=0)
    nxt = np.concatenate([np.cos(after), -np.sin(after)], axis=0)
    own_hi, own_lo = split_np(own)
    nxt_hi, nxt_lo = split_np(nxt)
    own_two = np.concatenate([own_hi, own_lo], axis=1)
    own_three = np.concatenate([own_hi, own_hi, own_lo], axis=1)
    nxt_two = np.concatenate([nxt_hi, nxt_lo], axis=1)
    back = np.concatenate([own_hi.T, own_lo.T], axis=0)
    return own_two, own_three, nxt_two, back


def mxu(matrix, data):
    return lax.dot_general(
        matrix, data, (((1,), (0,)), ((), ())), preferred_element_type=jnp.float32
    )


def split(value):
    high = value.astype(jnp.bfloat16)
    low = (value - high.astype(jnp.float32)).astype(jnp.bfloat16)
    return high, low


def dft_exact(matrix_two, data):
    return mxu(matrix_two, jnp.concatenate([data, data], axis=0))


def dft_full(matrix_three, data):
    high, low = split(data)
    return mxu(matrix_three, jnp.concatenate([high, low, high], axis=0))


def dft_back(back, spec_re, spec_im):
    block = spec_re.shape[0]
    high, low = split(jnp.concatenate([spec_re, spec_im], axis=0))
    both = mxu(back, high)
    return both[:block] + both[block:] + mxu(back[:block], low)


def halves(spec):
    block = spec.shape[0] // 2
    return spec[:block], spec[block:]


def times(left, right):
    left_re, left_im = halves(left)
    right_re, right_im = halves(right)
    return left_re * right_re - left_im * right_im, left_re * right_im + left_im * right_re


def times_conj(left, right):
    left_re, left_im = halves(left)
    right_re, right_im = halves(right)
    return left_re * right_re + left_im * right_im, left_im * right_re - left_re * right_im


def sublane(shape):
    return lax.broadcasted_iota(jnp.int32, shape, 0).astype(jnp.float32)


def spread(row):
    return jnp.broadcast_to(row, (ROWS, row.shape[1]))


def mode_sum(rate, weight, start, forward, block):
    sub = sublane((ROWS, rate.shape[1]))
    age = start + (sub if forward else ROWS - 1 - sub)
    waves, falls = [], []
    for mode in range(rate.shape[0]):
        pace = spread(rate[mode : mode + 1])
        waves.append(spread(weight[mode : mode + 1]) * jnp.exp(-pace * age))
        falls.append(jnp.exp(-ROWS * pace))
    tiles = []
    count = block // ROWS
    for step in range(count):
        total = waves[0]
        for wave in waves[1:]:
            total = total + wave
        tiles.append(total)
        if step < count - 1:
            waves = [wave * fall for wave, fall in zip(waves, falls)]
    if not forward:
        tiles = tiles[::-1]
    return jnp.concatenate(tiles, axis=0)


def mode_state(rate, data, forward, out_ref, lanes):
    block = data.shape[0]
    sub = sublane((ROWS, rate.shape[1]))
    age = (ROWS - 1 - sub) if forward else sub
    tiles = [data[t : t + ROWS] for t in range(0, block, ROWS)]
    if not forward:
        tiles = tiles[::-1]
    for mode in range(rate.shape[0]):
        pace = spread(rate[mode : mode + 1])
        fall = jnp.exp(-ROWS * pace)
        total = tiles[0]
        for tile in tiles[1:]:
            total = total * fall + tile
        out_ref[mode : mode + 1, lanes] = jnp.sum(total * jnp.exp(-pace * age), axis=0, keepdims=True)


def lane_blocks(width):
    return [slice(at, at + LANES) for at in range(0, width, LANES)]


def wide(ref, lanes=slice(None)):
    return ref[:, lanes].astype(jnp.float32)


def in_vmem(value):
    return pltpu.with_memory_space_constraint(value, pltpu.VMEM)


def in_hbm(value):
    return pltpu.with_memory_space_constraint(value, pltpu.HBM)


def front(key_short, value_short, query_long, cotangent, rate, others, width):
    block, channels = key_short.shape
    half, full = jnp.bfloat16, jnp.float32
    parts = range(0, channels, width)
    brought = [rate, cotangent, query_long, key_short, value_short, *others]
    pieces = [1] + [len(parts)] * 4 + [1] * len(others)
    count = len(brought)

    def body(*refs):
        sources, results, sems = refs[:count], refs[count : 2 * count], refs[-1]
        si, state = refs[2 * count : 2 * count + 2]
        copies, at = [], 0
        for source, result, many in zip(sources, results, pieces):
            step = source.shape[1] // many
            row = []
            for i in range(many):
                cut = pl.ds(i * step, step)
                row.append(pltpu.make_async_copy(source.at[:, cut], result.at[:, cut], sems.at[at]))
                at += 1
            copies.append(row)
        order = [copies[0][0]]
        for i in range(len(parts)):
            order += [copies[1][i], copies[2][i]]
        for i in range(len(parts)):
            order += [copies[3][i], copies[4][i]]
        for row in copies[5:]:
            order += row
        for copy in order:
            copy.start()
        copies[0][0].wait()
        pace, ct, ql, ks, vs = results[:5]
        for i, start in enumerate(parts):
            copies[1][i].wait()
            copies[2][i].wait()
            for lane in range(start, start + width, LANES):
                lanes = slice(lane, lane + LANES)
                back = wide(ct, lanes) * wide(ql, lanes)
                mode_state(pace[:, lanes], back, False, state, lanes)
        for i, start in enumerate(parts):
            copies[3][i].wait()
            copies[4][i].wait()
            lanes = slice(start, start + width)
            si[:, lanes] = (wide(ks, lanes) * wide(vs, lanes)).astype(half)
        for row in copies[5:]:
            row[0].wait()

    out_shape = [pltpu.VMEM(a.shape, a.dtype) for a in brought]
    out_shape += [pltpu.VMEM((block, channels), half), pltpu.VMEM(rate.shape, full)]
    results = pl.pallas_call(
        body,
        in_specs=[pl.BlockSpec(memory_space=pltpu.HBM)] * count,
        out_specs=[pl.BlockSpec(memory_space=pltpu.VMEM)] * (count + 2),
        out_shape=out_shape,
        scratch_shapes=[pltpu.SemaphoreType.DMA((sum(pieces),))],
        compiler_params=pltpu.CompilerParams(vmem_limit_bytes=VMEM_BYTES),
        cost_estimate=pl.CostEstimate(flops=0, bytes_accessed=8 * 1024 * 1024, transcendentals=0),
        name="front",
    )(*[in_hbm(a) for a in brought])
    return results[:count], results[count], results[count + 1]


def filters_kernel(ql, ct, rate, res, own_three, back, local_out, long_spec, hold):
    block = ql.shape[0]
    for lanes in lane_blocks(ql.shape[1]):
        hold[:, lanes] = mode_sum(rate[:, lanes], res[:, lanes], 0.0, True, block)
    filt = dft_full(own_three[...], hold[...]) * (1.0 / block)
    long_spec[...] = filt
    upstream = dft_full(own_three[...], wide(ct) * wide(ql))
    local_out[...] = dft_back(back[...], *times_conj(upstream, filt))


def long_grad_kernel(local, state, rate, res, kl, qs, grad_out, back_out):
    block = local.shape[0]
    for lanes in lane_blocks(local.shape[1]):
        far = mode_sum(rate[:, lanes], res[:, lanes] * state[:, lanes], 1.0, False, block)
        grad = (local[:, lanes] + far).astype(jnp.bfloat16)
        grad_out[:, lanes] = grad
        hidden_grad = grad.astype(jnp.float32) * wide(kl, lanes)
        back_out[:, lanes] = (hidden_grad * wide(qs, lanes)).astype(jnp.bfloat16)


def taps_kernel(sb, si, halo, own_two, nxt_two, back, sb_spec, in_spec, part_out):
    signal = dft_exact(own_two[...], si[...]) - dft_exact(nxt_two[...], halo[...])
    in_spec[...] = signal
    spec = dft_exact(own_two[...], sb[...])
    sb_spec[...] = spec
    part = dft_back(back[...], *times_conj(spec, signal)) * (1.0 / sb.shape[0])
    part_out[...] = part.astype(jnp.bfloat16)


def short_kernel(in_spec, taps, qs, kl, rate, grad, own_three, back, spec_out, long_in, state_out, key_grad, query_grad):
    spec = dft_full(own_three[...], taps[...]) * (1.0 / qs.shape[0])
    spec_out[...] = spec
    mix = dft_back(back[...], *times(in_spec[...], spec))
    hidden = (wide(qs) * mix).astype(jnp.bfloat16).astype(jnp.float32)
    values = (wide(kl) * hidden).astype(jnp.bfloat16)
    long_in[...] = values
    slope = wide(grad)
    key_grad[...] = (slope * hidden).astype(jnp.bfloat16)
    query_grad[...] = (slope * wide(kl) * mix).astype(jnp.bfloat16)
    for lanes in lane_blocks(qs.shape[1]):
        mode_state(rate[:, lanes], values[:, lanes].astype(jnp.float32), True, state_out, lanes)


def input_grad_kernel(sb_next, sb_spec, spec, ks, vs, nxt_two, back, key_out, value_out):
    total = sb_spec[...] + dft_exact(nxt_two[...], sb_next[...])
    grad = dft_back(back[...], *times_conj(total, spec[...]))
    key_out[...] = (grad * wide(vs)).astype(jnp.bfloat16)
    value_out[...] = (grad * wide(ks)).astype(jnp.bfloat16)


def long_kernel(values, long_spec, state, rate, res, ql, ct, own_two, back, core_out, gate_out, hold):
    block = values.shape[0]
    for lanes in lane_blocks(values.shape[1]):
        weight = res[:, lanes] * state[:, lanes]
        hold[:, lanes] = mode_sum(rate[:, lanes], weight, 1.0, True, block)
    spec = dft_exact(own_two[...], values[...])
    mix = dft_back(back[...], *times(spec, long_spec[...])) + hold[...]
    core_out[...] = (wide(ql) * mix).astype(jnp.bfloat16)
    gate_out[...] = (wide(ct) * mix).astype(jnp.bfloat16)


def run(body, name, blocked, fixed, outs, width, flops, scratch=()):
    channels = blocked[0].shape[1]
    n_in, n_fix, n_out = len(blocked), len(fixed), len(outs)
    leaves = [i for i, (_, _, place) in enumerate(outs) if place == "hbm"]
    count = channels // width

    def whole(*refs):
        ins, fix = refs[:n_in], refs[n_in : n_in + n_fix]
        results, rest = list(refs[n_in + n_fix : n_in + n_fix + n_out]), refs[n_in + n_fix + n_out :]
        hold, staged = rest[: len(scratch)], rest[len(scratch) : len(scratch) + len(leaves)]
        copies = []
        for step in range(count):
            cut = pl.ds(step * width, width)
            there = [r.at[:, cut] for r in results]
            for slot, i in enumerate(leaves):
                there[i] = staged[slot].at[:, cut]
            body(*[r.at[:, cut] for r in ins], *fix, *there, *hold)
            for slot, i in enumerate(leaves):
                copy = pltpu.make_async_copy(there[i], results[i].at[:, cut], rest[-1].at[slot, step])
                copy.start()
                copies.append(copy)
        for copy in copies:
            copy.wait()

    places = {"hbm": pltpu.HBM, "vmem": pltpu.VMEM}
    scratch_shapes = [pltpu.VMEM((rows, width), dtype) for rows, dtype in scratch]
    scratch_shapes += [pltpu.VMEM((outs[i][0], channels), outs[i][1]) for i in leaves]
    if leaves:
        scratch_shapes.append(pltpu.SemaphoreType.DMA((len(leaves), count)))
    moved = sum(rows * channels * jnp.dtype(dtype).itemsize for rows, dtype, _ in outs)
    return pl.pallas_call(
        whole,
        in_specs=[pl.BlockSpec(memory_space=pltpu.VMEM)] * (n_in + n_fix),
        out_specs=[pl.BlockSpec(memory_space=places[place]) for _, _, place in outs],
        out_shape=[places[place]((rows, channels), dtype) for rows, dtype, place in outs],
        scratch_shapes=scratch_shapes,
        compiler_params=pltpu.CompilerParams(vmem_limit_bytes=VMEM_BYTES),
        cost_estimate=pl.CostEstimate(flops=flops, bytes_accessed=moved, transcendentals=0),
        name=name,
    )(*[in_vmem(a) for a in [*blocked, *fixed]])


def small(body, name, operands, outs, place=pltpu.VMEM):
    return pl.pallas_call(
        body,
        in_specs=[pl.BlockSpec(memory_space=pltpu.VMEM)] * len(operands),
        out_specs=[pl.BlockSpec(memory_space=pltpu.VMEM)] * len(outs),
        out_shape=[place(shape, dtype) for shape, dtype in outs],
        compiler_params=pltpu.CompilerParams(vmem_limit_bytes=VMEM_BYTES),
        cost_estimate=pl.CostEstimate(flops=0, bytes_accessed=1024, transcendentals=0),
        name=name,
    )(*[in_vmem(a) for a in operands])


def shifted(value, distance):
    size = lax.axis_size("ctx")
    pairs = [(i, i + distance) for i in range(size) if 0 <= i + distance < size]
    return lax.ppermute(value, "ctx", pairs)


def swapped(value, mask):
    size = lax.axis_size("ctx")
    return lax.ppermute(value, "ctx", [(i, i ^ mask) for i in range(size)])


def masks():
    size = lax.axis_size("ctx")
    return [1 << bit for bit in range(size.bit_length() - 1)]


def states_from(state, rate, block, later):
    got, total = None, state
    for mask in masks():
        other = swapped(total, mask)

        def body(*refs, mask=mask, start=got is None):
            total, other, rate = refs[0][...], refs[1][...], refs[2][...]
            total_out, got_out = refs[-2:]
            me = lax.axis_index("ctx")
            place = lax.rem(me, mask)
            mine_low = lax.rem(lax.div(me, mask), 2) == 0
            fade = jnp.exp(-(block * mask) * rate)
            takes = mine_low if later else jnp.logical_not(mine_low)
            steps = mask - 1 - place if later else place
            taken = jnp.where(takes, jnp.exp((-block * steps).astype(jnp.float32) * rate) * other, 0.0)
            got_out[...] = taken if start else refs[3][...] + taken
            total_out[...] = jnp.where(takes, total + fade * other, other + fade * total)

        operands = [total, other, rate] + ([] if got is None else [got])
        total, got = small(body, "merge", operands, [(state.shape, jnp.float32)] * 2)
    return got


def added(pairs):
    def body(*refs):
        for i in range(len(pairs)):
            total = refs[2 * i][...].astype(jnp.float32) + refs[2 * i + 1][...].astype(jnp.float32)
            refs[2 * len(pairs) + i][...] = total.astype(jnp.bfloat16)

    flat = [value for pair in pairs for value in pair]
    return small(body, "added", flat, [(mine.shape, jnp.bfloat16) for mine, _ in pairs])


def taps_total(part, scale):
    steps = masks()
    block, channels = part.shape
    half = channels // 2
    quarter = half // 2

    def apart(part, send, *keep):
        first = lax.rem(lax.axis_index("ctx"), 2) == 0
        low, high = part[:, :half], part[:, half:]
        send[...] = jnp.where(first, high, low)
        kept = jnp.where(first, low, high)
        for i, piece in enumerate(keep):
            piece[...] = kept[:, i * quarter : (i + 1) * quarter]

    def merged(left, right, out):
        out[:, :quarter] = left[...]
        out[:, quarter:] = right[...]

    def finish(left, right, other, out):
        first = lax.rem(lax.axis_index("ctx"), 2) == 0
        mine = jnp.concatenate([left[...], right[...]], axis=1).astype(jnp.float32) * scale
        theirs = other[...].astype(jnp.float32) * scale
        out[:, :half] = jnp.where(first, mine, theirs)
        out[:, half:] = jnp.where(first, theirs, mine)

    bf = jnp.bfloat16
    send, *pieces = small(apart, "apart", [part], [((block, half), bf)] + [((block, quarter), bf)] * 2)
    other = swapped(send, 1)

    def first_sum(left, right, other, *outs):
        for i, mine in enumerate((left, right)):
            theirs = other[:, i * quarter : (i + 1) * quarter].astype(jnp.float32)
            outs[i][...] = (mine[...].astype(jnp.float32) + theirs).astype(bf)

    pieces = small(first_sum, "first_sum", [*pieces, other], [((block, quarter), bf)] * 2)
    rest = steps[1:]
    orders = [rest, rest[1:] + rest[:1]]
    for at in range(len(rest)):
        pieces = added([(piece, swapped(piece, order[at])) for piece, order in zip(pieces, orders)])
    (mine,) = small(merged, "merged", pieces, [((block, half), bf)])
    other = swapped(mine, 1)
    return small(finish, "finish", [*pieces, other], [((block, channels), jnp.float32)], pltpu.HBM)[0]


def local(
    query_short,
    key_short,
    value_short,
    short_taps,
    query_long,
    key_long,
    long_residue,
    long_rate,
    cotangent,
):
    block, channels = query_short.shape
    modes = long_rate.shape[0]
    sequence = block * lax.axis_size("ctx")
    half, full = jnp.bfloat16, jnp.float32
    matrices = [jnp.asarray(t) for t in tables(block)]
    width = 512
    unit = 2 * block * block * channels * 2

    brought, short_in, back_state = front(
        key_short,
        value_short,
        query_long,
        cotangent,
        long_rate,
        [long_residue, query_short, key_long, short_taps, *matrices],
        width,
    )
    rate, ct, ql, ks, vs, res, qs, kl, taps, own_two, own_three, nxt_two, back = brought
    back_far = states_from(back_state, rate, block, True)
    halo = shifted(short_in, 1)
    grad_local, long_spec = run(
        filters_kernel,
        "filters",
        [ql, ct, rate, res],
        [own_three, back],
        [(block, full, "vmem"), (2 * block, full, "vmem")],
        width,
        12 * unit,
        [(block, full)],
    )
    long_grad, short_back = run(
        long_grad_kernel,
        "long_grad",
        [grad_local, back_far, rate, res, kl, qs],
        [],
        [(block, half, "vmem"), (block, half, "vmem")],
        width,
        4 * modes * block * channels,
    )
    sb_spec, in_spec, part = run(
        taps_kernel,
        "taps",
        [short_back, short_in, halo],
        [own_two, nxt_two, back],
        [(2 * block, full, "vmem"), (2 * block, full, "vmem"), (block, half, "vmem")],
        width,
        5 * unit,
    )
    taps_grad = taps_total(part, sequence ** (-0.5))
    sb_next = shifted(short_back, -1)
    short_spec, long_in, fore_state, key_long_grad, query_short_grad = run(
        short_kernel,
        "short",
        [in_spec, taps, qs, kl, rate, long_grad],
        [own_three, back],
        [
            (2 * block, full, "vmem"),
            (block, half, "vmem"),
            (modes, full, "vmem"),
            (block, half, "hbm"),
            (block, half, "hbm"),
        ],
        width,
        7 * unit,
    )
    fore_far = states_from(fore_state, rate, block, False)
    core_output, query_long_grad = run(
        long_kernel,
        "long",
        [long_in, long_spec, fore_far, rate, res, ql, ct],
        [own_two, back],
        [(block, half, "hbm"), (block, half, "hbm")],
        width,
        5 * unit,
        [(block, full)],
    )
    key_short_grad, value_short_grad = run(
        input_grad_kernel,
        "input_grad",
        [sb_next, sb_spec, short_spec, ks, vs],
        [nxt_two, back],
        [(block, half, "hbm"), (block, half, "hbm")],
        width,
        5 * unit,
    )
    return (
        core_output,
        query_short_grad,
        key_short_grad,
        value_short_grad,
        query_long_grad,
        key_long_grad,
        taps_grad,
    )


def solution(mesh):
    tokens, shared = P("ctx", "ch"), P(None, "ch")
    return jax.shard_map(
        local,
        mesh=mesh,
        in_specs=(tokens, tokens, tokens, shared, tokens, tokens, shared, shared, tokens),
        out_specs=(tokens,) * 6 + (shared,),
        check_vma=False,
    )
```

```python
import jax
import jax.numpy as jnp
import numpy as np
from jax import lax
from jax.experimental import pallas as pl
from jax.experimental.pallas import tpu as pltpu
from jax.sharding import PartitionSpec as P

ROWS = 8
LANES = 128
VMEM_BYTES = 16 * 1024 * 1024


def split_np(matrix):
    high = matrix.astype(jnp.bfloat16)
    low = (matrix - high.astype(np.float64)).astype(jnp.bfloat16)
    return high, low


def tables(block):
    length = 2 * block
    freq = np.pi * (2 * np.arange(block)[:, None] + 1) / length
    here = freq * np.arange(block)[None, :]
    after = freq * (np.arange(block)[None, :] + block)
    own = np.concatenate([np.cos(here), -np.sin(here)], axis=0)
    nxt = np.concatenate([np.cos(after), -np.sin(after)], axis=0)
    own_hi, own_lo = split_np(own)
    nxt_hi, nxt_lo = split_np(nxt)
    own_two = np.concatenate([own_hi, own_lo], axis=1)
    own_three = np.concatenate([own_hi, own_hi, own_lo], axis=1)
    nxt_two = np.concatenate([nxt_hi, nxt_lo], axis=1)
    back = np.concatenate([own_hi.T, own_lo.T], axis=0)
    return own_two, own_three, nxt_two, back


def mxu(matrix, data):
    return lax.dot_general(
        matrix, data, (((1,), (0,)), ((), ())), preferred_element_type=jnp.float32
    )


def split(value):
    high = value.astype(jnp.bfloat16)
    low = (value - high.astype(jnp.float32)).astype(jnp.bfloat16)
    return high, low


def dft_exact(matrix_two, data):
    return mxu(matrix_two, jnp.concatenate([data, data], axis=0))


def dft_full(matrix_three, data):
    high, low = split(data)
    return mxu(matrix_three, jnp.concatenate([high, low, high], axis=0))


def dft_back(back, spec_re, spec_im):
    block = spec_re.shape[0]
    high, low = split(jnp.concatenate([spec_re, spec_im], axis=0))
    both = mxu(back, high)
    return both[:block] + both[block:] + mxu(back[:block], low)


def halves(spec):
    block = spec.shape[0] // 2
    return spec[:block], spec[block:]


def times(left, right):
    left_re, left_im = halves(left)
    right_re, right_im = halves(right)
    return left_re * right_re - left_im * right_im, left_re * right_im + left_im * right_re


def times_conj(left, right):
    left_re, left_im = halves(left)
    right_re, right_im = halves(right)
    return left_re * right_re + left_im * right_im, left_im * right_re - left_re * right_im


def sublane(shape):
    return lax.broadcasted_iota(jnp.int32, shape, 0).astype(jnp.float32)


def spread(row):
    return jnp.broadcast_to(row, (ROWS, row.shape[1]))


def mode_sum(rate, weight, start, forward, block):
    sub = sublane((ROWS, rate.shape[1]))
    age = start + (sub if forward else ROWS - 1 - sub)
    waves, falls = [], []
    for mode in range(rate.shape[0]):
        pace = spread(rate[mode : mode + 1])
        waves.append(spread(weight[mode : mode + 1]) * jnp.exp(-pace * age))
        falls.append(jnp.exp(-ROWS * pace))
    tiles = []
    count = block // ROWS
    for step in range(count):
        total = waves[0]
        for wave in waves[1:]:
            total = total + wave
        tiles.append(total)
        if step < count - 1:
            waves = [wave * fall for wave, fall in zip(waves, falls)]
    if not forward:
        tiles = tiles[::-1]
    return jnp.concatenate(tiles, axis=0)


def mode_state(rate, data, forward, out_ref, lanes):
    block = data.shape[0]
    sub = sublane((ROWS, rate.shape[1]))
    age = (ROWS - 1 - sub) if forward else sub
    tiles = [data[t : t + ROWS] for t in range(0, block, ROWS)]
    if not forward:
        tiles = tiles[::-1]
    for mode in range(rate.shape[0]):
        pace = spread(rate[mode : mode + 1])
        fall = jnp.exp(-ROWS * pace)
        total = tiles[0]
        for tile in tiles[1:]:
            total = total * fall + tile
        out_ref[mode : mode + 1, lanes] = jnp.sum(total * jnp.exp(-pace * age), axis=0, keepdims=True)


def lane_blocks(width):
    return [slice(at, at + LANES) for at in range(0, width, LANES)]


def wide(ref, lanes=slice(None)):
    return ref[:, lanes].astype(jnp.float32)


def in_vmem(value):
    return pltpu.with_memory_space_constraint(value, pltpu.VMEM)


def in_hbm(value):
    return pltpu.with_memory_space_constraint(value, pltpu.HBM)


def load(brought, outs, body, name, first, width, after=(), scratch=(), blocked=(), fixed=()):
    count, n_after, ready = len(brought), len(after), len(blocked) + len(fixed)
    channels = brought[0].shape[1]
    parts = channels // width
    pieces = [parts] * first + [1] * (count - first)
    offsets = [sum(pieces[:i]) for i in range(count)]

    def whole(*refs):
        sources, refs = refs[:count], refs[count:]
        ins, fix, refs = refs[: len(blocked)], refs[len(blocked) : ready], refs[ready + n_after :]
        results, more, sems = refs[:count], refs[count:-1], refs[-1]
        copies = []
        for i in range(count):
            step = sources[i].shape[1] // pieces[i]
            row = []
            for k in range(pieces[i]):
                cut = pl.ds(k * step, step)
                row.append(
                    pltpu.make_async_copy(sources[i].at[:, cut], results[i].at[:, cut], sems.at[offsets[i] + k])
                )
            copies.append(row)
        for k in range(parts):
            for row in copies[:first]:
                row[k].start()
        for row in copies[first:]:
            row[0].start()
        for k in range(parts):
            for row in copies[:first]:
                row[k].wait()
            cut = pl.ds(k * width, width)
            held = more[len(outs) :]
            there = [r.at[:, cut] for r in more[: len(outs)]]
            body(*[r.at[:, cut] for r in [*results[:first], *ins]], *fix, *there, *held)
        for row in copies[first:]:
            row[0].wait()

    out_shape = [pltpu.VMEM(a.shape, a.dtype) for a in brought]
    out_shape += [pltpu.VMEM(shape, dtype) for shape, dtype in outs]
    results = pl.pallas_call(
        whole,
        in_specs=[pl.BlockSpec(memory_space=pltpu.HBM)] * count
        + [pl.BlockSpec(memory_space=pltpu.VMEM)] * ready
        + [pl.BlockSpec(memory_space=pl.ANY)] * n_after,
        out_specs=[pl.BlockSpec(memory_space=pltpu.VMEM)] * len(out_shape),
        out_shape=out_shape,
        scratch_shapes=[pltpu.VMEM((rows, width), dtype) for rows, dtype in scratch]
        + [pltpu.SemaphoreType.DMA((sum(pieces),))],
        compiler_params=pltpu.CompilerParams(vmem_limit_bytes=VMEM_BYTES),
        cost_estimate=pl.CostEstimate(flops=0, bytes_accessed=1024, transcendentals=0),
        name=name,
    )(*[in_hbm(a) for a in brought], *[in_vmem(a) for a in [*blocked, *fixed]], *after)
    return results[:count], results[count:]


def first_kernel(rate, ct, ql, state):
    for lanes in lane_blocks(ct.shape[1]):
        mode_state(rate[:, lanes], wide(ct, lanes) * wide(ql, lanes), False, state, lanes)


def filter_kernel(rate, res, own_three, long_spec, hold):
    block = hold.shape[0]
    for lanes in lane_blocks(rate.shape[1]):
        hold[:, lanes] = mode_sum(rate[:, lanes], res[:, lanes], 0.0, True, block)
    long_spec[...] = dft_full(own_three[...], hold[...]) * (1.0 / block)


def short_filter_kernel(taps, own_three, short_spec):
    short_spec[...] = dft_full(own_three[...], taps[...]) * (1.0 / taps.shape[0])


def product_kernel(ks, vs, short_in):
    short_in[...] = (wide(ks) * wide(vs)).astype(jnp.bfloat16)


def grad_local_kernel(ql, ct, long_spec, own_three, back, local_out):
    upstream = dft_full(own_three[...], wide(ct) * wide(ql))
    local_out[...] = dft_back(back[...], *times_conj(upstream, long_spec[...]))


def long_grad_kernel(local, state, rate, res, kl, qs, grad_out, back_out):
    block = local.shape[0]
    for lanes in lane_blocks(local.shape[1]):
        far = mode_sum(rate[:, lanes], res[:, lanes] * state[:, lanes], 1.0, False, block)
        grad = (local[:, lanes] + far).astype(jnp.bfloat16)
        grad_out[:, lanes] = grad
        hidden_grad = grad.astype(jnp.float32) * wide(kl, lanes)
        back_out[:, lanes] = (hidden_grad * wide(qs, lanes)).astype(jnp.bfloat16)


def short_kernel(si, halo, spec, qs, kl, rate, own_two, nxt_two, back, in_spec, mix_out, hidden_out, long_in, state_out):
    signal = dft_exact(own_two[...], si[...]) - dft_exact(nxt_two[...], halo[...])
    in_spec[...] = signal
    mix = dft_back(back[...], *times(signal, spec[...]))
    mix_out[...] = mix
    hidden = (wide(qs) * mix).astype(jnp.bfloat16)
    hidden_out[...] = hidden
    values = (wide(kl) * hidden.astype(jnp.float32)).astype(jnp.bfloat16)
    long_in[...] = values
    for lanes in lane_blocks(si.shape[1]):
        mode_state(rate[:, lanes], values[:, lanes].astype(jnp.float32), True, state_out, lanes)


def taps_kernel(sb, in_spec, own_two, back, sb_spec, part_out):
    spec = dft_exact(own_two[...], sb[...])
    sb_spec[...] = spec
    part = dft_back(back[...], *times_conj(spec, in_spec[...])) * (1.0 / sb.shape[0])
    part_out[...] = part.astype(jnp.bfloat16)


def input_grad_kernel(sb_next, sb_spec, spec, ks, vs, grad, kl, hidden, mix, nxt_two, back, key_out, value_out, gate_out, query_out, token):
    token[...] = jnp.zeros(token.shape, jnp.float32)
    slope = wide(grad)
    gate_out[...] = (slope * wide(hidden)).astype(jnp.bfloat16)
    query_out[...] = (slope * wide(kl) * mix[...]).astype(jnp.bfloat16)
    total = sb_spec[...] + dft_exact(nxt_two[...], sb_next[...])
    grad_in = dft_back(back[...], *times_conj(total, spec[...]))
    key_out[...] = (grad_in * wide(vs)).astype(jnp.bfloat16)
    value_out[...] = (grad_in * wide(ks)).astype(jnp.bfloat16)


def long_local_kernel(values, long_spec, own_two, back, mix_out):
    spec = dft_exact(own_two[...], values[...])
    mix_out[...] = dft_back(back[...], *times(spec, long_spec[...]))


def run(body, name, blocked, fixed, outs, width, scratch=(), after=()):
    channels = blocked[0].shape[1]
    n_in, n_fix, n_out = len(blocked), len(fixed), len(outs)
    leaves = [i for i, (_, _, place) in enumerate(outs) if place == "hbm"]
    count = channels // width

    def whole(*refs):
        ins, fix, refs = refs[:n_in], refs[n_in : n_in + n_fix], refs[n_in + n_fix + len(after) :]
        results, rest = list(refs[:n_out]), refs[n_out:]
        hold, staged = rest[: len(scratch)], rest[len(scratch) : len(scratch) + len(leaves)]
        copies = []
        for step in range(count):
            cut = pl.ds(step * width, width)
            there = [r.at[:, cut] for r in results]
            for slot, i in enumerate(leaves):
                there[i] = staged[slot].at[:, cut]
            body(*[r.at[:, cut] for r in ins], *fix, *there, *hold)
            for slot, i in enumerate(leaves):
                copy = pltpu.make_async_copy(there[i], results[i].at[:, cut], rest[-1].at[slot, step])
                copy.start()
                copies.append(copy)
        for copy in copies:
            copy.wait()

    places = {"hbm": pltpu.HBM, "vmem": pltpu.VMEM}
    scratch_shapes = [pltpu.VMEM((rows, width), dtype) for rows, dtype in scratch]
    scratch_shapes += [pltpu.VMEM((outs[i][0], channels), outs[i][1]) for i in leaves]
    if leaves:
        scratch_shapes.append(pltpu.SemaphoreType.DMA((len(leaves), count)))
    return pl.pallas_call(
        whole,
        in_specs=[pl.BlockSpec(memory_space=pltpu.VMEM)] * (n_in + n_fix)
        + [pl.BlockSpec(memory_space=pl.ANY)] * len(after),
        out_specs=[pl.BlockSpec(memory_space=places[place]) for _, _, place in outs],
        out_shape=[places[place]((rows, channels), dtype) for rows, dtype, place in outs],
        scratch_shapes=scratch_shapes,
        compiler_params=pltpu.CompilerParams(vmem_limit_bytes=VMEM_BYTES),
        cost_estimate=pl.CostEstimate(flops=0, bytes_accessed=1024, transcendentals=0),
        name=name,
    )(*[in_vmem(a) for a in [*blocked, *fixed]], *after)


def small(body, name, operands, outs, after=()):
    count, n_after = len(operands), len(after)
    return pl.pallas_call(
        lambda *refs: body(*refs[:count], *refs[count + n_after :]),
        in_specs=[pl.BlockSpec(memory_space=pltpu.VMEM)] * count + [pl.BlockSpec(memory_space=pl.ANY)] * n_after,
        out_specs=[pl.BlockSpec(memory_space=pltpu.VMEM)] * len(outs),
        out_shape=[pltpu.VMEM(shape, dtype) for shape, dtype in outs],
        compiler_params=pltpu.CompilerParams(vmem_limit_bytes=VMEM_BYTES),
        cost_estimate=pl.CostEstimate(flops=0, bytes_accessed=1024, transcendentals=0),
        name=name,
    )(*[in_vmem(a) for a in operands], *after)


def shifted(value, distance):
    size = lax.axis_size("ctx")
    pairs = [(i, i + distance) for i in range(size) if 0 <= i + distance < size]
    return lax.ppermute(value, "ctx", pairs)


def swapped(value, mask):
    size = lax.axis_size("ctx")
    return lax.ppermute(value, "ctx", [(i, i ^ mask) for i in range(size)])


def masks():
    size = lax.axis_size("ctx")
    return [1 << bit for bit in range(size.bit_length() - 1)]


def merge_states(total, other, got, rate, block, mask, last, after):
    def body(*refs):
        other, rate = refs[1][...], refs[2][...]
        me = lax.axis_index("ctx")
        takes = lax.rem(lax.div(me, mask), 2) == 0
        steps = mask - 1 - lax.rem(me, mask)
        taken = jnp.where(takes, jnp.exp((-block * steps).astype(jnp.float32) * rate) * other, 0.0)
        refs[-1][...] = taken if got is None else refs[3][...] + taken
        if not last:
            own = refs[0][...]
            fade = jnp.exp(-(block * mask) * rate)
            refs[-2][...] = jnp.where(takes, own + fade * other, other + fade * own)

    operands = [total, other, rate] + ([] if got is None else [got])
    outs = [(total.shape, jnp.float32)] * (1 if last else 2)
    merged = small(body, "merge", operands, outs, after)
    return (total, merged[0]) if last else merged


def pack(out, row, value):
    high, low = split(value)
    width = out.shape[1]
    rows = value.shape[0]
    for at in range(0, value.shape[1], width):
        out[row : row + rows, :] = high[:, at : at + width]
        out[row + rows : row + 2 * rows, :] = low[:, at : at + width]
        row += 2 * rows


def unpack(ref, row, rows, count):
    pieces = []
    for _ in range(count):
        high = ref[row : row + rows, :].astype(jnp.float32)
        pieces.append(high + ref[row + rows : row + 2 * rows, :].astype(jnp.float32))
        row += 2 * rows
    return jnp.concatenate(pieces, axis=1)


def taps_and_states(part, state, rate, beside, before):
    block, channels = part.shape
    modes = state.shape[0]
    half, quarter = channels // 2, channels // 4
    bf, f32 = jnp.bfloat16, jnp.float32

    def is_first():
        return lax.rem(lax.axis_index("ctx"), 2) == 0

    def mine_of(value):
        return jnp.where(is_first(), value[:, :half], value[:, half:])

    def apart(part, state, send, keep):
        first = is_first()
        low, high = part[:, :half], part[:, half:]
        send[:block, :] = jnp.where(first, high, low)
        keep[...] = jnp.where(first, low, high)
        pack(send, block, state[...])

    tall = (block + 4 * modes, half)
    send, keep = small(apart, "apart", [part, state], [(tall, bf), ((block, half), bf)])
    other = swapped(send, 1)

    def first_sum(keep, other, state, rate, left, right, total, near):
        for i, out in enumerate((left, right)):
            lanes = slice(i * quarter, (i + 1) * quarter)
            both = wide(keep, lanes) + other[:block, lanes].astype(f32)
            out[:block, :] = both.astype(bf)
        own, theirs = state[...], unpack(other, block, modes, 2)
        first = is_first()
        near[...] = jnp.where(first, 0.0, theirs)
        fade = jnp.exp(-block * rate[...])
        chip = mine_of(jnp.where(first, theirs + fade * own, own + fade * theirs))
        total[...] = chip
        pack(left, block, chip)

    wide_piece, piece = ((block + 4 * modes, quarter), bf), ((block, quarter), bf)
    states = ((modes, half), f32)
    left, right, total, near = small(
        first_sum, "first_sum", [keep, other, state, rate], [wide_piece, piece, states, (state.shape, f32)], before
    )
    rest = masks()[1:]
    orders = [rest, rest[1:] + rest[:1]]
    got = None
    for at, mask in enumerate(rest):
        left_other, right_other = swapped(left, orders[0][at]), swapped(right, orders[1][at])
        last = at == len(rest) - 1

        def step(*refs, mask=mask, start=got is None, last=last):
            left, right, left_other, right_other, total, rate = refs[:6]
            sums = [
                (mine[:block, :].astype(f32) + theirs[:block, :].astype(f32)).astype(bf)
                for mine, theirs in ((left, left_other), (right, right_other))
            ]
            me = lax.axis_index("ctx")
            takes = lax.rem(lax.div(me, mask), 2) == 1
            steps = lax.div(lax.rem(me, mask), 2) * 2
            pace = mine_of(rate)
            own, theirs = total[...], unpack(left_other, block, modes, 2)
            taken = jnp.where(takes, jnp.exp((-block * steps).astype(f32) * pace) * theirs, 0.0)
            reached = taken if start else refs[6][...] + taken
            if last:
                mine, got_out = refs[-2:]
                mine[:block, :quarter] = sums[0]
                mine[:block, quarter:] = sums[1]
                pack(mine, block, reached)
                got_out[...] = reached
            else:
                left_out, right_out, total_out, got_out = refs[-4:]
                left_out[:block, :] = sums[0]
                right_out[...] = sums[1]
                fade = jnp.exp(-(block * mask) * pace)
                merged = jnp.where(takes, own + fade * theirs, theirs + fade * own)
                total_out[...] = merged
                pack(left_out, block, merged)
                got_out[...] = reached

        operands = [left, right, left_other, right_other, total, rate] + ([] if got is None else [got])
        after = beside[at] if at < len(beside) else ()
        if last:
            mine, got = small(step, "last_sum", operands, [((block + 2 * modes, half), bf), states], after)
        else:
            left, right, total, got = small(step, "next_sum", operands, [wide_piece, piece, states, states], after)
    other = swapped(mine, 1)
    return mine, other, got, near


def tail(mine, other, got, near, local_mix, rate, res, ql, ct, width, scale):
    block, channels = local_mix.shape
    modes, half = got.shape
    bf, f32 = jnp.bfloat16, jnp.float32
    parts = channels // width

    def body(mine, other, got, near, local_mix, rate, res, ql, ct, core, gate, taps, core_at, gate_at, taps_at, weight, sems):
        first = lax.rem(lax.axis_index("ctx"), 2) == 0
        copies = []

        def leave(source, target, sem):
            copy = pltpu.make_async_copy(source, target, sem)
            copy.start()
            copies.append(copy)

        theirs = unpack(other, block, modes, 1)
        own = got[...]
        fade = jnp.where(first, 1.0, jnp.exp(-block * rate[...]))
        weight[:, :half] = jnp.where(first, own, theirs)
        weight[:, half:] = jnp.where(first, theirs, own)
        weight[...] = res[...] * (near[...] + fade * weight[...])
        taps_at[:, :half] = jnp.where(first, mine[:block, :], other[:block, :]).astype(f32) * scale
        leave(taps_at.at[:, pl.ds(0, half)], taps.at[:, pl.ds(0, half)], sems.at[2 * parts])
        taps_at[:, half:] = jnp.where(first, other[:block, :], mine[:block, :]).astype(f32) * scale
        leave(taps_at.at[:, pl.ds(half, half)], taps.at[:, pl.ds(half, half)], sems.at[2 * parts + 1])
        for k in range(parts):
            for lane in range(k * width, (k + 1) * width, LANES):
                lanes = slice(lane, lane + LANES)
                far = mode_sum(rate[:, lanes], weight[:, lanes], 1.0, True, block)
                mix = local_mix[:, lanes] + far
                core_at[:, lanes] = (wide(ql, lanes) * mix).astype(bf)
                gate_at[:, lanes] = (wide(ct, lanes) * mix).astype(bf)
            cut = pl.ds(k * width, width)
            leave(core_at.at[:, cut], core.at[:, cut], sems.at[k])
            leave(gate_at.at[:, cut], gate.at[:, cut], sems.at[parts + k])
        for copy in copies:
            copy.wait()

    operands = [mine, other, got, near, local_mix, rate, res, ql, ct]
    shape = (block, channels)
    return pl.pallas_call(
        body,
        in_specs=[pl.BlockSpec(memory_space=pltpu.VMEM)] * len(operands),
        out_specs=[pl.BlockSpec(memory_space=pltpu.HBM)] * 3,
        out_shape=[pltpu.HBM(shape, bf), pltpu.HBM(shape, bf), pltpu.HBM(shape, f32)],
        scratch_shapes=[
            pltpu.VMEM(shape, bf),
            pltpu.VMEM(shape, bf),
            pltpu.VMEM(shape, f32),
            pltpu.VMEM((modes, channels), f32),
            pltpu.SemaphoreType.DMA((2 * parts + 2,)),
        ],
        compiler_params=pltpu.CompilerParams(vmem_limit_bytes=VMEM_BYTES),
        cost_estimate=pl.CostEstimate(flops=0, bytes_accessed=1024, transcendentals=0),
        name="tail",
    )(*[in_vmem(a) for a in operands])


def local(
    query_short,
    key_short,
    value_short,
    short_taps,
    query_long,
    key_long,
    long_residue,
    long_rate,
    cotangent,
):
    block, channels = query_short.shape
    modes = long_rate.shape[0]
    sequence = block * lax.axis_size("ctx")
    half, full = jnp.bfloat16, jnp.float32
    matrices = [jnp.asarray(t) for t in tables(block)]
    width = min(512, channels)

    (rate, ct, ql, res, own_three, ks, vs), (total,) = load(
        [long_rate, cotangent, query_long, long_residue, matrices[1], key_short, value_short],
        [((modes, channels), full)],
        first_kernel,
        "first",
        3,
        width,
    )
    far, steps = None, masks()
    for at, mask in enumerate(steps):
        other = swapped(total, mask)
        beside = []
        if at == 1:
            (qs, kl, taps, own_two, nxt_two, back), (long_spec,) = load(
                [query_short, key_long, short_taps, matrices[0], matrices[2], matrices[3]],
                [((2 * block, channels), full)],
                filter_kernel,
                "filter",
                0,
                width,
                [total],
                [(block, full)],
                [rate, res],
                [own_three],
            )
            beside = [long_spec]
        if at == 2:
            (grad_local,) = run(
                grad_local_kernel,
                "grad_local",
                [ql, ct, long_spec],
                [own_three, back],
                [(block, full, "vmem")],
                width,
                (),
                [total],
            )
            beside = [grad_local]
        total, far = merge_states(total, other, far, rate, block, mask, at == len(steps) - 1, beside)
    (short_in,) = run(product_kernel, "product", [ks, vs], [], [(block, half, "vmem")], width, (), [far])
    halo = shifted(short_in, 1)
    (short_spec,) = run(
        short_filter_kernel, "short_filter", [taps], [own_three], [(2 * block, full, "vmem")], width, (), [far]
    )
    in_spec, short_mix, hidden, long_in, fore_state = run(
        short_kernel,
        "short",
        [short_in, halo, short_spec, qs, kl, rate],
        [own_two, nxt_two, back],
        [
            (2 * block, full, "vmem"),
            (block, full, "vmem"),
            (block, half, "vmem"),
            (block, half, "vmem"),
            (modes, full, "vmem"),
        ],
        width,
    )
    long_grad, short_back = run(
        long_grad_kernel,
        "long_grad",
        [grad_local, far, rate, res, kl, qs],
        [],
        [(block, half, "vmem"), (block, half, "vmem")],
        width,
    )
    sb_spec, part = run(
        taps_kernel,
        "taps",
        [short_back, in_spec],
        [own_two, back],
        [(2 * block, full, "vmem"), (block, half, "vmem")],
        width,
    )
    sb_next = shifted(short_back, -1)
    (local_mix,) = run(
        long_local_kernel,
        "long_local",
        [long_in, long_spec],
        [own_two, back],
        [(block, full, "vmem")],
        width,
    )
    key_short_grad, value_short_grad, key_long_grad, query_short_grad, token = run(
        input_grad_kernel,
        "input_grad",
        [sb_next, sb_spec, short_spec, ks, vs, long_grad, kl, hidden, short_mix],
        [nxt_two, back],
        [(block, half, "hbm")] * 4 + [(ROWS, full, "vmem")],
        width,
    )
    mine, other, got, near = taps_and_states(part, fore_state, rate, [[token], [local_mix]], [sb_next])
    core_output, query_long_grad, taps_grad = tail(
        mine, other, got, near, local_mix, rate, res, ql, ct, width, sequence ** (-0.5)
    )
    return (
        core_output,
        query_short_grad,
        key_short_grad,
        value_short_grad,
        query_long_grad,
        key_long_grad,
        taps_grad,
    )


def solution(mesh):
    tokens, shared = P("ctx", "ch"), P(None, "ch")
    return jax.shard_map(
        local,
        mesh=mesh,
        in_specs=(tokens, tokens, tokens, shared, tokens, tokens, shared, shared, tokens),
        out_specs=(tokens,) * 6 + (shared,),
        check_vma=False,
    )
```

```python
import jax
import jax.numpy as jnp
import numpy as np
from jax import lax
from jax.experimental import pallas as pl
from jax.experimental.pallas import tpu as pltpu
from jax.sharding import PartitionSpec as P

ROWS = 8
LANES = 128
VMEM_BYTES = 16 * 1024 * 1024


def split_np(matrix):
    high = matrix.astype(jnp.bfloat16)
    low = (matrix - high.astype(np.float64)).astype(jnp.bfloat16)
    return high, low


def tables(block):
    length = 2 * block
    freq = np.pi * (2 * np.arange(block)[:, None] + 1) / length
    here = freq * np.arange(block)[None, :]
    after = freq * (np.arange(block)[None, :] + block)
    own = np.concatenate([np.cos(here), -np.sin(here)], axis=0)
    nxt = np.concatenate([np.cos(after), -np.sin(after)], axis=0)
    own_hi, own_lo = split_np(own)
    nxt_hi, nxt_lo = split_np(nxt)
    own_two = np.concatenate([own_hi, own_lo], axis=1)
    own_three = np.concatenate([own_hi, own_hi, own_lo], axis=1)
    nxt_two = np.concatenate([nxt_hi, nxt_lo], axis=1)
    back = np.concatenate([own_hi.T, own_lo.T], axis=0)
    return own_two, own_three, nxt_two, back


def mxu(matrix, data):
    return lax.dot_general(
        matrix, data, (((1,), (0,)), ((), ())), preferred_element_type=jnp.float32
    )


def split(value):
    high = value.astype(jnp.bfloat16)
    low = (value - high.astype(jnp.float32)).astype(jnp.bfloat16)
    return high, low


def dft_exact(matrix_two, data):
    return mxu(matrix_two, jnp.concatenate([data, data], axis=0))


def dft_full(matrix_three, data):
    high, low = split(data)
    return mxu(matrix_three, jnp.concatenate([high, low, high], axis=0))


def dft_back(back, spec_re, spec_im):
    block = spec_re.shape[0]
    high, low = split(jnp.concatenate([spec_re, spec_im], axis=0))
    both = mxu(back, high)
    return both[:block] + both[block:] + mxu(back[:block], low)


def halves(spec):
    block = spec.shape[0] // 2
    return spec[:block], spec[block:]


def times(left, right):
    left_re, left_im = halves(left)
    right_re, right_im = halves(right)
    return left_re * right_re - left_im * right_im, left_re * right_im + left_im * right_re


def times_conj(left, right):
    left_re, left_im = halves(left)
    right_re, right_im = halves(right)
    return left_re * right_re + left_im * right_im, left_im * right_re - left_re * right_im


def sublane(shape):
    return lax.broadcasted_iota(jnp.int32, shape, 0).astype(jnp.float32)


def spread(row):
    return jnp.broadcast_to(row, (ROWS, row.shape[1]))


def mode_sum(rate, weight, start, forward, block):
    sub = sublane((ROWS, rate.shape[1]))
    age = start + (sub if forward else ROWS - 1 - sub)
    waves, falls = [], []
    for mode in range(rate.shape[0]):
        pace = spread(rate[mode : mode + 1])
        waves.append(spread(weight[mode : mode + 1]) * jnp.exp(-pace * age))
        falls.append(jnp.exp(-ROWS * pace))
    tiles = []
    count = block // ROWS
    for step in range(count):
        total = waves[0]
        for wave in waves[1:]:
            total = total + wave
        tiles.append(total)
        if step < count - 1:
            waves = [wave * fall for wave, fall in zip(waves, falls)]
    if not forward:
        tiles = tiles[::-1]
    return jnp.concatenate(tiles, axis=0)


def mode_state(rate, data, forward, out_ref, lanes):
    block = data.shape[0]
    sub = sublane((ROWS, rate.shape[1]))
    age = (ROWS - 1 - sub) if forward else sub
    tiles = [data[t : t + ROWS] for t in range(0, block, ROWS)]
    if not forward:
        tiles = tiles[::-1]
    for mode in range(rate.shape[0]):
        pace = spread(rate[mode : mode + 1])
        fall = jnp.exp(-ROWS * pace)
        total = tiles[0]
        for tile in tiles[1:]:
            total = total * fall + tile
        out_ref[mode : mode + 1, lanes] = jnp.sum(total * jnp.exp(-pace * age), axis=0, keepdims=True)


def lane_blocks(width):
    return [slice(at, at + LANES) for at in range(0, width, LANES)]


def wide(ref, lanes=slice(None)):
    return ref[:, lanes].astype(jnp.float32)


def in_vmem(value):
    return pltpu.with_memory_space_constraint(value, pltpu.VMEM)


def in_hbm(value):
    return pltpu.with_memory_space_constraint(value, pltpu.HBM)


def load(brought, outs, body, name, first, width, after=(), scratch=(), blocked=(), fixed=()):
    count, n_after, ready = len(brought), len(after), len(blocked) + len(fixed)
    channels = outs[0][0][1]
    parts = channels // width
    pieces = [parts if i < first or a.shape[1] == channels else 1 for i, a in enumerate(brought)]
    offsets = [sum(pieces[:i]) for i in range(count)]

    def whole(*refs):
        sources, refs = refs[:count], refs[count:]
        ins, fix, refs = refs[: len(blocked)], refs[len(blocked) : ready], refs[ready + n_after :]
        results, more, sems = refs[:count], refs[count:-1], refs[-1]
        copies = []
        for i in range(count):
            step = sources[i].shape[1] // pieces[i]
            row = []
            for k in range(pieces[i]):
                cut = pl.ds(k * step, step)
                row.append(
                    pltpu.make_async_copy(sources[i].at[:, cut], results[i].at[:, cut], sems.at[offsets[i] + k])
                )
            copies.append(row)
        for k in range(parts):
            for row in copies[:first]:
                row[k].start()
        for row in copies[first:]:
            for copy in row:
                copy.start()
        for k in range(parts):
            for row in copies[:first]:
                row[k].wait()
            cut = pl.ds(k * width, width)
            held = more[len(outs) :]
            there = [r.at[:, cut] for r in more[: len(outs)]]
            body(*[r.at[:, cut] for r in [*results[:first], *ins]], *fix, *there, *held)
        for row in copies[first:]:
            for copy in row:
                copy.wait()

    out_shape = [pltpu.VMEM(a.shape, a.dtype) for a in brought]
    out_shape += [pltpu.VMEM(shape, dtype) for shape, dtype in outs]
    results = pl.pallas_call(
        whole,
        in_specs=[pl.BlockSpec(memory_space=pltpu.HBM)] * count
        + [pl.BlockSpec(memory_space=pltpu.VMEM)] * ready
        + [pl.BlockSpec(memory_space=pl.ANY)] * n_after,
        out_specs=[pl.BlockSpec(memory_space=pltpu.VMEM)] * len(out_shape),
        out_shape=out_shape,
        scratch_shapes=[pltpu.VMEM((rows, width), dtype) for rows, dtype in scratch]
        + [pltpu.SemaphoreType.DMA((sum(pieces),))],
        compiler_params=pltpu.CompilerParams(vmem_limit_bytes=VMEM_BYTES),
        cost_estimate=pl.CostEstimate(flops=0, bytes_accessed=1024, transcendentals=0),
        name=name,
    )(*[in_hbm(a) for a in brought], *[in_vmem(a) for a in [*blocked, *fixed]], *after)
    return results[:count], results[count:]


def first_kernel(rate, ct, ql, state):
    for lanes in lane_blocks(ct.shape[1]):
        mode_state(rate[:, lanes], wide(ct, lanes) * wide(ql, lanes), False, state, lanes)


def filter_kernel(rate, res, own_three, long_spec, hold):
    block = hold.shape[0]
    for lanes in lane_blocks(rate.shape[1]):
        hold[:, lanes] = mode_sum(rate[:, lanes], res[:, lanes], 0.0, True, block)
    long_spec[...] = dft_full(own_three[...], hold[...]) * (1.0 / block)


def short_filter_kernel(taps, si, own_three, own_two, short_spec, own_spec):
    short_spec[...] = dft_full(own_three[...], taps[...]) * (1.0 / taps.shape[0])
    own_spec[...] = dft_exact(own_two[...], si[...])


def product_kernel(ks, vs, short_in):
    short_in[...] = (wide(ks) * wide(vs)).astype(jnp.bfloat16)


def grad_local_kernel(ql, ct, long_spec, own_three, back, local_out):
    upstream = dft_full(own_three[...], wide(ct) * wide(ql))
    local_out[...] = dft_back(back[...], *times_conj(upstream, long_spec[...]))


def long_grad_kernel(local, state, rate, res, kl, qs, grad_out, back_out):
    block = local.shape[0]
    for lanes in lane_blocks(local.shape[1]):
        far = mode_sum(rate[:, lanes], res[:, lanes] * state[:, lanes], 1.0, False, block)
        grad = (local[:, lanes] + far).astype(jnp.bfloat16)
        grad_out[:, lanes] = grad
        hidden_grad = grad.astype(jnp.float32) * wide(kl, lanes)
        back_out[:, lanes] = (hidden_grad * wide(qs, lanes)).astype(jnp.bfloat16)


def short_kernel(own_spec, halo, spec, qs, kl, rate, nxt_two, back, in_spec, mix_out, hidden_out, long_in, state_out):
    signal = own_spec[...] - dft_exact(nxt_two[...], halo[...])
    in_spec[...] = signal
    mix = dft_back(back[...], *times(signal, spec[...]))
    mix_out[...] = mix
    hidden = (wide(qs) * mix).astype(jnp.bfloat16)
    hidden_out[...] = hidden
    values = (wide(kl) * hidden.astype(jnp.float32)).astype(jnp.bfloat16)
    long_in[...] = values
    for lanes in lane_blocks(halo.shape[1]):
        mode_state(rate[:, lanes], values[:, lanes].astype(jnp.float32), True, state_out, lanes)


def taps_kernel(sb, in_spec, own_two, back, sb_spec, part_out):
    spec = dft_exact(own_two[...], sb[...])
    sb_spec[...] = spec
    part = dft_back(back[...], *times_conj(spec, in_spec[...])) * (1.0 / sb.shape[0])
    part_out[...] = part.astype(jnp.bfloat16)


def input_grad_kernel(sb_next, sb_spec, spec, ks, vs, grad, kl, hidden, mix, nxt_two, back, key_out, value_out, gate_out, query_out, token):
    token[...] = jnp.zeros(token.shape, jnp.float32)
    slope = wide(grad)
    gate_out[...] = (slope * wide(hidden)).astype(jnp.bfloat16)
    query_out[...] = (slope * wide(kl) * mix[...]).astype(jnp.bfloat16)
    total = sb_spec[...] + dft_exact(nxt_two[...], sb_next[...])
    grad_in = dft_back(back[...], *times_conj(total, spec[...]))
    key_out[...] = (grad_in * wide(vs)).astype(jnp.bfloat16)
    value_out[...] = (grad_in * wide(ks)).astype(jnp.bfloat16)


def long_local_kernel(values, long_spec, own_two, back, mix_out):
    spec = dft_exact(own_two[...], values[...])
    mix_out[...] = dft_back(back[...], *times(spec, long_spec[...]))


def run(body, name, blocked, fixed, outs, width, scratch=(), after=()):
    channels = blocked[0].shape[1]
    n_in, n_fix, n_out = len(blocked), len(fixed), len(outs)
    leaves = [i for i, (_, _, place) in enumerate(outs) if place == "hbm"]
    count = channels // width

    def whole(*refs):
        ins, fix, refs = refs[:n_in], refs[n_in : n_in + n_fix], refs[n_in + n_fix + len(after) :]
        results, rest = list(refs[:n_out]), refs[n_out:]
        hold, staged = rest[: len(scratch)], rest[len(scratch) : len(scratch) + len(leaves)]
        copies = []
        for step in range(count):
            cut = pl.ds(step * width, width)
            there = [r.at[:, cut] for r in results]
            for slot, i in enumerate(leaves):
                there[i] = staged[slot].at[:, cut]
            body(*[r.at[:, cut] for r in ins], *fix, *there, *hold)
            for slot, i in enumerate(leaves):
                copy = pltpu.make_async_copy(there[i], results[i].at[:, cut], rest[-1].at[slot, step])
                copy.start()
                copies.append(copy)
        for copy in copies:
            copy.wait()

    places = {"hbm": pltpu.HBM, "vmem": pltpu.VMEM}
    scratch_shapes = [pltpu.VMEM((rows, width), dtype) for rows, dtype in scratch]
    scratch_shapes += [pltpu.VMEM((outs[i][0], channels), outs[i][1]) for i in leaves]
    if leaves:
        scratch_shapes.append(pltpu.SemaphoreType.DMA((len(leaves), count)))
    return pl.pallas_call(
        whole,
        in_specs=[pl.BlockSpec(memory_space=pltpu.VMEM)] * (n_in + n_fix)
        + [pl.BlockSpec(memory_space=pl.ANY)] * len(after),
        out_specs=[pl.BlockSpec(memory_space=places[place]) for _, _, place in outs],
        out_shape=[places[place]((rows, channels), dtype) for rows, dtype, place in outs],
        scratch_shapes=scratch_shapes,
        compiler_params=pltpu.CompilerParams(vmem_limit_bytes=VMEM_BYTES),
        cost_estimate=pl.CostEstimate(flops=0, bytes_accessed=1024, transcendentals=0),
        name=name,
    )(*[in_vmem(a) for a in [*blocked, *fixed]], *after)


def small(body, name, operands, outs, after=()):
    count, n_after = len(operands), len(after)
    return pl.pallas_call(
        lambda *refs: body(*refs[:count], *refs[count + n_after :]),
        in_specs=[pl.BlockSpec(memory_space=pltpu.VMEM)] * count + [pl.BlockSpec(memory_space=pl.ANY)] * n_after,
        out_specs=[pl.BlockSpec(memory_space=pltpu.VMEM)] * len(outs),
        out_shape=[pltpu.VMEM(shape, dtype) for shape, dtype in outs],
        compiler_params=pltpu.CompilerParams(vmem_limit_bytes=VMEM_BYTES),
        cost_estimate=pl.CostEstimate(flops=0, bytes_accessed=1024, transcendentals=0),
        name=name,
    )(*[in_vmem(a) for a in operands], *after)


def shifted(value, distance):
    size = lax.axis_size("ctx")
    pairs = [(i, i + distance) for i in range(size) if 0 <= i + distance < size]
    return lax.ppermute(value, "ctx", pairs)


def swapped(value, mask):
    size = lax.axis_size("ctx")
    return lax.ppermute(value, "ctx", [(i, i ^ mask) for i in range(size)])


def masks():
    size = lax.axis_size("ctx")
    return [1 << bit for bit in range(size.bit_length() - 1)]


def merge_states(total, other, got, rate, block, mask, last, after):
    def body(*refs):
        other, rate = refs[1][...], refs[2][...]
        me = lax.axis_index("ctx")
        takes = lax.rem(lax.div(me, mask), 2) == 0
        steps = mask - 1 - lax.rem(me, mask)
        taken = jnp.where(takes, jnp.exp((-block * steps).astype(jnp.float32) * rate) * other, 0.0)
        refs[-1][...] = taken if got is None else refs[3][...] + taken
        if not last:
            own = refs[0][...]
            fade = jnp.exp(-(block * mask) * rate)
            refs[-2][...] = jnp.where(takes, own + fade * other, other + fade * own)

    operands = [total, other, rate] + ([] if got is None else [got])
    outs = [(total.shape, jnp.float32)] * (1 if last else 2)
    merged = small(body, "merge", operands, outs, after)
    return (total, merged[0]) if last else merged


def pack(out, row, value):
    high, low = split(value)
    rows, channels = value.shape
    for at in range(0, channels, out.shape[1]):
        here = min(out.shape[1], channels - at)
        out[row : row + rows, :here] = high[:, at : at + here]
        out[row + rows : row + 2 * rows, :here] = low[:, at : at + here]
        row += 2 * rows


def unpack(ref, row, rows, channels):
    pieces = []
    for at in range(0, channels, ref.shape[1]):
        here = min(ref.shape[1], channels - at)
        high = ref[row : row + rows, :here].astype(jnp.float32)
        pieces.append(high + ref[row + rows : row + 2 * rows, :here].astype(jnp.float32))
        row += 2 * rows
    return jnp.concatenate(pieces, axis=1)


def taps_and_states(part, state, rate, beside, before):
    block, channels = part.shape
    modes = state.shape[0]
    half = channels // 2
    cut = half * 3 // 8 // LANES * LANES
    bf, f32 = jnp.bfloat16, jnp.float32

    def mine_of(value):
        return jnp.where(lax.rem(lax.axis_index("ctx"), 2) == 0, value[:, :half], value[:, half:])

    def sum_of(mine, theirs):
        return (mine[:block, :].astype(f32) + theirs[:block, :].astype(f32)).astype(bf)

    def apart(part, state, send, keep):
        first = lax.rem(lax.axis_index("ctx"), 2) == 0
        low, high = part[:, :half], part[:, half:]
        send[:block, :] = jnp.where(first, high, low)
        keep[...] = jnp.where(first, low, high)
        pack(send, block, state[...])

    tall = (block + 4 * modes, half)
    send, keep = small(apart, "apart", [part, state], [(tall, bf), ((block, half), bf)])
    other = swapped(send, 1)

    def first_sum(keep, other, state, rate, left, right, total, near):
        both = sum_of(keep, other)
        left[:block, :] = both[:, :cut]
        right[...] = both[:, cut:]
        own, theirs = state[...], unpack(other, block, modes, channels)
        first = lax.rem(lax.axis_index("ctx"), 2) == 0
        near[...] = jnp.where(first, 0.0, theirs)
        fade = jnp.exp(-block * rate[...])
        chip = mine_of(jnp.where(first, theirs + fade * own, own + fade * theirs))
        total[...] = chip
        pack(left, block, chip)

    lefts = ((block + 2 * modes * -(-half // cut), cut), bf)
    rights, states = ((block, half - cut), bf), ((modes, half), f32)
    left, right, total, near = small(
        first_sum, "first_sum", [keep, other, state, rate], [lefts, rights, states, (state.shape, f32)], before
    )
    rest = masks()[1:]
    got = None
    for at, mask in enumerate(rest):
        left_other, right_other = swapped(left, mask), swapped(right, rest[(at + 1) % len(rest)])
        last = at == len(rest) - 1

        def reach(total, other, rate, got, mask):
            me = lax.axis_index("ctx")
            takes = lax.rem(lax.div(me, mask), 2) == 1
            steps = lax.div(lax.rem(me, mask), 2) * 2
            pace = mine_of(rate)
            theirs = unpack(other, block, modes, half)
            taken = jnp.where(takes, jnp.exp((-block * steps).astype(f32) * pace) * theirs, 0.0)
            reached = taken if got is None else got[...] + taken
            own, fade = total[...], jnp.exp(-(block * mask) * pace)
            return reached, jnp.where(takes, own + fade * theirs, theirs + fade * own)

        before_got = () if got is None else (got,)
        after = beside[at] if at < len(beside) else ()
        if last:

            def finish(left, left_other, right, right_other, total, rate, *refs, mask=mask):
                mine, got_out = refs[-2:]
                mine[:block, :cut] = sum_of(left, left_other)
                mine[:block, cut:] = sum_of(right, right_other)
                reached, _ = reach(total, left_other, rate, refs[0] if len(refs) > 2 else None, mask)
                got_out[...] = reached
                pack(mine, block, reached)

            operands = [left, left_other, right, right_other, total, rate, *before_got]
            mine, got = small(finish, "last_sum", operands, [((block + 2 * modes, half), bf), states], after)
        else:

            def go_left(left, left_other, total, rate, *refs, mask=mask):
                out, total_out, got_out = refs[-3:]
                out[:block, :] = sum_of(left, left_other)
                reached, merged = reach(total, left_other, rate, refs[0] if len(refs) > 3 else None, mask)
                got_out[...] = reached
                total_out[...] = merged
                pack(out, block, merged)

            def go_right(right, right_other, out):
                out[...] = sum_of(right, right_other)

            left, total, got = small(
                go_left, "go_left", [left, left_other, total, rate, *before_got], [lefts, states, states], after
            )
            (right,) = small(go_right, "go_right", [right, right_other], [rights])
    return mine, got, near


def gated(own, name, got, near, local_mix, rate, res, ql, ct, width, scale=None, mine=None, outputs=()):
    block, channels = local_mix.shape
    modes, half = near.shape[0], channels // 2
    bf, f32 = jnp.bfloat16, jnp.float32
    parts = half // width

    def body(*refs):
        got, near, local_mix, rate, res, ql, ct = refs[:7]
        refs = refs[7:]
        if not own:
            mine, refs = refs[0], refs[3:]
        outs, refs = refs[: 2 if own else 3], refs[2 if own else 3 :]
        core_at, gate_at, sems = refs[0], refs[1], refs[-1]
        side = lax.rem(lax.axis_index("ctx"), 2)
        first = side == 0
        start = (side if own else 1 - side) * half
        states = got[...] if own else unpack(got, block, modes, half)
        copies = []

        def leave(source, target, sem):
            copy = pltpu.make_async_copy(source, target, sem)
            copy.start()
            copies.append(copy)

        if not own:
            taps_at = refs[2]
            low, high = mine[:block, :], got[:block, :]
            taps_at[:, :half] = jnp.where(first, low, high).astype(f32) * scale
            leave(taps_at.at[:, pl.ds(0, half)], outs[2].at[:, pl.ds(0, half)], sems.at[2 * parts])
            taps_at[:, half:] = jnp.where(first, high, low).astype(f32) * scale
            leave(taps_at.at[:, pl.ds(half, half)], outs[2].at[:, pl.ds(half, half)], sems.at[2 * parts + 1])
        for k in range(parts):
            for lane in range(k * width, (k + 1) * width, LANES):
                there = pl.ds(pl.multiple_of(start + lane, LANES), LANES)
                lanes = slice(lane, lane + LANES)
                pace = rate[:, there]
                fade = jnp.where(first, 1.0, jnp.exp(-block * pace))
                weight = res[:, there] * (near[:, there] + fade * states[:, lanes])
                mix = local_mix[:, there] + mode_sum(pace, weight, 1.0, True, block)
                core_at[:, lanes] = (ql[:, there].astype(f32) * mix).astype(bf)
                gate_at[:, lanes] = (ct[:, there].astype(f32) * mix).astype(bf)
            here = pl.ds(k * width, width)
            there = pl.ds(pl.multiple_of(start + k * width, width), width)
            leave(core_at.at[:, here], outs[0].at[:, there], sems.at[k])
            leave(gate_at.at[:, here], outs[1].at[:, there], sems.at[parts + k])
        for copy in copies:
            copy.wait()

    operands = [got, near, local_mix, rate, res, ql, ct] + ([] if own else [mine])
    shape = (block, channels)
    scratch_shapes = [pltpu.VMEM((block, half), bf)] * 2 + ([] if own else [pltpu.VMEM(shape, f32)])
    return pl.pallas_call(
        body,
        in_specs=[pl.BlockSpec(memory_space=pltpu.VMEM)] * len(operands)
        + [pl.BlockSpec(memory_space=pltpu.HBM)] * len(outputs),
        out_specs=[pl.BlockSpec(memory_space=pltpu.HBM)] * (2 if own else 3),
        out_shape=[pltpu.HBM(shape, bf)] * 2 + ([] if own else [pltpu.HBM(shape, f32)]),
        input_output_aliases={} if own else {len(operands): 0, len(operands) + 1: 1},
        scratch_shapes=[*scratch_shapes, pltpu.SemaphoreType.DMA((2 * parts + 2,))],
        compiler_params=pltpu.CompilerParams(vmem_limit_bytes=VMEM_BYTES),
        cost_estimate=pl.CostEstimate(flops=0, bytes_accessed=1024, transcendentals=0),
        name=name,
    )(*[in_vmem(a) for a in operands], *[in_hbm(a) for a in outputs])


def local(
    query_short,
    key_short,
    value_short,
    short_taps,
    query_long,
    key_long,
    long_residue,
    long_rate,
    cotangent,
):
    block, channels = query_short.shape
    modes = long_rate.shape[0]
    sequence = block * lax.axis_size("ctx")
    half, full = jnp.bfloat16, jnp.float32
    matrices = [jnp.asarray(t) for t in tables(block)]
    width = min(512, channels)

    (ks, vs, rate, ct, ql), (short_in,) = load(
        [key_short, value_short, long_rate, cotangent, query_long],
        [((block, channels), half)],
        product_kernel,
        "product",
        2,
        width,
    )
    halo = shifted(short_in, 1)
    (res, own_three, qs, kl, taps, own_two, nxt_two, back), (total,) = load(
        [long_residue, matrices[1], query_short, key_long, short_taps, matrices[0], matrices[2], matrices[3]],
        [((modes, channels), full)],
        first_kernel,
        "states",
        0,
        width,
        blocked=[rate, ct, ql],
    )
    far, steps = None, masks()
    for at, mask in enumerate(steps):
        other = swapped(total, mask)
        beside = []
        if at == 1:
            (long_spec,) = run(
                filter_kernel,
                "filter",
                [rate, res],
                [own_three],
                [(2 * block, full, "vmem")],
                width,
                [(block, full)],
                [total],
            )
            (grad_local,) = run(
                grad_local_kernel,
                "grad_local",
                [ql, ct, long_spec],
                [own_three, back],
                [(block, full, "vmem")],
                width,
            )
            short_spec, own_spec = run(
                short_filter_kernel,
                "short_filter",
                [taps, short_in],
                [own_three, own_two],
                [(2 * block, full, "vmem"), (2 * block, full, "vmem")],
                width,
            )
            beside = [grad_local, short_spec]
        if at == 2:
            in_spec, short_mix, hidden, long_in, fore_state = run(
                short_kernel,
                "short",
                [own_spec, halo, short_spec, qs, kl, rate],
                [nxt_two, back],
                [
                    (2 * block, full, "vmem"),
                    (block, full, "vmem"),
                    (block, half, "vmem"),
                    (block, half, "vmem"),
                    (modes, full, "vmem"),
                ],
                width,
                (),
                [total],
            )
            beside = [hidden]
        total, far = merge_states(total, other, far, rate, block, mask, at == len(steps) - 1, beside)
    long_grad, short_back = run(
        long_grad_kernel,
        "long_grad",
        [grad_local, far, rate, res, kl, qs],
        [],
        [(block, half, "vmem"), (block, half, "vmem")],
        width,
    )
    sb_spec, part = run(
        taps_kernel,
        "taps",
        [short_back, in_spec],
        [own_two, back],
        [(2 * block, full, "vmem"), (block, half, "vmem")],
        width,
    )
    sb_next = shifted(short_back, -1)
    (local_mix,) = run(
        long_local_kernel,
        "long_local",
        [long_in, long_spec],
        [own_two, back],
        [(block, full, "vmem")],
        width,
    )
    key_short_grad, value_short_grad, key_long_grad, query_short_grad, token = run(
        input_grad_kernel,
        "input_grad",
        [sb_next, sb_spec, short_spec, ks, vs, long_grad, kl, hidden, short_mix],
        [nxt_two, back],
        [(block, half, "hbm")] * 4 + [(ROWS, full, "vmem")],
        width,
    )
    mine, got, near = taps_and_states(part, fore_state, rate, [[local_mix], [token]], ())
    other = swapped(mine, 1)
    ready = [near, local_mix, rate, res, ql, ct]
    some = gated(True, "gated_own", got, *ready, min(width, channels // 2))
    core_output, query_long_grad, taps_grad = gated(
        False, "gated_other", other, *ready, min(width, channels // 2), sequence ** (-0.5), mine, some
    )
    return (
        core_output,
        query_short_grad,
        key_short_grad,
        value_short_grad,
        query_long_grad,
        key_long_grad,
        taps_grad,
    )


def solution(mesh):
    tokens, shared = P("ctx", "ch"), P(None, "ch")
    return jax.shard_map(
        local,
        mesh=mesh,
        in_specs=(tokens, tokens, tokens, shared, tokens, tokens, shared, shared, tokens),
        out_specs=(tokens,) * 6 + (shared,),
        check_vma=False,
    )
```

```python
import jax
import jax.numpy as jnp
import numpy as np
from jax import lax
from jax.experimental import pallas as pl
from jax.experimental.pallas import tpu as pltpu
from jax.sharding import PartitionSpec as P

ROWS = 8
LANES = 128
VMEM_BYTES = 16 * 1024 * 1024


def split_np(matrix):
    high = matrix.astype(jnp.bfloat16)
    low = (matrix - high.astype(np.float64)).astype(jnp.bfloat16)
    return high, low


def tables(block):
    length = 2 * block
    freq = np.pi * (2 * np.arange(block)[:, None] + 1) / length
    here = freq * np.arange(block)[None, :]
    after = freq * (np.arange(block)[None, :] + block)
    own = np.concatenate([np.cos(here), -np.sin(here)], axis=0)
    nxt = np.concatenate([np.cos(after), -np.sin(after)], axis=0)
    own_hi, own_lo = split_np(own)
    nxt_hi, nxt_lo = split_np(nxt)
    own_two = np.concatenate([own_hi, own_lo], axis=1)
    own_three = np.concatenate([own_hi, own_hi, own_lo], axis=1)
    nxt_two = np.concatenate([nxt_hi, nxt_lo], axis=1)
    back = np.concatenate([own_hi.T, own_lo.T], axis=0)
    return own_two, own_three, nxt_two, back


def mxu(matrix, data):
    return lax.dot_general(
        matrix, data, (((1,), (0,)), ((), ())), preferred_element_type=jnp.float32
    )


def split(value):
    high = value.astype(jnp.bfloat16)
    low = (value - high.astype(jnp.float32)).astype(jnp.bfloat16)
    return high, low


def dft_exact(matrix_two, data):
    return mxu(matrix_two, jnp.concatenate([data, data], axis=0))


def dft_full(matrix_three, data):
    high, low = split(data)
    return mxu(matrix_three, jnp.concatenate([high, low, high], axis=0))


def dft_back(back, spec_re, spec_im):
    block = spec_re.shape[0]
    high, low = split(jnp.concatenate([spec_re, spec_im], axis=0))
    both = mxu(back, high)
    return both[:block] + both[block:] + mxu(back[:block], low)


def halves(spec):
    block = spec.shape[0] // 2
    return spec[:block], spec[block:]


def times(left, right):
    left_re, left_im = halves(left)
    right_re, right_im = halves(right)
    return left_re * right_re - left_im * right_im, left_re * right_im + left_im * right_re


def times_conj(left, right):
    left_re, left_im = halves(left)
    right_re, right_im = halves(right)
    return left_re * right_re + left_im * right_im, left_im * right_re - left_re * right_im


def sublane(shape):
    return lax.broadcasted_iota(jnp.int32, shape, 0).astype(jnp.float32)


def spread(row):
    return jnp.broadcast_to(row, (ROWS, row.shape[1]))


def mode_sum(rate, weight, start, forward, block):
    sub = sublane((ROWS, rate.shape[1]))
    age = start + (sub if forward else ROWS - 1 - sub)
    waves, falls = [], []
    for mode in range(rate.shape[0]):
        pace = spread(rate[mode : mode + 1])
        waves.append(spread(weight[mode : mode + 1]) * jnp.exp(-pace * age))
        falls.append(jnp.exp(-ROWS * pace))
    tiles = []
    count = block // ROWS
    for step in range(count):
        total = waves[0]
        for wave in waves[1:]:
            total = total + wave
        tiles.append(total)
        if step < count - 1:
            waves = [wave * fall for wave, fall in zip(waves, falls)]
    if not forward:
        tiles = tiles[::-1]
    return jnp.concatenate(tiles, axis=0)


def mode_state(rate, data, forward, out_ref, lanes):
    block = data.shape[0]
    sub = sublane((ROWS, rate.shape[1]))
    age = (ROWS - 1 - sub) if forward else sub
    tiles = [data[t : t + ROWS] for t in range(0, block, ROWS)]
    if not forward:
        tiles = tiles[::-1]
    for mode in range(rate.shape[0]):
        pace = spread(rate[mode : mode + 1])
        fall = jnp.exp(-ROWS * pace)
        total = tiles[0]
        for tile in tiles[1:]:
            total = total * fall + tile
        out_ref[mode : mode + 1, lanes] = jnp.sum(total * jnp.exp(-pace * age), axis=0, keepdims=True)


def lane_blocks(width):
    return [slice(at, at + LANES) for at in range(0, width, LANES)]


def wide(ref, lanes=slice(None)):
    return ref[:, lanes].astype(jnp.float32)


def in_vmem(value):
    return pltpu.with_memory_space_constraint(value, pltpu.VMEM)


def in_hbm(value):
    return pltpu.with_memory_space_constraint(value, pltpu.HBM)


def load(brought, outs, body, name, first, width, after=(), scratch=(), blocked=(), fixed=()):
    count, n_after, ready = len(brought), len(after), len(blocked) + len(fixed)
    channels = outs[0][0][1]
    parts = channels // width
    pieces = [parts if i < first or a.shape[1] == channels else 1 for i, a in enumerate(brought)]
    offsets = [sum(pieces[:i]) for i in range(count)]

    def whole(*refs):
        sources, refs = refs[:count], refs[count:]
        ins, fix, refs = refs[: len(blocked)], refs[len(blocked) : ready], refs[ready + n_after :]
        results, more, sems = refs[:count], refs[count:-1], refs[-1]
        copies = []
        for i in range(count):
            step = sources[i].shape[1] // pieces[i]
            row = []
            for k in range(pieces[i]):
                cut = pl.ds(k * step, step)
                row.append(
                    pltpu.make_async_copy(sources[i].at[:, cut], results[i].at[:, cut], sems.at[offsets[i] + k])
                )
            copies.append(row)
        for k in range(parts):
            for row in copies[:first]:
                row[k].start()
        for row in copies[first:]:
            for copy in row:
                copy.start()
        for k in range(parts):
            for row in copies[:first]:
                row[k].wait()
            cut = pl.ds(k * width, width)
            held = more[len(outs) :]
            there = [r.at[:, cut] for r in more[: len(outs)]]
            body(*[r.at[:, cut] for r in [*results[:first], *ins]], *fix, *there, *held)
        for row in copies[first:]:
            for copy in row:
                copy.wait()

    out_shape = [pltpu.VMEM(a.shape, a.dtype) for a in brought]
    out_shape += [pltpu.VMEM(shape, dtype) for shape, dtype in outs]
    results = pl.pallas_call(
        whole,
        in_specs=[pl.BlockSpec(memory_space=pltpu.HBM)] * count
        + [pl.BlockSpec(memory_space=pltpu.VMEM)] * ready
        + [pl.BlockSpec(memory_space=pl.ANY)] * n_after,
        out_specs=[pl.BlockSpec(memory_space=pltpu.VMEM)] * len(out_shape),
        out_shape=out_shape,
        scratch_shapes=[pltpu.VMEM((rows, width), dtype) for rows, dtype in scratch]
        + [pltpu.SemaphoreType.DMA((sum(pieces),))],
        compiler_params=pltpu.CompilerParams(vmem_limit_bytes=VMEM_BYTES),
        cost_estimate=pl.CostEstimate(flops=0, bytes_accessed=1024, transcendentals=0),
        name=name,
    )(*[in_hbm(a) for a in brought], *[in_vmem(a) for a in [*blocked, *fixed]], *after)
    return results[:count], results[count:]


def first_kernel(rate, ct, ql, state):
    for lanes in lane_blocks(ct.shape[1]):
        mode_state(rate[:, lanes], wide(ct, lanes) * wide(ql, lanes), False, state, lanes)


def filter_kernel(rate, res, own_three, long_spec, hold):
    block = hold.shape[0]
    for lanes in lane_blocks(rate.shape[1]):
        hold[:, lanes] = mode_sum(rate[:, lanes], res[:, lanes], 0.0, True, block)
    long_spec[...] = dft_full(own_three[...], hold[...]) * (1.0 / block)


def short_filter_kernel(taps, si, own_three, own_two, short_spec, own_spec):
    short_spec[...] = dft_full(own_three[...], taps[...]) * (1.0 / taps.shape[0])
    own_spec[...] = dft_exact(own_two[...], si[...])


def product_kernel(ks, vs, short_in):
    short_in[...] = (wide(ks) * wide(vs)).astype(jnp.bfloat16)


def grad_local_kernel(ql, ct, long_spec, own_three, back, local_out):
    upstream = dft_full(own_three[...], wide(ct) * wide(ql))
    local_out[...] = dft_back(back[...], *times_conj(upstream, long_spec[...]))


def long_grad_kernel(local, state, rate, res, kl, qs, grad_out, back_out):
    block = local.shape[0]
    for lanes in lane_blocks(local.shape[1]):
        far = mode_sum(rate[:, lanes], res[:, lanes] * state[:, lanes], 1.0, False, block)
        grad = (local[:, lanes] + far).astype(jnp.bfloat16)
        grad_out[:, lanes] = grad
        hidden_grad = grad.astype(jnp.float32) * wide(kl, lanes)
        back_out[:, lanes] = (hidden_grad * wide(qs, lanes)).astype(jnp.bfloat16)


def short_kernel(own_spec, halo, spec, qs, kl, rate, nxt_two, back, in_spec, mix_out, hidden_out, long_in, state_out):
    signal = own_spec[...] - dft_exact(nxt_two[...], halo[...])
    in_spec[...] = signal
    mix = dft_back(back[...], *times(signal, spec[...]))
    mix_out[...] = mix
    hidden = (wide(qs) * mix).astype(jnp.bfloat16)
    hidden_out[...] = hidden
    values = (wide(kl) * hidden.astype(jnp.float32)).astype(jnp.bfloat16)
    long_in[...] = values
    for lanes in lane_blocks(halo.shape[1]):
        mode_state(rate[:, lanes], values[:, lanes].astype(jnp.float32), True, state_out, lanes)


def taps_kernel(sb, in_spec, own_two, back, sb_spec, part_out):
    spec = dft_exact(own_two[...], sb[...])
    sb_spec[...] = spec
    part = dft_back(back[...], *times_conj(spec, in_spec[...])) * (1.0 / sb.shape[0])
    part_out[...] = part.astype(jnp.bfloat16)


def input_grad_kernel(sb_next, sb_spec, spec, ks, vs, grad, kl, hidden, mix, nxt_two, back, key_out, value_out, gate_out, query_out, token):
    token[...] = jnp.zeros(token.shape, jnp.float32)
    slope = wide(grad)
    gate_out[...] = (slope * wide(hidden)).astype(jnp.bfloat16)
    query_out[...] = (slope * wide(kl) * mix[...]).astype(jnp.bfloat16)
    total = sb_spec[...] + dft_exact(nxt_two[...], sb_next[...])
    grad_in = dft_back(back[...], *times_conj(total, spec[...]))
    key_out[...] = (grad_in * wide(vs)).astype(jnp.bfloat16)
    value_out[...] = (grad_in * wide(ks)).astype(jnp.bfloat16)


def long_local_kernel(values, long_spec, own_two, back, mix_out):
    spec = dft_exact(own_two[...], values[...])
    mix_out[...] = dft_back(back[...], *times(spec, long_spec[...]))


def run(body, name, blocked, fixed, outs, width, scratch=(), after=()):
    channels = blocked[0].shape[1]
    n_in, n_fix, n_out = len(blocked), len(fixed), len(outs)
    leaves = [i for i, (_, _, place) in enumerate(outs) if place == "hbm"]
    count = channels // width

    def whole(*refs):
        ins, fix, refs = refs[:n_in], refs[n_in : n_in + n_fix], refs[n_in + n_fix + len(after) :]
        results, rest = list(refs[:n_out]), refs[n_out:]
        hold, staged = rest[: len(scratch)], rest[len(scratch) : len(scratch) + len(leaves)]
        copies = []
        for step in range(count):
            cut = pl.ds(step * width, width)
            there = [r.at[:, cut] for r in results]
            for slot, i in enumerate(leaves):
                there[i] = staged[slot].at[:, cut]
            body(*[r.at[:, cut] for r in ins], *fix, *there, *hold)
            for slot, i in enumerate(leaves):
                copy = pltpu.make_async_copy(there[i], results[i].at[:, cut], rest[-1].at[slot, step])
                copy.start()
                copies.append(copy)
        for copy in copies:
            copy.wait()

    places = {"hbm": pltpu.HBM, "vmem": pltpu.VMEM}
    scratch_shapes = [pltpu.VMEM((rows, width), dtype) for rows, dtype in scratch]
    scratch_shapes += [pltpu.VMEM((outs[i][0], channels), outs[i][1]) for i in leaves]
    if leaves:
        scratch_shapes.append(pltpu.SemaphoreType.DMA((len(leaves), count)))
    return pl.pallas_call(
        whole,
        in_specs=[pl.BlockSpec(memory_space=pltpu.VMEM)] * (n_in + n_fix)
        + [pl.BlockSpec(memory_space=pl.ANY)] * len(after),
        out_specs=[pl.BlockSpec(memory_space=places[place]) for _, _, place in outs],
        out_shape=[places[place]((rows, channels), dtype) for rows, dtype, place in outs],
        scratch_shapes=scratch_shapes,
        compiler_params=pltpu.CompilerParams(vmem_limit_bytes=VMEM_BYTES),
        cost_estimate=pl.CostEstimate(flops=0, bytes_accessed=1024, transcendentals=0),
        name=name,
    )(*[in_vmem(a) for a in [*blocked, *fixed]], *after)


def small(body, name, operands, outs, after=()):
    count, n_after = len(operands), len(after)
    return pl.pallas_call(
        lambda *refs: body(*refs[:count], *refs[count + n_after :]),
        in_specs=[pl.BlockSpec(memory_space=pltpu.VMEM)] * count + [pl.BlockSpec(memory_space=pl.ANY)] * n_after,
        out_specs=[pl.BlockSpec(memory_space=pltpu.VMEM)] * len(outs),
        out_shape=[pltpu.VMEM(shape, dtype) for shape, dtype in outs],
        compiler_params=pltpu.CompilerParams(vmem_limit_bytes=VMEM_BYTES),
        cost_estimate=pl.CostEstimate(flops=0, bytes_accessed=1024, transcendentals=0),
        name=name,
    )(*[in_vmem(a) for a in operands], *after)


def shifted(value, distance):
    size = lax.axis_size("ctx")
    pairs = [(i, i + distance) for i in range(size) if 0 <= i + distance < size]
    return lax.ppermute(value, "ctx", pairs)


def swapped(value, mask):
    size = lax.axis_size("ctx")
    return lax.ppermute(value, "ctx", [(i, i ^ mask) for i in range(size)])


def masks():
    size = lax.axis_size("ctx")
    return [1 << bit for bit in range(size.bit_length() - 1)]


def merge_states(total, other, got, rate, block, mask, last, after):
    def body(*refs):
        other, rate = refs[1][...], refs[2][...]
        me = lax.axis_index("ctx")
        takes = lax.rem(lax.div(me, mask), 2) == 0
        steps = mask - 1 - lax.rem(me, mask)
        taken = jnp.where(takes, jnp.exp((-block * steps).astype(jnp.float32) * rate) * other, 0.0)
        refs[-1][...] = taken if got is None else refs[3][...] + taken
        if not last:
            own = refs[0][...]
            fade = jnp.exp(-(block * mask) * rate)
            refs[-2][...] = jnp.where(takes, own + fade * other, other + fade * own)

    operands = [total, other, rate] + ([] if got is None else [got])
    outs = [(total.shape, jnp.float32)] * (1 if last else 2)
    merged = small(body, "merge", operands, outs, after)
    return (total, merged[0]) if last else merged


def pack(out, row, value):
    high, low = split(value)
    rows, channels = value.shape
    for at in range(0, channels, out.shape[1]):
        here = min(out.shape[1], channels - at)
        out[row : row + rows, :here] = high[:, at : at + here]
        out[row + rows : row + 2 * rows, :here] = low[:, at : at + here]
        row += 2 * rows


def unpack(ref, row, rows, channels):
    pieces = []
    for at in range(0, channels, ref.shape[1]):
        here = min(ref.shape[1], channels - at)
        high = ref[row : row + rows, :here].astype(jnp.float32)
        pieces.append(high + ref[row + rows : row + 2 * rows, :here].astype(jnp.float32))
        row += 2 * rows
    return jnp.concatenate(pieces, axis=1)


def taps_and_states(part, state, rate, beside, before):
    block, channels = part.shape
    modes = state.shape[0]
    half = channels // 2
    cut = half * 3 // 8 // LANES * LANES
    bf, f32 = jnp.bfloat16, jnp.float32

    def mine_of(value):
        return jnp.where(lax.rem(lax.axis_index("ctx"), 2) == 0, value[:, :half], value[:, half:])

    def sum_of(mine, theirs):
        return (mine[:block, :].astype(f32) + theirs[:block, :].astype(f32)).astype(bf)

    pieces = 4
    piece = half // pieces

    def apart(part, state, keep, states, *sends):
        first = lax.rem(lax.axis_index("ctx"), 2) == 0
        low, high = part[:, :half], part[:, half:]
        gone = jnp.where(first, high, low)
        for i, send in enumerate(sends):
            send[...] = gone[:, i * piece : (i + 1) * piece]
        keep[...] = jnp.where(first, low, high)
        pack(states, 0, state[...])

    keep, packed, *sends = small(
        apart,
        "apart",
        [part, state],
        [((block, half), bf), ((4 * modes, half), bf)] + [((block, piece), bf)] * pieces,
    )
    packed = swapped(packed, 1)
    others = [swapped(send, 1) for send in sends]

    def first_sum(keep, packed, state, rate, *refs):
        others, (left, right, total, near) = refs[:pieces], refs[pieces:]
        both = sum_of(keep, jnp.concatenate([other[...] for other in others], axis=1))
        left[:block, :] = both[:, :cut]
        right[...] = both[:, cut:]
        own, theirs = state[...], unpack(packed, 0, modes, channels)
        first = lax.rem(lax.axis_index("ctx"), 2) == 0
        near[...] = jnp.where(first, 0.0, theirs)
        fade = jnp.exp(-block * rate[...])
        chip = mine_of(jnp.where(first, theirs + fade * own, own + fade * theirs))
        total[...] = chip
        pack(left, block, chip)

    lefts = ((block + 2 * modes * -(-half // cut), cut), bf)
    rights, states = ((block, half - cut), bf), ((modes, half), f32)
    left, right, total, near = small(
        first_sum, "first_sum", [keep, packed, state, rate, *others], [lefts, rights, states, (state.shape, f32)], before
    )
    rest = masks()[1:]
    got = None
    for at, mask in enumerate(rest):
        left_other, right_other = swapped(left, mask), swapped(right, rest[(at + 1) % len(rest)])
        last = at == len(rest) - 1

        def reach(total, other, rate, got, mask):
            me = lax.axis_index("ctx")
            takes = lax.rem(lax.div(me, mask), 2) == 1
            steps = lax.div(lax.rem(me, mask), 2) * 2
            pace = mine_of(rate)
            theirs = unpack(other, block, modes, half)
            taken = jnp.where(takes, jnp.exp((-block * steps).astype(f32) * pace) * theirs, 0.0)
            reached = taken if got is None else got[...] + taken
            own, fade = total[...], jnp.exp(-(block * mask) * pace)
            return reached, jnp.where(takes, own + fade * theirs, theirs + fade * own)

        before_got = () if got is None else (got,)
        after = beside[at] if at < len(beside) else ()
        if last:

            def finish(left, left_other, right, right_other, total, rate, *refs, mask=mask):
                mine, got_out = refs[-2:]
                mine[:block, :cut] = sum_of(left, left_other)
                mine[:block, cut:] = sum_of(right, right_other)
                reached, _ = reach(total, left_other, rate, refs[0] if len(refs) > 2 else None, mask)
                got_out[...] = reached
                pack(mine, block, reached)

            operands = [left, left_other, right, right_other, total, rate, *before_got]
            mine, got = small(finish, "last_sum", operands, [((block + 2 * modes, half), bf), states], after)
        else:

            def go_left(left, left_other, total, rate, *refs, mask=mask):
                out, total_out, got_out = refs[-3:]
                out[:block, :] = sum_of(left, left_other)
                reached, merged = reach(total, left_other, rate, refs[0] if len(refs) > 3 else None, mask)
                got_out[...] = reached
                total_out[...] = merged
                pack(out, block, merged)

            def go_right(right, right_other, out):
                out[...] = sum_of(right, right_other)

            left, total, got = small(
                go_left, "go_left", [left, left_other, total, rate, *before_got], [lefts, states, states], after
            )
            (right,) = small(go_right, "go_right", [right, right_other], [rights])
    return mine, got, near


def gated(own, name, got, near, local_mix, rate, res, ql, ct, width, scale=None, mine=None, outputs=()):
    block, channels = local_mix.shape
    modes, half = near.shape[0], channels // 2
    bf, f32 = jnp.bfloat16, jnp.float32
    parts = half // width

    def body(*refs):
        got, near, local_mix, rate, res, ql, ct = refs[:7]
        refs = refs[7:]
        if not own:
            mine, refs = refs[0], refs[3:]
        outs, refs = refs[: 2 if own else 3], refs[2 if own else 3 :]
        core_at, gate_at, sems = refs[0], refs[1], refs[-1]
        side = lax.rem(lax.axis_index("ctx"), 2)
        first = side == 0
        start = (side if own else 1 - side) * half
        states = got[...] if own else unpack(got, block, modes, half)
        copies = []

        def leave(source, target, sem):
            copy = pltpu.make_async_copy(source, target, sem)
            copy.start()
            copies.append(copy)

        if not own:
            taps_at = refs[2]
            low, high = mine[:block, :], got[:block, :]
            taps_at[:, :half] = jnp.where(first, low, high).astype(f32) * scale
            leave(taps_at.at[:, pl.ds(0, half)], outs[2].at[:, pl.ds(0, half)], sems.at[2 * parts])
            taps_at[:, half:] = jnp.where(first, high, low).astype(f32) * scale
            leave(taps_at.at[:, pl.ds(half, half)], outs[2].at[:, pl.ds(half, half)], sems.at[2 * parts + 1])
        for k in range(parts):
            for lane in range(k * width, (k + 1) * width, LANES):
                there = pl.ds(pl.multiple_of(start + lane, LANES), LANES)
                lanes = slice(lane, lane + LANES)
                pace = rate[:, there]
                fade = jnp.where(first, 1.0, jnp.exp(-block * pace))
                weight = res[:, there] * (near[:, there] + fade * states[:, lanes])
                mix = local_mix[:, there] + mode_sum(pace, weight, 1.0, True, block)
                core_at[:, lanes] = (ql[:, there].astype(f32) * mix).astype(bf)
                gate_at[:, lanes] = (ct[:, there].astype(f32) * mix).astype(bf)
            here = pl.ds(k * width, width)
            there = pl.ds(pl.multiple_of(start + k * width, width), width)
            leave(core_at.at[:, here], outs[0].at[:, there], sems.at[k])
            leave(gate_at.at[:, here], outs[1].at[:, there], sems.at[parts + k])
        for copy in copies:
            copy.wait()

    operands = [got, near, local_mix, rate, res, ql, ct] + ([] if own else [mine])
    shape = (block, channels)
    scratch_shapes = [pltpu.VMEM((block, half), bf)] * 2 + ([] if own else [pltpu.VMEM(shape, f32)])
    return pl.pallas_call(
        body,
        in_specs=[pl.BlockSpec(memory_space=pltpu.VMEM)] * len(operands)
        + [pl.BlockSpec(memory_space=pltpu.HBM)] * len(outputs),
        out_specs=[pl.BlockSpec(memory_space=pltpu.HBM)] * (2 if own else 3),
        out_shape=[pltpu.HBM(shape, bf)] * 2 + ([] if own else [pltpu.HBM(shape, f32)]),
        input_output_aliases={} if own else {len(operands): 0, len(operands) + 1: 1},
        scratch_shapes=[*scratch_shapes, pltpu.SemaphoreType.DMA((2 * parts + 2,))],
        compiler_params=pltpu.CompilerParams(vmem_limit_bytes=VMEM_BYTES),
        cost_estimate=pl.CostEstimate(flops=0, bytes_accessed=1024, transcendentals=0),
        name=name,
    )(*[in_vmem(a) for a in operands], *[in_hbm(a) for a in outputs])


def local(
    query_short,
    key_short,
    value_short,
    short_taps,
    query_long,
    key_long,
    long_residue,
    long_rate,
    cotangent,
):
    block, channels = query_short.shape
    modes = long_rate.shape[0]
    sequence = block * lax.axis_size("ctx")
    half, full = jnp.bfloat16, jnp.float32
    matrices = [jnp.asarray(t) for t in tables(block)]
    width = min(512, channels)

    (ks, vs, rate, ct, ql), (short_in,) = load(
        [key_short, value_short, long_rate, cotangent, query_long],
        [((block, channels), half)],
        product_kernel,
        "product",
        2,
        width,
    )
    halo = shifted(short_in, 1)
    (res, own_three, qs, kl, taps, own_two, nxt_two, back), (total,) = load(
        [long_residue, matrices[1], query_short, key_long, short_taps, matrices[0], matrices[2], matrices[3]],
        [((modes, channels), full)],
        first_kernel,
        "states",
        0,
        width,
        blocked=[rate, ct, ql],
    )
    far, steps = None, masks()
    for at, mask in enumerate(steps):
        other = swapped(total, mask)
        beside = []
        if at == 1:
            (long_spec,) = run(
                filter_kernel,
                "filter",
                [rate, res],
                [own_three],
                [(2 * block, full, "vmem")],
                width,
                [(block, full)],
                [total],
            )
            (grad_local,) = run(
                grad_local_kernel,
                "grad_local",
                [ql, ct, long_spec],
                [own_three, back],
                [(block, full, "vmem")],
                width,
            )
            short_spec, own_spec = run(
                short_filter_kernel,
                "short_filter",
                [taps, short_in],
                [own_three, own_two],
                [(2 * block, full, "vmem"), (2 * block, full, "vmem")],
                width,
            )
            beside = [grad_local, short_spec]
        if at == 2:
            in_spec, short_mix, hidden, long_in, fore_state = run(
                short_kernel,
                "short",
                [own_spec, halo, short_spec, qs, kl, rate],
                [nxt_two, back],
                [
                    (2 * block, full, "vmem"),
                    (block, full, "vmem"),
                    (block, half, "vmem"),
                    (block, half, "vmem"),
                    (modes, full, "vmem"),
                ],
                width,
                (),
                [total],
            )
            beside = [hidden]
        total, far = merge_states(total, other, far, rate, block, mask, at == len(steps) - 1, beside)
    long_grad, short_back = run(
        long_grad_kernel,
        "long_grad",
        [grad_local, far, rate, res, kl, qs],
        [],
        [(block, half, "vmem"), (block, half, "vmem")],
        width,
    )
    sb_spec, part = run(
        taps_kernel,
        "taps",
        [short_back, in_spec],
        [own_two, back],
        [(2 * block, full, "vmem"), (block, half, "vmem")],
        width,
    )
    sb_next = shifted(short_back, -1)
    (local_mix,) = run(
        long_local_kernel,
        "long_local",
        [long_in, long_spec],
        [own_two, back],
        [(block, full, "vmem")],
        width,
    )
    key_short_grad, value_short_grad, key_long_grad, query_short_grad, token = run(
        input_grad_kernel,
        "input_grad",
        [sb_next, sb_spec, short_spec, ks, vs, long_grad, kl, hidden, short_mix],
        [nxt_two, back],
        [(block, half, "hbm")] * 4 + [(ROWS, full, "vmem")],
        width,
    )
    mine, got, near = taps_and_states(part, fore_state, rate, [[token], [local_mix]], ())
    other = swapped(mine, 1)
    ready = [near, local_mix, rate, res, ql, ct]
    some = gated(True, "gated_own", got, *ready, min(width, channels // 2))
    core_output, query_long_grad, taps_grad = gated(
        False, "gated_other", other, *ready, min(width, channels // 2), sequence ** (-0.5), mine, some
    )
    return (
        core_output,
        query_short_grad,
        key_short_grad,
        value_short_grad,
        query_long_grad,
        key_long_grad,
        taps_grad,
    )


def solution(mesh):
    tokens, shared = P("ctx", "ch"), P(None, "ch")
    return jax.shard_map(
        local,
        mesh=mesh,
        in_specs=(tokens, tokens, tokens, shared, tokens, tokens, shared, shared, tokens),
        out_specs=(tokens,) * 6 + (shared,),
        check_vma=False,
    )
```

```python
import jax
import jax.numpy as jnp
import numpy as np
from jax import lax
from jax.experimental import pallas as pl
from jax.experimental.pallas import tpu as pltpu
from jax.sharding import PartitionSpec as P

ROWS = 8
LANES = 128
VMEM_BYTES = 16 * 1024 * 1024


def split_np(matrix):
    high = matrix.astype(jnp.bfloat16)
    low = (matrix - high.astype(np.float64)).astype(jnp.bfloat16)
    return high, low


def tables(block):
    length = 2 * block
    freq = np.pi * (2 * np.arange(block)[:, None] + 1) / length
    here = freq * np.arange(block)[None, :]
    after = freq * (np.arange(block)[None, :] + block)
    own = np.concatenate([np.cos(here), -np.sin(here)], axis=0)
    nxt = np.concatenate([np.cos(after), -np.sin(after)], axis=0)
    own_hi, own_lo = split_np(own)
    nxt_hi, nxt_lo = split_np(nxt)
    own_two = np.concatenate([own_hi, own_lo], axis=1)
    own_three = np.concatenate([own_hi, own_hi, own_lo], axis=1)
    nxt_two = np.concatenate([nxt_hi, nxt_lo], axis=1)
    back = np.concatenate([own_hi.T, own_lo.T], axis=0)
    return own_two, own_three, nxt_two, back


def mxu(matrix, data):
    return lax.dot_general(
        matrix, data, (((1,), (0,)), ((), ())), preferred_element_type=jnp.float32
    )


def split(value):
    high = value.astype(jnp.bfloat16)
    low = (value - high.astype(jnp.float32)).astype(jnp.bfloat16)
    return high, low


def dft_exact(matrix_two, data):
    return mxu(matrix_two, jnp.concatenate([data, data], axis=0))


def dft_full(matrix_three, data):
    high, low = split(data)
    return mxu(matrix_three, jnp.concatenate([high, low, high], axis=0))


def dft_back(back, spec_re, spec_im):
    block = spec_re.shape[0]
    high, low = split(jnp.concatenate([spec_re, spec_im], axis=0))
    both = mxu(back, high)
    return both[:block] + both[block:] + mxu(back[:block], low)


def halves(spec):
    block = spec.shape[0] // 2
    return spec[:block], spec[block:]


def times(left, right):
    left_re, left_im = halves(left)
    right_re, right_im = halves(right)
    return left_re * right_re - left_im * right_im, left_re * right_im + left_im * right_re


def times_conj(left, right):
    left_re, left_im = halves(left)
    right_re, right_im = halves(right)
    return left_re * right_re + left_im * right_im, left_im * right_re - left_re * right_im


def sublane(shape):
    return lax.broadcasted_iota(jnp.int32, shape, 0).astype(jnp.float32)


def spread(row):
    return jnp.broadcast_to(row, (ROWS, row.shape[1]))


def mode_sum(rate, weight, start, forward, block):
    sub = sublane((ROWS, rate.shape[1]))
    age = start + (sub if forward else ROWS - 1 - sub)
    waves, falls = [], []
    for mode in range(rate.shape[0]):
        pace = spread(rate[mode : mode + 1])
        waves.append(spread(weight[mode : mode + 1]) * jnp.exp(-pace * age))
        falls.append(jnp.exp(-ROWS * pace))
    tiles = []
    count = block // ROWS
    for step in range(count):
        total = waves[0]
        for wave in waves[1:]:
            total = total + wave
        tiles.append(total)
        if step < count - 1:
            waves = [wave * fall for wave, fall in zip(waves, falls)]
    if not forward:
        tiles = tiles[::-1]
    return jnp.concatenate(tiles, axis=0)


def mode_state(rate, data, forward, out_ref, lanes):
    block = data.shape[0]
    sub = sublane((ROWS, rate.shape[1]))
    age = (ROWS - 1 - sub) if forward else sub
    tiles = [data[t : t + ROWS] for t in range(0, block, ROWS)]
    if not forward:
        tiles = tiles[::-1]
    for mode in range(rate.shape[0]):
        pace = spread(rate[mode : mode + 1])
        fall = jnp.exp(-ROWS * pace)
        total = tiles[0]
        for tile in tiles[1:]:
            total = total * fall + tile
        out_ref[mode : mode + 1, lanes] = jnp.sum(total * jnp.exp(-pace * age), axis=0, keepdims=True)


def lane_blocks(width):
    return [slice(at, at + LANES) for at in range(0, width, LANES)]


def wide(ref, lanes=slice(None)):
    return ref[:, lanes].astype(jnp.float32)


def in_vmem(value):
    return pltpu.with_memory_space_constraint(value, pltpu.VMEM)


def in_hbm(value):
    return pltpu.with_memory_space_constraint(value, pltpu.HBM)


def load(brought, outs, body, name, first, width, after=(), scratch=(), blocked=(), fixed=()):
    count, n_after, ready = len(brought), len(after), len(blocked) + len(fixed)
    channels = outs[0][0][1]
    parts = channels // width
    pieces = [parts if i < first or a.shape[1] == channels else 1 for i, a in enumerate(brought)]
    offsets = [sum(pieces[:i]) for i in range(count)]

    def whole(*refs):
        sources, refs = refs[:count], refs[count:]
        ins, fix, refs = refs[: len(blocked)], refs[len(blocked) : ready], refs[ready + n_after :]
        results, more, sems = refs[:count], refs[count:-1], refs[-1]
        copies = []
        for i in range(count):
            step = sources[i].shape[1] // pieces[i]
            row = []
            for k in range(pieces[i]):
                cut = pl.ds(k * step, step)
                row.append(
                    pltpu.make_async_copy(sources[i].at[:, cut], results[i].at[:, cut], sems.at[offsets[i] + k])
                )
            copies.append(row)
        for k in range(parts):
            for row in copies[:first]:
                row[k].start()
        for row in copies[first:]:
            for copy in row:
                copy.start()
        for k in range(parts):
            for row in copies[:first]:
                row[k].wait()
            cut = pl.ds(k * width, width)
            held = more[len(outs) :]
            there = [r.at[:, cut] for r in more[: len(outs)]]
            body(*[r.at[:, cut] for r in [*results[:first], *ins]], *fix, *there, *held)
        for row in copies[first:]:
            for copy in row:
                copy.wait()

    out_shape = [pltpu.VMEM(a.shape, a.dtype) for a in brought]
    out_shape += [pltpu.VMEM(shape, dtype) for shape, dtype in outs]
    results = pl.pallas_call(
        whole,
        in_specs=[pl.BlockSpec(memory_space=pltpu.HBM)] * count
        + [pl.BlockSpec(memory_space=pltpu.VMEM)] * ready
        + [pl.BlockSpec(memory_space=pl.ANY)] * n_after,
        out_specs=[pl.BlockSpec(memory_space=pltpu.VMEM)] * len(out_shape),
        out_shape=out_shape,
        scratch_shapes=[pltpu.VMEM((rows, width), dtype) for rows, dtype in scratch]
        + [pltpu.SemaphoreType.DMA((sum(pieces),))],
        compiler_params=pltpu.CompilerParams(vmem_limit_bytes=VMEM_BYTES),
        cost_estimate=pl.CostEstimate(flops=0, bytes_accessed=1024, transcendentals=0),
        name=name,
    )(*[in_hbm(a) for a in brought], *[in_vmem(a) for a in [*blocked, *fixed]], *after)
    return results[:count], results[count:]


def first_kernel(rate, ct, ql, state):
    for lanes in lane_blocks(ct.shape[1]):
        mode_state(rate[:, lanes], wide(ct, lanes) * wide(ql, lanes), False, state, lanes)


def filter_kernel(rate, res, own_three, long_spec, hold):
    block = hold.shape[0]
    for lanes in lane_blocks(rate.shape[1]):
        hold[:, lanes] = mode_sum(rate[:, lanes], res[:, lanes], 0.0, True, block)
    long_spec[...] = dft_full(own_three[...], hold[...]) * (1.0 / block)


def short_filter_kernel(taps, si, own_three, own_two, short_spec, own_spec):
    short_spec[...] = dft_full(own_three[...], taps[...]) * (1.0 / taps.shape[0])
    own_spec[...] = dft_exact(own_two[...], si[...])


def product_kernel(ks, vs, short_in):
    short_in[...] = (wide(ks) * wide(vs)).astype(jnp.bfloat16)


def grad_local_kernel(ql, ct, long_spec, own_three, back, local_out):
    upstream = dft_full(own_three[...], wide(ct) * wide(ql))
    local_out[...] = dft_back(back[...], *times_conj(upstream, long_spec[...]))


def long_grad_kernel(local, state, rate, res, kl, qs, grad_out, back_out):
    block = local.shape[0]
    for lanes in lane_blocks(local.shape[1]):
        far = mode_sum(rate[:, lanes], res[:, lanes] * state[:, lanes], 1.0, False, block)
        grad = (local[:, lanes] + far).astype(jnp.bfloat16)
        grad_out[:, lanes] = grad
        hidden_grad = grad.astype(jnp.float32) * wide(kl, lanes)
        back_out[:, lanes] = (hidden_grad * wide(qs, lanes)).astype(jnp.bfloat16)


def short_kernel(own_spec, halo, spec, qs, kl, rate, nxt_two, back, in_spec, mix_out, hidden_out, long_in, state_out):
    signal = own_spec[...] - dft_exact(nxt_two[...], halo[...])
    in_spec[...] = signal
    mix = dft_back(back[...], *times(signal, spec[...]))
    mix_out[...] = mix
    hidden = (wide(qs) * mix).astype(jnp.bfloat16)
    hidden_out[...] = hidden
    values = (wide(kl) * hidden.astype(jnp.float32)).astype(jnp.bfloat16)
    long_in[...] = values
    for lanes in lane_blocks(halo.shape[1]):
        mode_state(rate[:, lanes], values[:, lanes].astype(jnp.float32), True, state_out, lanes)


def taps_kernel(sb, in_spec, own_two, back, sb_spec, part_out):
    spec = dft_exact(own_two[...], sb[...])
    sb_spec[...] = spec
    part = dft_back(back[...], *times_conj(spec, in_spec[...])) * (1.0 / sb.shape[0])
    part_out[...] = part.astype(jnp.bfloat16)


def input_grad_kernel(sb_next, sb_spec, spec, ks, vs, grad, kl, hidden, mix, nxt_two, back, key_out, value_out, gate_out, query_out, token):
    token[...] = jnp.zeros(token.shape, jnp.float32)
    slope = wide(grad)
    gate_out[...] = (slope * wide(hidden)).astype(jnp.bfloat16)
    query_out[...] = (slope * wide(kl) * mix[...]).astype(jnp.bfloat16)
    total = sb_spec[...] + dft_exact(nxt_two[...], sb_next[...])
    grad_in = dft_back(back[...], *times_conj(total, spec[...]))
    key_out[...] = (grad_in * wide(vs)).astype(jnp.bfloat16)
    value_out[...] = (grad_in * wide(ks)).astype(jnp.bfloat16)


def long_local_kernel(values, long_spec, own_two, back, mix_out):
    spec = dft_exact(own_two[...], values[...])
    mix_out[...] = dft_back(back[...], *times(spec, long_spec[...]))


def run(body, name, blocked, fixed, outs, width, scratch=(), after=()):
    channels = blocked[0].shape[1]
    n_in, n_fix, n_out = len(blocked), len(fixed), len(outs)
    leaves = [i for i, (_, _, place) in enumerate(outs) if place == "hbm"]
    count = channels // width

    def whole(*refs):
        ins, fix, refs = refs[:n_in], refs[n_in : n_in + n_fix], refs[n_in + n_fix + len(after) :]
        results, rest = list(refs[:n_out]), refs[n_out:]
        hold, staged = rest[: len(scratch)], rest[len(scratch) : len(scratch) + len(leaves)]
        copies = []
        for step in range(count):
            cut = pl.ds(step * width, width)
            there = [r.at[:, cut] for r in results]
            for slot, i in enumerate(leaves):
                there[i] = staged[slot].at[:, cut]
            body(*[r.at[:, cut] for r in ins], *fix, *there, *hold)
            for slot, i in enumerate(leaves):
                copy = pltpu.make_async_copy(there[i], results[i].at[:, cut], rest[-1].at[slot, step])
                copy.start()
                copies.append(copy)
        for copy in copies:
            copy.wait()

    places = {"hbm": pltpu.HBM, "vmem": pltpu.VMEM}
    scratch_shapes = [pltpu.VMEM((rows, width), dtype) for rows, dtype in scratch]
    scratch_shapes += [pltpu.VMEM((outs[i][0], channels), outs[i][1]) for i in leaves]
    if leaves:
        scratch_shapes.append(pltpu.SemaphoreType.DMA((len(leaves), count)))
    return pl.pallas_call(
        whole,
        in_specs=[pl.BlockSpec(memory_space=pltpu.VMEM)] * (n_in + n_fix)
        + [pl.BlockSpec(memory_space=pl.ANY)] * len(after),
        out_specs=[pl.BlockSpec(memory_space=places[place]) for _, _, place in outs],
        out_shape=[places[place]((rows, channels), dtype) for rows, dtype, place in outs],
        scratch_shapes=scratch_shapes,
        compiler_params=pltpu.CompilerParams(vmem_limit_bytes=VMEM_BYTES),
        cost_estimate=pl.CostEstimate(flops=0, bytes_accessed=1024, transcendentals=0),
        name=name,
    )(*[in_vmem(a) for a in [*blocked, *fixed]], *after)


def small(body, name, operands, outs, after=()):
    count, n_after = len(operands), len(after)
    return pl.pallas_call(
        lambda *refs: body(*refs[:count], *refs[count + n_after :]),
        in_specs=[pl.BlockSpec(memory_space=pltpu.VMEM)] * count + [pl.BlockSpec(memory_space=pl.ANY)] * n_after,
        out_specs=[pl.BlockSpec(memory_space=pltpu.VMEM)] * len(outs),
        out_shape=[pltpu.VMEM(shape, dtype) for shape, dtype in outs],
        compiler_params=pltpu.CompilerParams(vmem_limit_bytes=VMEM_BYTES),
        cost_estimate=pl.CostEstimate(flops=0, bytes_accessed=1024, transcendentals=0),
        name=name,
    )(*[in_vmem(a) for a in operands], *after)


def shifted(value, distance):
    size = lax.axis_size("ctx")
    pairs = [(i, i + distance) for i in range(size) if 0 <= i + distance < size]
    return lax.ppermute(value, "ctx", pairs)


def swapped(value, mask):
    size = lax.axis_size("ctx")
    return lax.ppermute(value, "ctx", [(i, i ^ mask) for i in range(size)])


def masks():
    size = lax.axis_size("ctx")
    return [1 << bit for bit in range(size.bit_length() - 1)]


def chip_states(state, other, rate, block):
    def body(state, other, rate, chip):
        first = lax.rem(lax.axis_index("ctx"), 2) == 0
        own, theirs, fade = state[...], other[...], jnp.exp(-block * rate[...])
        chip[...] = jnp.where(first, own + fade * theirs, theirs + fade * own)

    return small(body, "chip_states", [state, other, rate], [(state.shape, jnp.float32)])[0]


def column_states(total, other, got, chip, rate, block, mask, last, after):
    def body(*refs):
        total, other, rate = refs[0][...], refs[1][...], refs[2][...]
        refs = refs[3:]
        me = lax.axis_index("ctx")
        takes = lax.rem(lax.div(me, mask), 2) == 0
        steps = mask - 4 - lax.div(lax.rem(me, mask), 4) * 4
        reached = jnp.where(takes, jnp.exp((-block * steps).astype(jnp.float32) * rate) * other, 0.0)
        if got is not None:
            reached = reached + refs[0][...]
        refs[-1][...] = reached
        if last:
            chip = refs[-3][...]
            later = lax.rem(lax.div(me, 2), 2) == 1
            refs[-2][...] = jnp.where(later, chip + jnp.exp(-4 * block * rate) * reached, reached)
        else:
            fade = jnp.exp(-(block * mask) * rate)
            refs[-2][...] = jnp.where(takes, total + fade * other, other + fade * total)

    operands = [total, other, rate] + ([] if got is None else [got]) + ([chip] if last else [])
    return small(body, "column_states", operands, [(total.shape, jnp.float32)] * 2, after)


def far_states(column, other, near, rate, block, after):
    def body(column, other, near, rate, out):
        pace = rate[...]
        far = jnp.exp(-2 * block * pace) * column[...] + other[...]
        first = lax.rem(lax.axis_index("ctx"), 2) == 0
        out[...] = jnp.where(first, near[...] + jnp.exp(-block * pace) * far, far)

    return small(body, "far_states", [column, other, near, rate], [(column.shape, jnp.float32)], after)[0]


def pack(out, row, value):
    high, low = split(value)
    rows, channels = value.shape
    for at in range(0, channels, out.shape[1]):
        here = min(out.shape[1], channels - at)
        out[row : row + rows, :here] = high[:, at : at + here]
        out[row + rows : row + 2 * rows, :here] = low[:, at : at + here]
        row += 2 * rows


def unpack(ref, row, rows, channels):
    pieces = []
    for at in range(0, channels, ref.shape[1]):
        here = min(ref.shape[1], channels - at)
        high = ref[row : row + rows, :here].astype(jnp.float32)
        pieces.append(high + ref[row + rows : row + 2 * rows, :here].astype(jnp.float32))
        row += 2 * rows
    return jnp.concatenate(pieces, axis=1)


def taps_and_states(part, state, rate, beside, before):
    block, channels = part.shape
    modes = state.shape[0]
    half = channels // 2
    cut = half * 3 // 8 // LANES * LANES
    bf, f32 = jnp.bfloat16, jnp.float32

    def mine_of(value):
        return jnp.where(lax.rem(lax.axis_index("ctx"), 2) == 0, value[:, :half], value[:, half:])

    def sum_of(mine, theirs):
        return (mine[:block, :].astype(f32) + theirs[:block, :].astype(f32)).astype(bf)

    pieces = 4
    piece = half // pieces

    def apart(part, state, keep, states, *sends):
        first = lax.rem(lax.axis_index("ctx"), 2) == 0
        low, high = part[:, :half], part[:, half:]
        gone = jnp.where(first, high, low)
        for i, send in enumerate(sends):
            send[...] = gone[:, i * piece : (i + 1) * piece]
        keep[...] = jnp.where(first, low, high)
        pack(states, 0, state[...])

    keep, packed, *sends = small(
        apart,
        "apart",
        [part, state],
        [((block, half), bf), ((4 * modes, half), bf)] + [((block, piece), bf)] * pieces,
    )
    packed = swapped(packed, 1)
    others = [swapped(send, 1) for send in sends]

    def first_sum(keep, packed, state, rate, *refs):
        others, (left, right, total, near) = refs[:pieces], refs[pieces:]
        both = sum_of(keep, jnp.concatenate([other[...] for other in others], axis=1))
        left[:block, :] = both[:, :cut]
        right[...] = both[:, cut:]
        own, theirs = state[...], unpack(packed, 0, modes, channels)
        first = lax.rem(lax.axis_index("ctx"), 2) == 0
        near[...] = jnp.where(first, 0.0, theirs)
        fade = jnp.exp(-block * rate[...])
        chip = mine_of(jnp.where(first, theirs + fade * own, own + fade * theirs))
        total[...] = chip
        pack(left, block, chip)

    lefts = ((block + 2 * modes * -(-half // cut), cut), bf)
    rights, states = ((block, half - cut), bf), ((modes, half), f32)
    left, right, total, near = small(
        first_sum, "first_sum", [keep, packed, state, rate, *others], [lefts, rights, states, (state.shape, f32)], before
    )
    rest = masks()[1:]
    got = None
    for at, mask in enumerate(rest):
        left_other, right_other = swapped(left, mask), swapped(right, rest[(at + 1) % len(rest)])
        last = at == len(rest) - 1

        def reach(total, other, rate, got, mask):
            me = lax.axis_index("ctx")
            takes = lax.rem(lax.div(me, mask), 2) == 1
            steps = lax.div(lax.rem(me, mask), 2) * 2
            pace = mine_of(rate)
            theirs = unpack(other, block, modes, half)
            taken = jnp.where(takes, jnp.exp((-block * steps).astype(f32) * pace) * theirs, 0.0)
            reached = taken if got is None else got[...] + taken
            own, fade = total[...], jnp.exp(-(block * mask) * pace)
            return reached, jnp.where(takes, own + fade * theirs, theirs + fade * own)

        before_got = () if got is None else (got,)
        after = beside[at] if at < len(beside) else ()
        if last:

            def finish(left, left_other, right, right_other, total, rate, *refs, mask=mask):
                mine, got_out = refs[-2:]
                mine[:block, :cut] = sum_of(left, left_other)
                mine[:block, cut:] = sum_of(right, right_other)
                reached, _ = reach(total, left_other, rate, refs[0] if len(refs) > 2 else None, mask)
                got_out[...] = reached
                pack(mine, block, reached)

            operands = [left, left_other, right, right_other, total, rate, *before_got]
            mine, got = small(finish, "last_sum", operands, [((block + 2 * modes, half), bf), states], after)
        else:

            def go_left(left, left_other, total, rate, *refs, mask=mask):
                out, total_out, got_out = refs[-3:]
                out[:block, :] = sum_of(left, left_other)
                reached, merged = reach(total, left_other, rate, refs[0] if len(refs) > 3 else None, mask)
                got_out[...] = reached
                total_out[...] = merged
                pack(out, block, merged)

            def go_right(right, right_other, out):
                out[...] = sum_of(right, right_other)

            left, total, got = small(
                go_left, "go_left", [left, left_other, total, rate, *before_got], [lefts, states, states], after
            )
            (right,) = small(go_right, "go_right", [right, right_other], [rights])
    return mine, got, near


def gated(own, name, got, near, local_mix, rate, res, ql, ct, width, scale=None, mine=None, outputs=()):
    block, channels = local_mix.shape
    modes, half = near.shape[0], channels // 2
    bf, f32 = jnp.bfloat16, jnp.float32
    parts = half // width

    def body(*refs):
        got, near, local_mix, rate, res, ql, ct = refs[:7]
        refs = refs[7:]
        if not own:
            mine, refs = refs[0], refs[3:]
        outs, refs = refs[: 2 if own else 3], refs[2 if own else 3 :]
        core_at, gate_at, sems = refs[0], refs[1], refs[-1]
        side = lax.rem(lax.axis_index("ctx"), 2)
        first = side == 0
        start = (side if own else 1 - side) * half
        states = got[...] if own else unpack(got, block, modes, half)
        copies = []

        def leave(source, target, sem):
            copy = pltpu.make_async_copy(source, target, sem)
            copy.start()
            copies.append(copy)

        if not own:
            taps_at = refs[2]
            low, high = mine[:block, :], got[:block, :]
            taps_at[:, :half] = jnp.where(first, low, high).astype(f32) * scale
            leave(taps_at.at[:, pl.ds(0, half)], outs[2].at[:, pl.ds(0, half)], sems.at[2 * parts])
            taps_at[:, half:] = jnp.where(first, high, low).astype(f32) * scale
            leave(taps_at.at[:, pl.ds(half, half)], outs[2].at[:, pl.ds(half, half)], sems.at[2 * parts + 1])
        for k in range(parts):
            for lane in range(k * width, (k + 1) * width, LANES):
                there = pl.ds(pl.multiple_of(start + lane, LANES), LANES)
                lanes = slice(lane, lane + LANES)
                pace = rate[:, there]
                fade = jnp.where(first, 1.0, jnp.exp(-block * pace))
                weight = res[:, there] * (near[:, there] + fade * states[:, lanes])
                mix = local_mix[:, there] + mode_sum(pace, weight, 1.0, True, block)
                core_at[:, lanes] = (ql[:, there].astype(f32) * mix).astype(bf)
                gate_at[:, lanes] = (ct[:, there].astype(f32) * mix).astype(bf)
            here = pl.ds(k * width, width)
            there = pl.ds(pl.multiple_of(start + k * width, width), width)
            leave(core_at.at[:, here], outs[0].at[:, there], sems.at[k])
            leave(gate_at.at[:, here], outs[1].at[:, there], sems.at[parts + k])
        for copy in copies:
            copy.wait()

    operands = [got, near, local_mix, rate, res, ql, ct] + ([] if own else [mine])
    shape = (block, channels)
    scratch_shapes = [pltpu.VMEM((block, half), bf)] * 2 + ([] if own else [pltpu.VMEM(shape, f32)])
    return pl.pallas_call(
        body,
        in_specs=[pl.BlockSpec(memory_space=pltpu.VMEM)] * len(operands)
        + [pl.BlockSpec(memory_space=pltpu.HBM)] * len(outputs),
        out_specs=[pl.BlockSpec(memory_space=pltpu.HBM)] * (2 if own else 3),
        out_shape=[pltpu.HBM(shape, bf)] * 2 + ([] if own else [pltpu.HBM(shape, f32)]),
        input_output_aliases={} if own else {len(operands): 0, len(operands) + 1: 1},
        scratch_shapes=[*scratch_shapes, pltpu.SemaphoreType.DMA((2 * parts + 2,))],
        compiler_params=pltpu.CompilerParams(vmem_limit_bytes=VMEM_BYTES),
        cost_estimate=pl.CostEstimate(flops=0, bytes_accessed=1024, transcendentals=0),
        name=name,
    )(*[in_vmem(a) for a in operands], *[in_hbm(a) for a in outputs])


def local(
    query_short,
    key_short,
    value_short,
    short_taps,
    query_long,
    key_long,
    long_residue,
    long_rate,
    cotangent,
):
    block, channels = query_short.shape
    modes = long_rate.shape[0]
    sequence = block * lax.axis_size("ctx")
    half, full = jnp.bfloat16, jnp.float32
    matrices = [jnp.asarray(t) for t in tables(block)]
    width = min(512, channels)

    (ks, vs), (short_in,) = load(
        [key_short, value_short], [((block, channels), half)], product_kernel, "product", 2, width
    )
    halo = shifted(short_in, 1)
    (rate, ct, ql, res, own_three, qs, kl, taps, own_two, nxt_two, back), (total,) = load(
        [
            long_rate,
            cotangent,
            query_long,
            long_residue,
            matrices[1],
            query_short,
            key_long,
            short_taps,
            matrices[0],
            matrices[2],
            matrices[3],
        ],
        [((modes, channels), full)],
        first_kernel,
        "states",
        3,
        width,
        [short_in],
    )
    near = swapped(total, 1)
    chip = chip_states(total, near, rate, block)
    total, column, rest = chip, None, masks()[2:]
    other = swapped(total, rest[0])
    (long_spec,) = run(
        filter_kernel,
        "filter",
        [rate, res],
        [own_three],
        [(2 * block, full, "vmem")],
        width,
        [(block, full)],
        [chip],
    )
    (grad_local,) = run(
        grad_local_kernel,
        "grad_local",
        [ql, ct, long_spec],
        [own_three, back],
        [(block, full, "vmem")],
        width,
    )
    short_spec, own_spec = run(
        short_filter_kernel,
        "short_filter",
        [taps, short_in],
        [own_three, own_two],
        [(2 * block, full, "vmem"), (2 * block, full, "vmem")],
        width,
    )
    for at, mask in enumerate(rest):
        if at > 0:
            other = swapped(total, mask)
        last = at == len(rest) - 1
        beside = [grad_local, short_spec] if at == 0 else []
        total, column = column_states(total, other, column, chip, rate, block, mask, last, beside)
    other = swapped(total, 2)
    in_spec, short_mix, hidden, long_in, fore_state = run(
        short_kernel,
        "short",
        [own_spec, halo, short_spec, qs, kl, rate],
        [nxt_two, back],
        [
            (2 * block, full, "vmem"),
            (block, full, "vmem"),
            (block, half, "vmem"),
            (block, half, "vmem"),
            (modes, full, "vmem"),
        ],
        width,
        (),
        [total],
    )
    far = far_states(column, other, near, rate, block, [hidden])
    long_grad, short_back = run(
        long_grad_kernel,
        "long_grad",
        [grad_local, far, rate, res, kl, qs],
        [],
        [(block, half, "vmem"), (block, half, "vmem")],
        width,
    )
    sb_spec, part = run(
        taps_kernel,
        "taps",
        [short_back, in_spec],
        [own_two, back],
        [(2 * block, full, "vmem"), (block, half, "vmem")],
        width,
    )
    sb_next = shifted(short_back, -1)
    (local_mix,) = run(
        long_local_kernel,
        "long_local",
        [long_in, long_spec],
        [own_two, back],
        [(block, full, "vmem")],
        width,
    )
    key_short_grad, value_short_grad, key_long_grad, query_short_grad, token = run(
        input_grad_kernel,
        "input_grad",
        [sb_next, sb_spec, short_spec, ks, vs, long_grad, kl, hidden, short_mix],
        [nxt_two, back],
        [(block, half, "hbm")] * 4 + [(ROWS, full, "vmem")],
        width,
    )
    mine, got, near = taps_and_states(part, fore_state, rate, [[token], [local_mix]], ())
    other = swapped(mine, 1)
    ready = [near, local_mix, rate, res, ql, ct]
    some = gated(True, "gated_own", got, *ready, min(width, channels // 2))
    core_output, query_long_grad, taps_grad = gated(
        False, "gated_other", other, *ready, min(width, channels // 2), sequence ** (-0.5), mine, some
    )
    return (
        core_output,
        query_short_grad,
        key_short_grad,
        value_short_grad,
        query_long_grad,
        key_long_grad,
        taps_grad,
    )


def solution(mesh):
    tokens, shared = P("ctx", "ch"), P(None, "ch")
    return jax.shard_map(
        local,
        mesh=mesh,
        in_specs=(tokens, tokens, tokens, shared, tokens, tokens, shared, shared, tokens),
        out_specs=(tokens,) * 6 + (shared,),
        check_vma=False,
    )
```

```python
import jax
import jax.numpy as jnp
import numpy as np
from jax import lax
from jax.experimental import pallas as pl
from jax.experimental.pallas import tpu as pltpu
from jax.sharding import PartitionSpec as P

ROWS = 8
LANES = 128
VMEM_BYTES = 16 * 1024 * 1024


def split_np(matrix):
    high = matrix.astype(jnp.bfloat16)
    low = (matrix - high.astype(np.float64)).astype(jnp.bfloat16)
    return high, low


def tables(block):
    length = 2 * block
    freq = np.pi * (2 * np.arange(block)[:, None] + 1) / length
    here = freq * np.arange(block)[None, :]
    after = freq * (np.arange(block)[None, :] + block)
    own = np.concatenate([np.cos(here), -np.sin(here)], axis=0)
    nxt = np.concatenate([np.cos(after), -np.sin(after)], axis=0)
    own_hi, own_lo = split_np(own)
    nxt_hi, nxt_lo = split_np(nxt)
    own_two = np.concatenate([own_hi, own_lo], axis=1)
    own_three = np.concatenate([own_hi, own_hi, own_lo], axis=1)
    nxt_two = np.concatenate([nxt_hi, nxt_lo], axis=1)
    back = np.concatenate([own_hi.T, own_lo.T], axis=0)
    return own_two, own_three, nxt_two, back


def mxu(matrix, data):
    return lax.dot_general(
        matrix, data, (((1,), (0,)), ((), ())), preferred_element_type=jnp.float32
    )


def split(value):
    high = value.astype(jnp.bfloat16)
    low = (value - high.astype(jnp.float32)).astype(jnp.bfloat16)
    return high, low


def dft_exact(matrix_two, data):
    return mxu(matrix_two, jnp.concatenate([data, data], axis=0))


def dft_full(matrix_three, data):
    high, low = split(data)
    return mxu(matrix_three, jnp.concatenate([high, low, high], axis=0))


def dft_back(back, spec_re, spec_im):
    block = spec_re.shape[0]
    high, low = split(jnp.concatenate([spec_re, spec_im], axis=0))
    both = mxu(back, high)
    return both[:block] + both[block:] + mxu(back[:block], low)


def halves(spec):
    block = spec.shape[0] // 2
    return spec[:block], spec[block:]


def times(left, right):
    left_re, left_im = halves(left)
    right_re, right_im = halves(right)
    return left_re * right_re - left_im * right_im, left_re * right_im + left_im * right_re


def times_conj(left, right):
    left_re, left_im = halves(left)
    right_re, right_im = halves(right)
    return left_re * right_re + left_im * right_im, left_im * right_re - left_re * right_im


def sublane(shape):
    return lax.broadcasted_iota(jnp.int32, shape, 0).astype(jnp.float32)


def spread(row):
    return jnp.broadcast_to(row, (ROWS, row.shape[1]))


def mode_sum(rate, weight, start, forward, block):
    sub = sublane((ROWS, rate.shape[1]))
    age = start + (sub if forward else ROWS - 1 - sub)
    waves, falls = [], []
    for mode in range(rate.shape[0]):
        pace = spread(rate[mode : mode + 1])
        waves.append(spread(weight[mode : mode + 1]) * jnp.exp(-pace * age))
        falls.append(jnp.exp(-ROWS * pace))
    tiles = []
    count = block // ROWS
    for step in range(count):
        total = waves[0]
        for wave in waves[1:]:
            total = total + wave
        tiles.append(total)
        if step < count - 1:
            waves = [wave * fall for wave, fall in zip(waves, falls)]
    if not forward:
        tiles = tiles[::-1]
    return jnp.concatenate(tiles, axis=0)


def mode_state(rate, data, forward, out_ref, lanes):
    block = data.shape[0]
    sub = sublane((ROWS, rate.shape[1]))
    age = (ROWS - 1 - sub) if forward else sub
    tiles = [data[t : t + ROWS] for t in range(0, block, ROWS)]
    if not forward:
        tiles = tiles[::-1]
    for mode in range(rate.shape[0]):
        pace = spread(rate[mode : mode + 1])
        fall = jnp.exp(-ROWS * pace)
        total = tiles[0]
        for tile in tiles[1:]:
            total = total * fall + tile
        out_ref[mode : mode + 1, lanes] = jnp.sum(total * jnp.exp(-pace * age), axis=0, keepdims=True)


def lane_blocks(width):
    return [slice(at, at + LANES) for at in range(0, width, LANES)]


def wide(ref, lanes=slice(None)):
    return ref[:, lanes].astype(jnp.float32)


def in_vmem(value):
    return pltpu.with_memory_space_constraint(value, pltpu.VMEM)


def in_hbm(value):
    return pltpu.with_memory_space_constraint(value, pltpu.HBM)


def load(brought, outs, body, name, first, width, after=(), scratch=(), blocked=(), fixed=()):
    count, n_after, ready = len(brought), len(after), len(blocked) + len(fixed)
    channels = outs[0][0][1]
    parts = channels // width
    pieces = [parts if i < first or a.shape[1] == channels else 1 for i, a in enumerate(brought)]
    offsets = [sum(pieces[:i]) for i in range(count)]

    def whole(*refs):
        sources, refs = refs[:count], refs[count:]
        ins, fix, refs = refs[: len(blocked)], refs[len(blocked) : ready], refs[ready + n_after :]
        results, more, sems = refs[:count], refs[count:-1], refs[-1]
        copies = []
        for i in range(count):
            step = sources[i].shape[1] // pieces[i]
            row = []
            for k in range(pieces[i]):
                cut = pl.ds(k * step, step)
                row.append(
                    pltpu.make_async_copy(sources[i].at[:, cut], results[i].at[:, cut], sems.at[offsets[i] + k])
                )
            copies.append(row)
        for k in range(parts):
            for row in copies[:first]:
                row[k].start()
        for row in copies[first:]:
            for copy in row:
                copy.start()
        for k in range(parts):
            for row in copies[:first]:
                row[k].wait()
            cut = pl.ds(k * width, width)
            held = more[len(outs) :]
            there = [r.at[:, cut] for r in more[: len(outs)]]
            body(*[r.at[:, cut] for r in [*results[:first], *ins]], *fix, *there, *held)
        for row in copies[first:]:
            for copy in row:
                copy.wait()

    out_shape = [pltpu.VMEM(a.shape, a.dtype) for a in brought]
    out_shape += [pltpu.VMEM(shape, dtype) for shape, dtype in outs]
    results = pl.pallas_call(
        whole,
        in_specs=[pl.BlockSpec(memory_space=pltpu.HBM)] * count
        + [pl.BlockSpec(memory_space=pltpu.VMEM)] * ready
        + [pl.BlockSpec(memory_space=pl.ANY)] * n_after,
        out_specs=[pl.BlockSpec(memory_space=pltpu.VMEM)] * len(out_shape),
        out_shape=out_shape,
        scratch_shapes=[pltpu.VMEM((rows, width), dtype) for rows, dtype in scratch]
        + [pltpu.SemaphoreType.DMA((sum(pieces),))],
        compiler_params=pltpu.CompilerParams(vmem_limit_bytes=VMEM_BYTES),
        cost_estimate=pl.CostEstimate(flops=0, bytes_accessed=1024, transcendentals=0),
        name=name,
    )(*[in_hbm(a) for a in brought], *[in_vmem(a) for a in [*blocked, *fixed]], *after)
    return results[:count], results[count:]


def first_kernel(rate, ct, ql, state):
    for lanes in lane_blocks(ct.shape[1]):
        mode_state(rate[:, lanes], wide(ct, lanes) * wide(ql, lanes), False, state, lanes)


def filter_kernel(rate, res, own_three, long_spec, hold):
    block = hold.shape[0]
    for lanes in lane_blocks(rate.shape[1]):
        hold[:, lanes] = mode_sum(rate[:, lanes], res[:, lanes], 0.0, True, block)
    long_spec[...] = dft_full(own_three[...], hold[...]) * (1.0 / block)


def short_filter_kernel(taps, si, own_three, own_two, short_spec, own_spec):
    short_spec[...] = dft_full(own_three[...], taps[...]) * (1.0 / taps.shape[0])
    own_spec[...] = dft_exact(own_two[...], si[...])


def product_kernel(ks, vs, short_in):
    short_in[...] = (wide(ks) * wide(vs)).astype(jnp.bfloat16)


def grad_local_kernel(ql, ct, long_spec, own_three, back, local_out):
    upstream = dft_full(own_three[...], wide(ct) * wide(ql))
    local_out[...] = dft_back(back[...], *times_conj(upstream, long_spec[...]))


def long_grad_kernel(local, state, rate, res, kl, qs, grad_out, back_out):
    block = local.shape[0]
    for lanes in lane_blocks(local.shape[1]):
        far = mode_sum(rate[:, lanes], res[:, lanes] * state[:, lanes], 1.0, False, block)
        grad = (local[:, lanes] + far).astype(jnp.bfloat16)
        grad_out[:, lanes] = grad
        hidden_grad = grad.astype(jnp.float32) * wide(kl, lanes)
        back_out[:, lanes] = (hidden_grad * wide(qs, lanes)).astype(jnp.bfloat16)


def short_kernel(own_spec, halo, spec, qs, kl, rate, nxt_two, back, in_spec, mix_out, hidden_out, long_in, state_out):
    signal = own_spec[...] - dft_exact(nxt_two[...], halo[...])
    in_spec[...] = signal
    mix = dft_back(back[...], *times(signal, spec[...]))
    mix_out[...] = mix
    hidden = (wide(qs) * mix).astype(jnp.bfloat16)
    hidden_out[...] = hidden
    values = (wide(kl) * hidden.astype(jnp.float32)).astype(jnp.bfloat16)
    long_in[...] = values
    for lanes in lane_blocks(halo.shape[1]):
        mode_state(rate[:, lanes], values[:, lanes].astype(jnp.float32), True, state_out, lanes)


def taps_kernel(sb, in_spec, own_two, back, sb_spec, part_out):
    spec = dft_exact(own_two[...], sb[...])
    sb_spec[...] = spec
    part = dft_back(back[...], *times_conj(spec, in_spec[...])) * (1.0 / sb.shape[0])
    part_out[...] = part.astype(jnp.bfloat16)


def gates_kernel(grad, kl, hidden, mix, gate_out, query_out, token):
    token[...] = jnp.zeros(token.shape, jnp.float32)
    slope = wide(grad)
    gate_out[...] = (slope * wide(hidden)).astype(jnp.bfloat16)
    query_out[...] = (slope * wide(kl) * mix[...]).astype(jnp.bfloat16)


def input_grad_kernel(sb_next, sb_spec, spec, ks, vs, nxt_two, back, key_out, value_out, token):
    token[...] = jnp.zeros(token.shape, jnp.float32)
    total = sb_spec[...] + dft_exact(nxt_two[...], sb_next[...])
    grad_in = dft_back(back[...], *times_conj(total, spec[...]))
    key_out[...] = (grad_in * wide(vs)).astype(jnp.bfloat16)
    value_out[...] = (grad_in * wide(ks)).astype(jnp.bfloat16)


def long_local_kernel(values, long_spec, own_two, back, mix_out):
    spec = dft_exact(own_two[...], values[...])
    mix_out[...] = dft_back(back[...], *times(spec, long_spec[...]))


def run(body, name, blocked, fixed, outs, width, scratch=(), after=()):
    channels = blocked[0].shape[1]
    n_in, n_fix, n_out = len(blocked), len(fixed), len(outs)
    leaves = [i for i, (_, _, place) in enumerate(outs) if place == "hbm"]
    count = channels // width

    def whole(*refs):
        ins, fix, refs = refs[:n_in], refs[n_in : n_in + n_fix], refs[n_in + n_fix + len(after) :]
        results, rest = list(refs[:n_out]), refs[n_out:]
        hold, staged = rest[: len(scratch)], rest[len(scratch) : len(scratch) + len(leaves)]
        copies = []
        for step in range(count):
            cut = pl.ds(step * width, width)
            there = [r.at[:, cut] for r in results]
            for slot, i in enumerate(leaves):
                there[i] = staged[slot].at[:, cut]
            body(*[r.at[:, cut] for r in ins], *fix, *there, *hold)
            for slot, i in enumerate(leaves):
                copy = pltpu.make_async_copy(there[i], results[i].at[:, cut], rest[-1].at[slot, step])
                copy.start()
                copies.append(copy)
        for copy in copies:
            copy.wait()

    places = {"hbm": pltpu.HBM, "vmem": pltpu.VMEM}
    scratch_shapes = [pltpu.VMEM((rows, width), dtype) for rows, dtype in scratch]
    scratch_shapes += [pltpu.VMEM((outs[i][0], channels), outs[i][1]) for i in leaves]
    if leaves:
        scratch_shapes.append(pltpu.SemaphoreType.DMA((len(leaves), count)))
    return pl.pallas_call(
        whole,
        in_specs=[pl.BlockSpec(memory_space=pltpu.VMEM)] * (n_in + n_fix)
        + [pl.BlockSpec(memory_space=pl.ANY)] * len(after),
        out_specs=[pl.BlockSpec(memory_space=places[place]) for _, _, place in outs],
        out_shape=[places[place]((rows, channels), dtype) for rows, dtype, place in outs],
        scratch_shapes=scratch_shapes,
        compiler_params=pltpu.CompilerParams(vmem_limit_bytes=VMEM_BYTES),
        cost_estimate=pl.CostEstimate(flops=0, bytes_accessed=1024, transcendentals=0),
        name=name,
    )(*[in_vmem(a) for a in [*blocked, *fixed]], *after)


def small(body, name, operands, outs, after=()):
    count, n_after = len(operands), len(after)
    return pl.pallas_call(
        lambda *refs: body(*refs[:count], *refs[count + n_after :]),
        in_specs=[pl.BlockSpec(memory_space=pltpu.VMEM)] * count + [pl.BlockSpec(memory_space=pl.ANY)] * n_after,
        out_specs=[pl.BlockSpec(memory_space=pltpu.VMEM)] * len(outs),
        out_shape=[pltpu.VMEM(shape, dtype) for shape, dtype in outs],
        compiler_params=pltpu.CompilerParams(vmem_limit_bytes=VMEM_BYTES),
        cost_estimate=pl.CostEstimate(flops=0, bytes_accessed=1024, transcendentals=0),
        name=name,
    )(*[in_vmem(a) for a in operands], *after)


def shifted(value, distance):
    size = lax.axis_size("ctx")
    pairs = [(i, i + distance) for i in range(size) if 0 <= i + distance < size]
    return lax.ppermute(value, "ctx", pairs)


def swapped(value, mask):
    size = lax.axis_size("ctx")
    return lax.ppermute(value, "ctx", [(i, i ^ mask) for i in range(size)])


def masks():
    size = lax.axis_size("ctx")
    return [1 << bit for bit in range(size.bit_length() - 1)]


def chip_states(state, other, rate, block):
    def body(state, other, rate, chip):
        first = lax.rem(lax.axis_index("ctx"), 2) == 0
        own, theirs, fade = state[...], other[...], jnp.exp(-block * rate[...])
        chip[...] = jnp.where(first, own + fade * theirs, theirs + fade * own)

    return small(body, "chip_states", [state, other, rate], [(state.shape, jnp.float32)])[0]


def column_states(total, other, got, chip, rate, block, mask, last, after):
    def body(*refs):
        total, other, rate = refs[0][...], refs[1][...], refs[2][...]
        refs = refs[3:]
        me = lax.axis_index("ctx")
        takes = lax.rem(lax.div(me, mask), 2) == 0
        steps = mask - 4 - lax.div(lax.rem(me, mask), 4) * 4
        reached = jnp.where(takes, jnp.exp((-block * steps).astype(jnp.float32) * rate) * other, 0.0)
        if got is not None:
            reached = reached + refs[0][...]
        refs[-1][...] = reached
        if last:
            chip = refs[-3][...]
            later = lax.rem(lax.div(me, 2), 2) == 1
            refs[-2][...] = jnp.where(later, chip + jnp.exp(-4 * block * rate) * reached, reached)
        else:
            fade = jnp.exp(-(block * mask) * rate)
            refs[-2][...] = jnp.where(takes, total + fade * other, other + fade * total)

    operands = [total, other, rate] + ([] if got is None else [got]) + ([chip] if last else [])
    return small(body, "column_states", operands, [(total.shape, jnp.float32)] * 2, after)


def far_states(column, other, near, rate, block, after):
    def body(column, other, near, rate, out):
        pace = rate[...]
        far = jnp.exp(-2 * block * pace) * column[...] + other[...]
        first = lax.rem(lax.axis_index("ctx"), 2) == 0
        out[...] = jnp.where(first, near[...] + jnp.exp(-block * pace) * far, far)

    return small(body, "far_states", [column, other, near, rate], [(column.shape, jnp.float32)], after)[0]


def pack(out, row, value):
    high, low = split(value)
    rows, channels = value.shape
    for at in range(0, channels, out.shape[1]):
        here = min(out.shape[1], channels - at)
        out[row : row + rows, :here] = high[:, at : at + here]
        out[row + rows : row + 2 * rows, :here] = low[:, at : at + here]
        row += 2 * rows


def unpack(ref, row, rows, channels):
    pieces = []
    for at in range(0, channels, ref.shape[1]):
        here = min(ref.shape[1], channels - at)
        high = ref[row : row + rows, :here].astype(jnp.float32)
        pieces.append(high + ref[row + rows : row + 2 * rows, :here].astype(jnp.float32))
        row += 2 * rows
    return jnp.concatenate(pieces, axis=1)


def taps_and_states(part, state, rate, beside, before):
    block, channels = part.shape
    modes = state.shape[0]
    half = channels // 2
    cut = half * 3 // 8 // LANES * LANES
    bf, f32 = jnp.bfloat16, jnp.float32

    def mine_of(value):
        return jnp.where(lax.rem(lax.axis_index("ctx"), 2) == 0, value[:, :half], value[:, half:])

    def sum_of(mine, theirs):
        return (mine[:block, :].astype(f32) + theirs[:block, :].astype(f32)).astype(bf)

    pieces = 4
    piece = half // pieces

    def apart(part, state, keep, states, *sends):
        first = lax.rem(lax.axis_index("ctx"), 2) == 0
        low, high = part[:, :half], part[:, half:]
        gone = jnp.where(first, high, low)
        for i, send in enumerate(sends):
            send[...] = gone[:, i * piece : (i + 1) * piece]
        keep[...] = jnp.where(first, low, high)
        pack(states, 0, state[...])

    keep, packed, *sends = small(
        apart,
        "apart",
        [part, state],
        [((block, half), bf), ((4 * modes, half), bf)] + [((block, piece), bf)] * pieces,
    )
    packed = swapped(packed, 1)
    others = [swapped(send, 1) for send in sends]

    def first_sum(keep, packed, state, rate, *refs):
        others, (left, right, total, near) = refs[:pieces], refs[pieces:]
        both = sum_of(keep, jnp.concatenate([other[...] for other in others], axis=1))
        left[:block, :] = both[:, :cut]
        right[...] = both[:, cut:]
        own, theirs = state[...], unpack(packed, 0, modes, channels)
        first = lax.rem(lax.axis_index("ctx"), 2) == 0
        near[...] = jnp.where(first, 0.0, theirs)
        fade = jnp.exp(-block * rate[...])
        chip = mine_of(jnp.where(first, theirs + fade * own, own + fade * theirs))
        total[...] = chip
        pack(left, block, chip)

    lefts = ((block + 2 * modes * -(-half // cut), cut), bf)
    rights, states = ((block, half - cut), bf), ((modes, half), f32)
    left, right, total, near = small(
        first_sum, "first_sum", [keep, packed, state, rate, *others], [lefts, rights, states, (state.shape, f32)], before
    )
    rest = masks()[1:]
    got = None
    for at, mask in enumerate(rest):
        left_other, right_other = swapped(left, mask), swapped(right, rest[(at + 1) % len(rest)])
        last = at == len(rest) - 1

        def reach(total, other, rate, got, mask):
            me = lax.axis_index("ctx")
            takes = lax.rem(lax.div(me, mask), 2) == 1
            steps = lax.div(lax.rem(me, mask), 2) * 2
            pace = mine_of(rate)
            theirs = unpack(other, block, modes, half)
            taken = jnp.where(takes, jnp.exp((-block * steps).astype(f32) * pace) * theirs, 0.0)
            reached = taken if got is None else got[...] + taken
            own, fade = total[...], jnp.exp(-(block * mask) * pace)
            return reached, jnp.where(takes, own + fade * theirs, theirs + fade * own)

        before_got = () if got is None else (got,)
        after = beside[at] if at < len(beside) else ()
        if last:

            def finish(left, left_other, right, right_other, total, rate, *refs, mask=mask):
                mine, got_out = refs[-2:]
                mine[:block, :cut] = sum_of(left, left_other)
                mine[:block, cut:] = sum_of(right, right_other)
                reached, _ = reach(total, left_other, rate, refs[0] if len(refs) > 2 else None, mask)
                got_out[...] = reached
                pack(mine, block, reached)

            operands = [left, left_other, right, right_other, total, rate, *before_got]
            mine, got = small(finish, "last_sum", operands, [((block + 2 * modes, half), bf), states], after)
        else:

            def go_left(left, left_other, total, rate, *refs, mask=mask):
                out, total_out, got_out = refs[-3:]
                out[:block, :] = sum_of(left, left_other)
                reached, merged = reach(total, left_other, rate, refs[0] if len(refs) > 3 else None, mask)
                got_out[...] = reached
                total_out[...] = merged
                pack(out, block, merged)

            def go_right(right, right_other, out):
                out[...] = sum_of(right, right_other)

            left, total, got = small(
                go_left, "go_left", [left, left_other, total, rate, *before_got], [lefts, states, states], after
            )
            (right,) = small(go_right, "go_right", [right, right_other], [rights])
    return mine, got, near


def gated(own, name, got, near, local_mix, rate, res, ql, ct, width, scale=None, mine=None, outputs=()):
    block, channels = local_mix.shape
    modes, half = near.shape[0], channels // 2
    bf, f32 = jnp.bfloat16, jnp.float32
    parts = half // width

    def body(*refs):
        got, near, local_mix, rate, res, ql, ct = refs[:7]
        refs = refs[7:]
        if not own:
            mine, refs = refs[0], refs[3:]
        outs, refs = refs[: 2 if own else 3], refs[2 if own else 3 :]
        core_at, gate_at, sems = refs[0], refs[1], refs[-1]
        side = lax.rem(lax.axis_index("ctx"), 2)
        first = side == 0
        start = (side if own else 1 - side) * half
        states = got[...] if own else unpack(got, block, modes, half)
        copies = []

        def leave(source, target, sem):
            copy = pltpu.make_async_copy(source, target, sem)
            copy.start()
            copies.append(copy)

        if not own:
            taps_at = refs[2]
            low, high = mine[:block, :], got[:block, :]
            taps_at[:, :half] = jnp.where(first, low, high).astype(f32) * scale
            leave(taps_at.at[:, pl.ds(0, half)], outs[2].at[:, pl.ds(0, half)], sems.at[2 * parts])
            taps_at[:, half:] = jnp.where(first, high, low).astype(f32) * scale
            leave(taps_at.at[:, pl.ds(half, half)], outs[2].at[:, pl.ds(half, half)], sems.at[2 * parts + 1])
        for k in range(parts):
            for lane in range(k * width, (k + 1) * width, LANES):
                there = pl.ds(pl.multiple_of(start + lane, LANES), LANES)
                lanes = slice(lane, lane + LANES)
                pace = rate[:, there]
                fade = jnp.where(first, 1.0, jnp.exp(-block * pace))
                weight = res[:, there] * (near[:, there] + fade * states[:, lanes])
                mix = local_mix[:, there] + mode_sum(pace, weight, 1.0, True, block)
                core_at[:, lanes] = (ql[:, there].astype(f32) * mix).astype(bf)
                gate_at[:, lanes] = (ct[:, there].astype(f32) * mix).astype(bf)
            here = pl.ds(k * width, width)
            there = pl.ds(pl.multiple_of(start + k * width, width), width)
            leave(core_at.at[:, here], outs[0].at[:, there], sems.at[k])
            leave(gate_at.at[:, here], outs[1].at[:, there], sems.at[parts + k])
        for copy in copies:
            copy.wait()

    operands = [got, near, local_mix, rate, res, ql, ct] + ([] if own else [mine])
    shape = (block, channels)
    scratch_shapes = [pltpu.VMEM((block, half), bf)] * 2 + ([] if own else [pltpu.VMEM(shape, f32)])
    return pl.pallas_call(
        body,
        in_specs=[pl.BlockSpec(memory_space=pltpu.VMEM)] * len(operands)
        + [pl.BlockSpec(memory_space=pltpu.HBM)] * len(outputs),
        out_specs=[pl.BlockSpec(memory_space=pltpu.HBM)] * (2 if own else 3),
        out_shape=[pltpu.HBM(shape, bf)] * 2 + ([] if own else [pltpu.HBM(shape, f32)]),
        input_output_aliases={} if own else {len(operands): 0, len(operands) + 1: 1},
        scratch_shapes=[*scratch_shapes, pltpu.SemaphoreType.DMA((2 * parts + 2,))],
        compiler_params=pltpu.CompilerParams(vmem_limit_bytes=VMEM_BYTES),
        cost_estimate=pl.CostEstimate(flops=0, bytes_accessed=1024, transcendentals=0),
        name=name,
    )(*[in_vmem(a) for a in operands], *[in_hbm(a) for a in outputs])


def local(
    query_short,
    key_short,
    value_short,
    short_taps,
    query_long,
    key_long,
    long_residue,
    long_rate,
    cotangent,
):
    block, channels = query_short.shape
    modes = long_rate.shape[0]
    sequence = block * lax.axis_size("ctx")
    half, full = jnp.bfloat16, jnp.float32
    matrices = [jnp.asarray(t) for t in tables(block)]
    width = min(512, channels)

    (ks, vs), (short_in,) = load(
        [key_short, value_short], [((block, channels), half)], product_kernel, "product", 2, width
    )
    halo = shifted(short_in, 1)
    (rate, ct, ql, res, own_three, qs, kl, taps, own_two, nxt_two, back), (total,) = load(
        [
            long_rate,
            cotangent,
            query_long,
            long_residue,
            matrices[1],
            query_short,
            key_long,
            short_taps,
            matrices[0],
            matrices[2],
            matrices[3],
        ],
        [((modes, channels), full)],
        first_kernel,
        "states",
        3,
        width,
        [short_in],
    )
    near = swapped(total, 1)
    chip = chip_states(total, near, rate, block)
    total, column, rest = chip, None, masks()[2:]
    other = swapped(total, rest[0])
    (long_spec,) = run(
        filter_kernel,
        "filter",
        [rate, res],
        [own_three],
        [(2 * block, full, "vmem")],
        width,
        [(block, full)],
        [chip],
    )
    (grad_local,) = run(
        grad_local_kernel,
        "grad_local",
        [ql, ct, long_spec],
        [own_three, back],
        [(block, full, "vmem")],
        width,
    )
    short_spec, own_spec = run(
        short_filter_kernel,
        "short_filter",
        [taps, short_in],
        [own_three, own_two],
        [(2 * block, full, "vmem"), (2 * block, full, "vmem")],
        width,
    )
    for at, mask in enumerate(rest):
        if at > 0:
            other = swapped(total, mask)
        last = at == len(rest) - 1
        beside = [grad_local, short_spec] if at == 0 else []
        total, column = column_states(total, other, column, chip, rate, block, mask, last, beside)
    other = swapped(total, 2)
    in_spec, short_mix, hidden, long_in, fore_state = run(
        short_kernel,
        "short",
        [own_spec, halo, short_spec, qs, kl, rate],
        [nxt_two, back],
        [
            (2 * block, full, "vmem"),
            (block, full, "vmem"),
            (block, half, "vmem"),
            (block, half, "vmem"),
            (modes, full, "vmem"),
        ],
        width,
        (),
        [total],
    )
    far = far_states(column, other, near, rate, block, [hidden])
    long_grad, short_back = run(
        long_grad_kernel,
        "long_grad",
        [grad_local, far, rate, res, kl, qs],
        [],
        [(block, half, "vmem"), (block, half, "vmem")],
        width,
    )
    sb_spec, part = run(
        taps_kernel,
        "taps",
        [short_back, in_spec],
        [own_two, back],
        [(2 * block, full, "vmem"), (block, half, "vmem")],
        width,
    )
    sb_next = shifted(short_back, -1)
    (local_mix,) = run(
        long_local_kernel,
        "long_local",
        [long_in, long_spec],
        [own_two, back],
        [(block, full, "vmem")],
        width,
    )
    key_short_grad, value_short_grad, token = run(
        input_grad_kernel,
        "input_grad",
        [sb_next, sb_spec, short_spec, ks, vs],
        [nxt_two, back],
        [(block, half, "hbm")] * 2 + [(ROWS, full, "vmem")],
        width,
    )
    key_long_grad, query_short_grad, gates_token = run(
        gates_kernel,
        "gates",
        [long_grad, kl, hidden, short_mix],
        [],
        [(block, half, "hbm")] * 2 + [(ROWS, full, "vmem")],
        width,
        (),
        [token],
    )
    mine, got, near = taps_and_states(part, fore_state, rate, [[token], [local_mix, gates_token]], ())
    other = swapped(mine, 1)
    ready = [near, local_mix, rate, res, ql, ct]
    some = gated(True, "gated_own", got, *ready, min(width, channels // 2))
    core_output, query_long_grad, taps_grad = gated(
        False, "gated_other", other, *ready, min(width, channels // 2), sequence ** (-0.5), mine, some
    )
    return (
        core_output,
        query_short_grad,
        key_short_grad,
        value_short_grad,
        query_long_grad,
        key_long_grad,
        taps_grad,
    )


def solution(mesh):
    tokens, shared = P("ctx", "ch"), P(None, "ch")
    return jax.shard_map(
        local,
        mesh=mesh,
        in_specs=(tokens, tokens, tokens, shared, tokens, tokens, shared, shared, tokens),
        out_specs=(tokens,) * 6 + (shared,),
        check_vma=False,
    )
```

```python
import jax
import jax.numpy as jnp
import numpy as np
from jax import lax
from jax.experimental import pallas as pl
from jax.experimental.pallas import tpu as pltpu
from jax.sharding import PartitionSpec as P

ROWS = 8
LANES = 128
VMEM_BYTES = 16 * 1024 * 1024


def split_np(matrix):
    high = matrix.astype(jnp.bfloat16)
    low = (matrix - high.astype(np.float64)).astype(jnp.bfloat16)
    return high, low


def tables(block):
    length = 2 * block
    freq = np.pi * (2 * np.arange(block)[:, None] + 1) / length
    here = freq * np.arange(block)[None, :]
    after = freq * (np.arange(block)[None, :] + block)
    own = np.concatenate([np.cos(here), -np.sin(here)], axis=0)
    nxt = np.concatenate([np.cos(after), -np.sin(after)], axis=0)
    own_hi, own_lo = split_np(own)
    nxt_hi, nxt_lo = split_np(nxt)
    own_two = np.concatenate([own_hi, own_lo], axis=1)
    own_three = np.concatenate([own_hi, own_hi, own_lo], axis=1)
    nxt_two = np.concatenate([nxt_hi, nxt_lo], axis=1)
    back = np.concatenate([own_hi.T, own_lo.T], axis=0)
    return own_two, own_three, nxt_two, back


def mxu(matrix, data):
    return lax.dot_general(
        matrix, data, (((1,), (0,)), ((), ())), preferred_element_type=jnp.float32
    )


def split(value):
    high = value.astype(jnp.bfloat16)
    low = (value - high.astype(jnp.float32)).astype(jnp.bfloat16)
    return high, low


def dft_exact(matrix_two, data):
    return mxu(matrix_two, jnp.concatenate([data, data], axis=0))


def dft_full(matrix_three, data):
    high, low = split(data)
    return mxu(matrix_three, jnp.concatenate([high, low, high], axis=0))


def dft_back(back, spec_re, spec_im):
    block = spec_re.shape[0]
    high, low = split(jnp.concatenate([spec_re, spec_im], axis=0))
    both = mxu(back, high)
    return both[:block] + both[block:] + mxu(back[:block], low)


def halves(spec):
    block = spec.shape[0] // 2
    return spec[:block], spec[block:]


def times(left, right):
    left_re, left_im = halves(left)
    right_re, right_im = halves(right)
    return left_re * right_re - left_im * right_im, left_re * right_im + left_im * right_re


def times_conj(left, right):
    left_re, left_im = halves(left)
    right_re, right_im = halves(right)
    return left_re * right_re + left_im * right_im, left_im * right_re - left_re * right_im


def sublane(shape):
    return lax.broadcasted_iota(jnp.int32, shape, 0).astype(jnp.float32)


def spread(row):
    return jnp.broadcast_to(row, (ROWS, row.shape[1]))


def mode_sum(rate, weight, start, forward, block):
    sub = sublane((ROWS, rate.shape[1]))
    age = start + (sub if forward else ROWS - 1 - sub)
    waves, falls = [], []
    slow = jnp.exp(-ROWS * rate)
    for mode in range(rate.shape[0]):
        pace = spread(rate[mode : mode + 1])
        waves.append(spread(weight[mode : mode + 1]) * jnp.exp(-pace * age))
        falls.append(spread(slow[mode : mode + 1]))
    tiles = []
    count = block // ROWS
    for step in range(count):
        level = waves
        while len(level) > 1:
            level = [sum(level[i : i + 2][1:], level[i]) for i in range(0, len(level), 2)]
        tiles.append(level[0])
        if step < count - 1:
            waves = [wave * fall for wave, fall in zip(waves, falls)]
    if not forward:
        tiles = tiles[::-1]
    return jnp.concatenate(tiles, axis=0)


def mode_state(rate, data, forward, out_ref, lanes):
    block = data.shape[0]
    sub = sublane((ROWS, rate.shape[1]))
    age = (ROWS - 1 - sub) if forward else sub
    tiles = [data[t : t + ROWS] for t in range(0, block, ROWS)]
    if not forward:
        tiles = tiles[::-1]
    slow = jnp.exp(-ROWS * rate)
    for mode in range(rate.shape[0]):
        pace = spread(rate[mode : mode + 1])
        fall = spread(slow[mode : mode + 1])
        total = tiles[0]
        for tile in tiles[1:]:
            total = total * fall + tile
        out_ref[mode : mode + 1, lanes] = jnp.sum(total * jnp.exp(-pace * age), axis=0, keepdims=True)


def lane_blocks(width):
    return [slice(at, at + LANES) for at in range(0, width, LANES)]


def wide(ref, lanes=slice(None)):
    return ref[:, lanes].astype(jnp.float32)


def in_vmem(value):
    return pltpu.with_memory_space_constraint(value, pltpu.VMEM)


def in_hbm(value):
    return pltpu.with_memory_space_constraint(value, pltpu.HBM)


def load(brought, outs, body, name, first, width, after=(), scratch=(), blocked=(), fixed=()):
    count, n_after, ready = len(brought), len(after), len(blocked) + len(fixed)
    channels = outs[0][0][1]
    parts = channels // width
    pieces = [parts if i < first or a.shape[1] == channels else 1 for i, a in enumerate(brought)]
    offsets = [sum(pieces[:i]) for i in range(count)]

    def whole(*refs):
        sources, refs = refs[:count], refs[count:]
        ins, fix, refs = refs[: len(blocked)], refs[len(blocked) : ready], refs[ready + n_after :]
        results, more, sems = refs[:count], refs[count:-1], refs[-1]
        copies = []
        for i in range(count):
            step = sources[i].shape[1] // pieces[i]
            row = []
            for k in range(pieces[i]):
                cut = pl.ds(k * step, step)
                row.append(
                    pltpu.make_async_copy(sources[i].at[:, cut], results[i].at[:, cut], sems.at[offsets[i] + k])
                )
            copies.append(row)
        for k in range(parts):
            for row in copies[:first]:
                row[k].start()
        for row in copies[first:]:
            for copy in row:
                copy.start()
        for k in range(parts):
            for row in copies[:first]:
                row[k].wait()
            cut = pl.ds(k * width, width)
            held = more[len(outs) :]
            there = [r.at[:, cut] for r in more[: len(outs)]]
            body(*[r.at[:, cut] for r in [*results[:first], *ins]], *fix, *there, *held)
        for row in copies[first:]:
            for copy in row:
                copy.wait()

    out_shape = [pltpu.VMEM(a.shape, a.dtype) for a in brought]
    out_shape += [pltpu.VMEM(shape, dtype) for shape, dtype in outs]
    results = pl.pallas_call(
        whole,
        in_specs=[pl.BlockSpec(memory_space=pltpu.HBM)] * count
        + [pl.BlockSpec(memory_space=pltpu.VMEM)] * ready
        + [pl.BlockSpec(memory_space=pl.ANY)] * n_after,
        out_specs=[pl.BlockSpec(memory_space=pltpu.VMEM)] * len(out_shape),
        out_shape=out_shape,
        scratch_shapes=[pltpu.VMEM((rows, width), dtype) for rows, dtype in scratch]
        + [pltpu.SemaphoreType.DMA((sum(pieces),))],
        compiler_params=pltpu.CompilerParams(vmem_limit_bytes=VMEM_BYTES),
        cost_estimate=pl.CostEstimate(flops=0, bytes_accessed=1024, transcendentals=0),
        name=name,
    )(*[in_hbm(a) for a in brought], *[in_vmem(a) for a in [*blocked, *fixed]], *after)
    return results[:count], results[count:]


def first_kernel(rate, ct, ql, state):
    for lanes in lane_blocks(ct.shape[1]):
        mode_state(rate[:, lanes], wide(ct, lanes) * wide(ql, lanes), False, state, lanes)


def filter_kernel(rate, res, own_three, long_spec, hold):
    block = hold.shape[0]
    for lanes in lane_blocks(rate.shape[1]):
        hold[:, lanes] = mode_sum(rate[:, lanes], res[:, lanes], 0.0, True, block)
    long_spec[...] = dft_full(own_three[...], hold[...]) * (1.0 / block)


def short_filter_kernel(taps, si, own_three, own_two, short_spec, own_spec):
    short_spec[...] = dft_full(own_three[...], taps[...]) * (1.0 / taps.shape[0])
    own_spec[...] = dft_exact(own_two[...], si[...])


def product_kernel(ks, vs, short_in):
    short_in[...] = (wide(ks) * wide(vs)).astype(jnp.bfloat16)


def grad_local_kernel(ql, ct, long_spec, own_three, back, local_out):
    upstream = dft_full(own_three[...], wide(ct) * wide(ql))
    local_out[...] = dft_back(back[...], *times_conj(upstream, long_spec[...]))


def long_grad_kernel(local, state, rate, res, kl, qs, grad_out, back_out):
    block = local.shape[0]
    for lanes in lane_blocks(local.shape[1]):
        far = mode_sum(rate[:, lanes], res[:, lanes] * state[:, lanes], 1.0, False, block)
        grad = (local[:, lanes] + far).astype(jnp.bfloat16)
        grad_out[:, lanes] = grad
        hidden_grad = grad.astype(jnp.float32) * wide(kl, lanes)
        back_out[:, lanes] = (hidden_grad * wide(qs, lanes)).astype(jnp.bfloat16)


def short_kernel(own_spec, halo, spec, qs, kl, rate, nxt_two, back, in_spec, mix_out, hidden_out, long_in, state_out):
    signal = own_spec[...] - dft_exact(nxt_two[...], halo[...])
    in_spec[...] = signal
    mix = dft_back(back[...], *times(signal, spec[...]))
    mix_out[...] = mix
    hidden = (wide(qs) * mix).astype(jnp.bfloat16)
    hidden_out[...] = hidden
    values = (wide(kl) * hidden.astype(jnp.float32)).astype(jnp.bfloat16)
    long_in[...] = values
    for lanes in lane_blocks(halo.shape[1]):
        mode_state(rate[:, lanes], values[:, lanes].astype(jnp.float32), True, state_out, lanes)


def taps_kernel(sb, in_spec, own_two, back, sb_spec, part_out):
    spec = dft_exact(own_two[...], sb[...])
    sb_spec[...] = spec
    part = dft_back(back[...], *times_conj(spec, in_spec[...])) * (1.0 / sb.shape[0])
    part_out[...] = part.astype(jnp.bfloat16)


def gates_kernel(grad, kl, hidden, mix, gate_out, query_out, token):
    token[...] = jnp.zeros(token.shape, jnp.float32)
    slope = wide(grad)
    gate_out[...] = (slope * wide(hidden)).astype(jnp.bfloat16)
    query_out[...] = (slope * wide(kl) * mix[...]).astype(jnp.bfloat16)


def input_grad_kernel(sb_next, sb_spec, spec, ks, vs, nxt_two, back, key_out, value_out, token):
    token[...] = jnp.zeros(token.shape, jnp.float32)
    total = sb_spec[...] + dft_exact(nxt_two[...], sb_next[...])
    grad_in = dft_back(back[...], *times_conj(total, spec[...]))
    key_out[...] = (grad_in * wide(vs)).astype(jnp.bfloat16)
    value_out[...] = (grad_in * wide(ks)).astype(jnp.bfloat16)


def long_local_kernel(values, long_spec, own_two, back, mix_out):
    spec = dft_exact(own_two[...], values[...])
    mix_out[...] = dft_back(back[...], *times(spec, long_spec[...]))


def run(body, name, blocked, fixed, outs, width, scratch=(), after=()):
    channels = blocked[0].shape[1]
    n_in, n_fix, n_out = len(blocked), len(fixed), len(outs)
    leaves = [i for i, (_, _, place) in enumerate(outs) if place == "hbm"]
    count = channels // width

    def whole(*refs):
        ins, fix, refs = refs[:n_in], refs[n_in : n_in + n_fix], refs[n_in + n_fix + len(after) :]
        results, rest = list(refs[:n_out]), refs[n_out:]
        hold, staged = rest[: len(scratch)], rest[len(scratch) : len(scratch) + len(leaves)]
        copies = []
        for step in range(count):
            cut = pl.ds(step * width, width)
            there = [r.at[:, cut] for r in results]
            for slot, i in enumerate(leaves):
                there[i] = staged[slot].at[:, cut]
            body(*[r.at[:, cut] for r in ins], *fix, *there, *hold)
            for slot, i in enumerate(leaves):
                copy = pltpu.make_async_copy(there[i], results[i].at[:, cut], rest[-1].at[slot, step])
                copy.start()
                copies.append(copy)
        for copy in copies:
            copy.wait()

    places = {"hbm": pltpu.HBM, "vmem": pltpu.VMEM}
    scratch_shapes = [pltpu.VMEM((rows, width), dtype) for rows, dtype in scratch]
    scratch_shapes += [pltpu.VMEM((outs[i][0], channels), outs[i][1]) for i in leaves]
    if leaves:
        scratch_shapes.append(pltpu.SemaphoreType.DMA((len(leaves), count)))
    return pl.pallas_call(
        whole,
        in_specs=[pl.BlockSpec(memory_space=pltpu.VMEM)] * (n_in + n_fix)
        + [pl.BlockSpec(memory_space=pl.ANY)] * len(after),
        out_specs=[pl.BlockSpec(memory_space=places[place]) for _, _, place in outs],
        out_shape=[places[place]((rows, channels), dtype) for rows, dtype, place in outs],
        scratch_shapes=scratch_shapes,
        compiler_params=pltpu.CompilerParams(vmem_limit_bytes=VMEM_BYTES),
        cost_estimate=pl.CostEstimate(flops=0, bytes_accessed=1024, transcendentals=0),
        name=name,
    )(*[in_vmem(a) for a in [*blocked, *fixed]], *after)


def small(body, name, operands, outs, after=()):
    count, n_after = len(operands), len(after)
    return pl.pallas_call(
        lambda *refs: body(*refs[:count], *refs[count + n_after :]),
        in_specs=[pl.BlockSpec(memory_space=pltpu.VMEM)] * count + [pl.BlockSpec(memory_space=pl.ANY)] * n_after,
        out_specs=[pl.BlockSpec(memory_space=pltpu.VMEM)] * len(outs),
        out_shape=[pltpu.VMEM(shape, dtype) for shape, dtype in outs],
        compiler_params=pltpu.CompilerParams(vmem_limit_bytes=VMEM_BYTES),
        cost_estimate=pl.CostEstimate(flops=0, bytes_accessed=1024, transcendentals=0),
        name=name,
    )(*[in_vmem(a) for a in operands], *after)


def shifted(value, distance):
    size = lax.axis_size("ctx")
    pairs = [(i, i + distance) for i in range(size) if 0 <= i + distance < size]
    return lax.ppermute(value, "ctx", pairs)


def swapped(value, mask):
    size = lax.axis_size("ctx")
    return lax.ppermute(value, "ctx", [(i, i ^ mask) for i in range(size)])


def masks():
    size = lax.axis_size("ctx")
    return [1 << bit for bit in range(size.bit_length() - 1)]


def chip_states(state, other, rate, block):
    def body(state, other, rate, chip):
        first = lax.rem(lax.axis_index("ctx"), 2) == 0
        own, theirs, fade = state[...], other[...], jnp.exp(-block * rate[...])
        chip[...] = jnp.where(first, own + fade * theirs, theirs + fade * own)

    return small(body, "chip_states", [state, other, rate], [(state.shape, jnp.float32)])[0]


def column_states(total, other, got, chip, rate, block, mask, last, after):
    def body(*refs):
        total, other, rate = refs[0][...], refs[1][...], refs[2][...]
        refs = refs[3:]
        me = lax.axis_index("ctx")
        takes = lax.rem(lax.div(me, mask), 2) == 0
        steps = mask - 4 - lax.div(lax.rem(me, mask), 4) * 4
        reached = jnp.where(takes, jnp.exp((-block * steps).astype(jnp.float32) * rate) * other, 0.0)
        if got is not None:
            reached = reached + refs[0][...]
        refs[-1][...] = reached
        if last:
            chip = refs[-3][...]
            later = lax.rem(lax.div(me, 2), 2) == 1
            refs[-2][...] = jnp.where(later, chip + jnp.exp(-4 * block * rate) * reached, reached)
        else:
            fade = jnp.exp(-(block * mask) * rate)
            refs[-2][...] = jnp.where(takes, total + fade * other, other + fade * total)

    operands = [total, other, rate] + ([] if got is None else [got]) + ([chip] if last else [])
    return small(body, "column_states", operands, [(total.shape, jnp.float32)] * 2, after)


def far_states(column, other, near, rate, block, after):
    def body(column, other, near, rate, out):
        pace = rate[...]
        far = jnp.exp(-2 * block * pace) * column[...] + other[...]
        first = lax.rem(lax.axis_index("ctx"), 2) == 0
        out[...] = jnp.where(first, near[...] + jnp.exp(-block * pace) * far, far)

    return small(body, "far_states", [column, other, near, rate], [(column.shape, jnp.float32)], after)[0]


def pack(out, row, value):
    high, low = split(value)
    rows, channels = value.shape
    for at in range(0, channels, out.shape[1]):
        here = min(out.shape[1], channels - at)
        out[row : row + rows, :here] = high[:, at : at + here]
        out[row + rows : row + 2 * rows, :here] = low[:, at : at + here]
        row += 2 * rows


def unpack(ref, row, rows, channels):
    pieces = []
    for at in range(0, channels, ref.shape[1]):
        here = min(ref.shape[1], channels - at)
        high = ref[row : row + rows, :here].astype(jnp.float32)
        pieces.append(high + ref[row + rows : row + 2 * rows, :here].astype(jnp.float32))
        row += 2 * rows
    return jnp.concatenate(pieces, axis=1)


def taps_and_states(part, state, rate, beside, before):
    block, channels = part.shape
    modes = state.shape[0]
    half = channels // 2
    cut = half * 3 // 8 // LANES * LANES
    bf, f32 = jnp.bfloat16, jnp.float32

    def mine_of(value):
        return jnp.where(lax.rem(lax.axis_index("ctx"), 2) == 0, value[:, :half], value[:, half:])

    def sum_of(mine, theirs):
        return (mine[:block, :].astype(f32) + theirs[:block, :].astype(f32)).astype(bf)

    pieces = 4
    piece = half // pieces

    def apart(part, state, keep, states, *sends):
        first = lax.rem(lax.axis_index("ctx"), 2) == 0
        low, high = part[:, :half], part[:, half:]
        gone = jnp.where(first, high, low)
        for i, send in enumerate(sends):
            send[...] = gone[:, i * piece : (i + 1) * piece]
        keep[...] = jnp.where(first, low, high)
        pack(states, 0, state[...])

    keep, packed, *sends = small(
        apart,
        "apart",
        [part, state],
        [((block, half), bf), ((4 * modes, half), bf)] + [((block, piece), bf)] * pieces,
    )
    packed = swapped(packed, 1)
    others = [swapped(send, 1) for send in sends]

    def first_sum(keep, packed, state, rate, *refs):
        others, (left, right, total, near) = refs[:pieces], refs[pieces:]
        both = sum_of(keep, jnp.concatenate([other[...] for other in others], axis=1))
        left[:block, :] = both[:, :cut]
        right[...] = both[:, cut:]
        own, theirs = state[...], unpack(packed, 0, modes, channels)
        first = lax.rem(lax.axis_index("ctx"), 2) == 0
        near[...] = jnp.where(first, 0.0, theirs)
        fade = jnp.exp(-block * rate[...])
        chip = mine_of(jnp.where(first, theirs + fade * own, own + fade * theirs))
        total[...] = chip
        pack(left, block, chip)

    lefts = ((block + 2 * modes * -(-half // cut), cut), bf)
    rights, states = ((block, half - cut), bf), ((modes, half), f32)
    left, right, total, near = small(
        first_sum, "first_sum", [keep, packed, state, rate, *others], [lefts, rights, states, (state.shape, f32)], before
    )
    rest = masks()[1:]
    got = None
    for at, mask in enumerate(rest):
        left_other, right_other = swapped(left, mask), swapped(right, rest[(at + 1) % len(rest)])
        last = at == len(rest) - 1

        def reach(total, other, rate, got, mask):
            me = lax.axis_index("ctx")
            takes = lax.rem(lax.div(me, mask), 2) == 1
            steps = lax.div(lax.rem(me, mask), 2) * 2
            pace = mine_of(rate)
            theirs = unpack(other, block, modes, half)
            taken = jnp.where(takes, jnp.exp((-block * steps).astype(f32) * pace) * theirs, 0.0)
            reached = taken if got is None else got[...] + taken
            own, fade = total[...], jnp.exp(-(block * mask) * pace)
            return reached, jnp.where(takes, own + fade * theirs, theirs + fade * own)

        before_got = () if got is None else (got,)
        after = beside[at] if at < len(beside) else ()
        if last:

            def finish(left, left_other, right, right_other, total, rate, *refs, mask=mask):
                mine, got_out = refs[-2:]
                mine[:block, :cut] = sum_of(left, left_other)
                mine[:block, cut:] = sum_of(right, right_other)
                reached, _ = reach(total, left_other, rate, refs[0] if len(refs) > 2 else None, mask)
                got_out[...] = reached
                pack(mine, block, reached)

            operands = [left, left_other, right, right_other, total, rate, *before_got]
            mine, got = small(finish, "last_sum", operands, [((block + 2 * modes, half), bf), states], after)
        else:

            def go_left(left, left_other, total, rate, *refs, mask=mask):
                out, total_out, got_out = refs[-3:]
                out[:block, :] = sum_of(left, left_other)
                reached, merged = reach(total, left_other, rate, refs[0] if len(refs) > 3 else None, mask)
                got_out[...] = reached
                total_out[...] = merged
                pack(out, block, merged)

            def go_right(right, right_other, out):
                out[...] = sum_of(right, right_other)

            left, total, got = small(
                go_left, "go_left", [left, left_other, total, rate, *before_got], [lefts, states, states], after
            )
            (right,) = small(go_right, "go_right", [right, right_other], [rights])
    return mine, got, near


def gated(own, name, got, near, local_mix, rate, res, ql, ct, width, scale=None, mine=None, outputs=()):
    block, channels = local_mix.shape
    modes, half = near.shape[0], channels // 2
    bf, f32 = jnp.bfloat16, jnp.float32
    parts = half // width

    def body(*refs):
        got, near, local_mix, rate, res, ql, ct = refs[:7]
        refs = refs[7:]
        if not own:
            mine, refs = refs[0], refs[3:]
        outs, refs = refs[: 2 if own else 3], refs[2 if own else 3 :]
        core_at, gate_at, sems = refs[0], refs[1], refs[-1]
        side = lax.rem(lax.axis_index("ctx"), 2)
        first = side == 0
        start = (side if own else 1 - side) * half
        states = got[...] if own else unpack(got, block, modes, half)
        copies = []

        def leave(source, target, sem):
            copy = pltpu.make_async_copy(source, target, sem)
            copy.start()
            copies.append(copy)

        if not own:
            taps_at = refs[2]
            low, high = mine[:block, :], got[:block, :]
            taps_at[:, :half] = jnp.where(first, low, high).astype(f32) * scale
            leave(taps_at.at[:, pl.ds(0, half)], outs[2].at[:, pl.ds(0, half)], sems.at[2 * parts])
            taps_at[:, half:] = jnp.where(first, high, low).astype(f32) * scale
            leave(taps_at.at[:, pl.ds(half, half)], outs[2].at[:, pl.ds(half, half)], sems.at[2 * parts + 1])
        for k in range(parts):
            for lane in range(k * width, (k + 1) * width, LANES):
                there = pl.ds(pl.multiple_of(start + lane, LANES), LANES)
                lanes = slice(lane, lane + LANES)
                pace = rate[:, there]
                fade = jnp.where(first, 1.0, jnp.exp(-block * pace))
                weight = res[:, there] * (near[:, there] + fade * states[:, lanes])
                mix = local_mix[:, there] + mode_sum(pace, weight, 1.0, True, block)
                core_at[:, lanes] = (ql[:, there].astype(f32) * mix).astype(bf)
                gate_at[:, lanes] = (ct[:, there].astype(f32) * mix).astype(bf)
            here = pl.ds(k * width, width)
            there = pl.ds(pl.multiple_of(start + k * width, width), width)
            leave(core_at.at[:, here], outs[0].at[:, there], sems.at[k])
            leave(gate_at.at[:, here], outs[1].at[:, there], sems.at[parts + k])
        for copy in copies:
            copy.wait()

    operands = [got, near, local_mix, rate, res, ql, ct] + ([] if own else [mine])
    shape = (block, channels)
    scratch_shapes = [pltpu.VMEM((block, half), bf)] * 2 + ([] if own else [pltpu.VMEM(shape, f32)])
    return pl.pallas_call(
        body,
        in_specs=[pl.BlockSpec(memory_space=pltpu.VMEM)] * len(operands)
        + [pl.BlockSpec(memory_space=pltpu.HBM)] * len(outputs),
        out_specs=[pl.BlockSpec(memory_space=pltpu.HBM)] * (2 if own else 3),
        out_shape=[pltpu.HBM(shape, bf)] * 2 + ([] if own else [pltpu.HBM(shape, f32)]),
        input_output_aliases={} if own else {len(operands): 0, len(operands) + 1: 1},
        scratch_shapes=[*scratch_shapes, pltpu.SemaphoreType.DMA((2 * parts + 2,))],
        compiler_params=pltpu.CompilerParams(vmem_limit_bytes=VMEM_BYTES),
        cost_estimate=pl.CostEstimate(flops=0, bytes_accessed=1024, transcendentals=0),
        name=name,
    )(*[in_vmem(a) for a in operands], *[in_hbm(a) for a in outputs])


def local(
    query_short,
    key_short,
    value_short,
    short_taps,
    query_long,
    key_long,
    long_residue,
    long_rate,
    cotangent,
):
    block, channels = query_short.shape
    modes = long_rate.shape[0]
    sequence = block * lax.axis_size("ctx")
    half, full = jnp.bfloat16, jnp.float32
    matrices = [jnp.asarray(t) for t in tables(block)]
    width = min(512, channels)

    (ks, vs), (short_in,) = load(
        [key_short, value_short], [((block, channels), half)], product_kernel, "product", 2, width
    )
    halo = shifted(short_in, 1)
    (rate, ct, ql, res, own_three, qs, kl, taps, own_two, nxt_two, back), (total,) = load(
        [
            long_rate,
            cotangent,
            query_long,
            long_residue,
            matrices[1],
            query_short,
            key_long,
            short_taps,
            matrices[0],
            matrices[2],
            matrices[3],
        ],
        [((modes, channels), full)],
        first_kernel,
        "states",
        3,
        width,
        [short_in],
    )
    near = swapped(total, 1)
    chip = chip_states(total, near, rate, block)
    total, column, rest = chip, None, masks()[2:]
    other = swapped(total, rest[0])
    (long_spec,) = run(
        filter_kernel,
        "filter",
        [rate, res],
        [own_three],
        [(2 * block, full, "vmem")],
        width,
        [(block, full)],
        [chip],
    )
    (grad_local,) = run(
        grad_local_kernel,
        "grad_local",
        [ql, ct, long_spec],
        [own_three, back],
        [(block, full, "vmem")],
        width,
    )
    short_spec, own_spec = run(
        short_filter_kernel,
        "short_filter",
        [taps, short_in],
        [own_three, own_two],
        [(2 * block, full, "vmem"), (2 * block, full, "vmem")],
        width,
    )
    for at, mask in enumerate(rest):
        if at > 0:
            other = swapped(total, mask)
        last = at == len(rest) - 1
        beside = [grad_local, short_spec] if at == 0 else []
        total, column = column_states(total, other, column, chip, rate, block, mask, last, beside)
    other = swapped(total, 2)
    in_spec, short_mix, hidden, long_in, fore_state = run(
        short_kernel,
        "short",
        [own_spec, halo, short_spec, qs, kl, rate],
        [nxt_two, back],
        [
            (2 * block, full, "vmem"),
            (block, full, "vmem"),
            (block, half, "vmem"),
            (block, half, "vmem"),
            (modes, full, "vmem"),
        ],
        width,
        (),
        [total],
    )
    far = far_states(column, other, near, rate, block, [hidden])
    long_grad, short_back = run(
        long_grad_kernel,
        "long_grad",
        [grad_local, far, rate, res, kl, qs],
        [],
        [(block, half, "vmem"), (block, half, "vmem")],
        width,
    )
    sb_spec, part = run(
        taps_kernel,
        "taps",
        [short_back, in_spec],
        [own_two, back],
        [(2 * block, full, "vmem"), (block, half, "vmem")],
        width,
    )
    sb_next = shifted(short_back, -1)
    (local_mix,) = run(
        long_local_kernel,
        "long_local",
        [long_in, long_spec],
        [own_two, back],
        [(block, full, "vmem")],
        width,
    )
    key_short_grad, value_short_grad, token = run(
        input_grad_kernel,
        "input_grad",
        [sb_next, sb_spec, short_spec, ks, vs],
        [nxt_two, back],
        [(block, half, "hbm")] * 2 + [(ROWS, full, "vmem")],
        width,
    )
    key_long_grad, query_short_grad, gates_token = run(
        gates_kernel,
        "gates",
        [long_grad, kl, hidden, short_mix],
        [],
        [(block, half, "hbm")] * 2 + [(ROWS, full, "vmem")],
        width,
        (),
        [token],
    )
    mine, got, near = taps_and_states(part, fore_state, rate, [[token], [local_mix, gates_token]], ())
    other = swapped(mine, 1)
    ready = [near, local_mix, rate, res, ql, ct]
    some = gated(True, "gated_own", got, *ready, min(width, channels // 2))
    core_output, query_long_grad, taps_grad = gated(
        False, "gated_other", other, *ready, min(width, channels // 2), sequence ** (-0.5), mine, some
    )
    return (
        core_output,
        query_short_grad,
        key_short_grad,
        value_short_grad,
        query_long_grad,
        key_long_grad,
        taps_grad,
    )


def solution(mesh):
    tokens, shared = P("ctx", "ch"), P(None, "ch")
    return jax.shard_map(
        local,
        mesh=mesh,
        in_specs=(tokens, tokens, tokens, shared, tokens, tokens, shared, shared, tokens),
        out_specs=(tokens,) * 6 + (shared,),
        check_vma=False,
    )
```
